32 devices in a mesh: pairs: 8 (over z, x), days: 4 (over y, core).
Axes of the slice: x: 2, y: 2, z: 4, core: 2. Of those that a mesh axis runs over, the one named last changes fastest.
Arguments:
- spectra: bfloat16 [4, 512, 2048], P('days', None, 'pairs'), may hold values from -6 to 6
- observed: bfloat16 [16, 64, 64, 128], P('pairs'), may hold values from -6 to 6
- pair_blocks: int32 [16, 2], replicated, may hold values from 0 to 7, as said below
- members: int32 [512], replicated, may hold values from 0 to 511, each once
- day_mask: int32 [16, 4], P('pairs'), may hold values from 0 to 1, as said below
Outputs:
- adjoint_spectra: float32 [4, 512, 2048], P('days', None, 'pairs')
The draws below stay inside these ranges and needn't reach their ends.
Inputs may be any that keep to these rules, and one draw needn't show every extreme that they name: `pair_blocks`: each row holds two station block numbers, the first not above the second; no two rows are alike. `members`: every station appears once. `day_mask`: every listed pair is used on at least one day.
All inputs are finite; a program needn't handle non-finite values.
Results may differ from the reference program's by a relative error of at most 0.0025.
Values may be sent and summed in bfloat16 or wider, within the bound.
No kernel may reach another device: no remote copies, remote signals or barrier semaphores. Data moves between devices by JAX's collectives and lax.ppermute only.
A program may use at most 64 MiB of HBM per device.

```python
import math
import jax
import jax.numpy as jnp
import numpy as np
from jax import lax

B = 64
NSTA = 512
F = 1024
L = 128
NBLK = 8
NPAIRS = 16
DAYS = 4


def draw_pair_blocks(key, part):
    upper_rows, upper_cols = np.triu_indices(NBLK)
    chosen = jax.random.permutation(key, upper_rows.shape[0])[:NPAIRS]
    left_blocks = jnp.asarray(upper_rows, jnp.int32)[chosen]
    right_blocks = jnp.asarray(upper_cols, jnp.int32)[chosen]
    return jnp.stack([left_blocks, right_blocks], axis=1).astype(jnp.int32)


def draw_day_mask(key, part):
    key_bits, key_pick = jax.random.split(jax.random.fold_in(key, 17))
    coin_draws = jax.random.randint(key_bits, (NPAIRS, DAYS), 0, 4)
    forced = jax.random.randint(key_pick, (NPAIRS,), 0, DAYS)
    picked = jnp.arange(DAYS, dtype=jnp.int32)[None, :] == forced[:, None]
    return jnp.where((coin_draws < 3) | picked, 1, 0).astype(jnp.int32)


def level_of(key, shape, pieces, low, largest):
    def one(axis_at, shards_of):
        draws = jax.random.uniform(jax.random.fold_in(jax.random.fold_in(key, 6), axis_at), (shards_of,), jnp.float32, low / len(pieces), largest / len(pieces))
        return jnp.repeat(jnp.exp(draws), shape[axis_at] // shards_of).reshape((-1,) + (1,) * (len(shape) - axis_at - 1))

    level = one(*pieces[0])
    for cut in pieces[1:]:
        level = level * one(*cut)
    return level


def normal_values(own_key, extent, scale, reach, pieces=(), kind=jnp.bfloat16):
    result = scale * jax.random.normal(own_key, extent, jnp.float32)
    if pieces:
        result = result * level_of(own_key, extent, pieces, -0.22, 0.18)
    return jnp.clip(result, -reach, reach).astype(kind)


def setup_inputs(seed: int = 0) -> dict:
    streams_of = jax.random.split(jax.random.key(seed), 6)
    return {
        "spectra": normal_values(streams_of[0], (DAYS, NSTA, 2 * F), 1.0, 6.0, ((0, 4), (2, 8))),
        "observed": normal_values(streams_of[1], (NPAIRS, B, B, L), 1.0, 6.0, ((0, 8),)),
        "pair_blocks": draw_pair_blocks(jax.random.fold_in(streams_of[5], 71), 0),
        "members": jax.random.permutation(streams_of[3], NSTA).astype(jnp.int32),
        "day_mask": draw_day_mask(jax.random.fold_in(streams_of[5], 71), 0),
    }


def dft_tables():
    column = jnp.arange(2 * F, dtype=jnp.int32)
    frequency = column // 128 * 64 + column % 64
    part_of = column % 128 // 64
    lag_of = jnp.arange(L, dtype=jnp.int32) - L // 2
    phase_idx = frequency[:, None] * lag_of[None, :] % (2 * F)
    angles = jnp.float32(math.pi) * phase_idx.astype(jnp.float32) / F
    norm_scale = 1.0 / math.sqrt(F)
    cosine = jnp.cos(angles) * norm_scale
    sine_part = jnp.sin(angles) * norm_scale
    forward = jnp.where(part_of[:, None] == 0, cosine, -sine_part).astype(jnp.bfloat16)
    backward = jnp.where(part_of[:, None] == 0, cosine, sine_part).T.astype(jnp.bfloat16)
    return (forward, backward)

def hilbert_table():
    lag_rows = jnp.arange(L, dtype=jnp.int32)[:, None]
    lag_cols = jnp.arange(L, dtype=jnp.int32)[None, :]
    offset = (lag_cols - lag_rows) % L
    is_odd = offset % 2 == 1
    angles = jnp.float32(math.pi) * offset.astype(jnp.float32) / L
    safe_sin = jnp.where(is_odd, jnp.sin(angles), jnp.float32(1.0))
    return jnp.where(is_odd, 2.0 / L * jnp.cos(angles) / safe_sin, jnp.float32(0.0)).astype(jnp.float32)

def split_tiles(spec_array):
    shaped = spec_array.reshape(spec_array.shape[:-1] + (F // 64, 2, 64))
    return (shaped[..., 0, :], shaped[..., 1, :])

def join_tiles(real_part, imag_part):
    joined = jnp.stack([real_part, imag_part], axis=-2)
    return joined.reshape(joined.shape[:-3] + (2 * F,))

def weighted_residual(stacked, observed_f, hilbert):
    flat_s = stacked.reshape(-1, L)
    flat_o = observed_f.reshape(-1, L)
    hil_s = jnp.dot(flat_s, hilbert, precision=lax.Precision.HIGHEST, preferred_element_type=jnp.float32)
    hil_o = jnp.dot(flat_o, hilbert, precision=lax.Precision.HIGHEST, preferred_element_type=jnp.float32)
    env_s = jnp.sqrt(flat_s * flat_s + hil_s * hil_s)
    env_o = jnp.sqrt(flat_o * flat_o + hil_o * hil_o)
    weight = (1.0 + env_s) / (1.0 + env_s + env_o)
    return ((flat_s - flat_o) * weight).reshape(stacked.shape)

def reference(spectra, observed, pair_blocks, members, day_mask):
    forward, backward = dft_tables()
    backward_f = backward.astype(jnp.float32)
    hilbert = hilbert_table()
    offsets = jnp.arange(B, dtype=jnp.int32)

    def one_pair(accum_total, inputs):
        blocks, obs_pair, mask_row = inputs
        rows_a = members[blocks[0] * B + offsets].astype(jnp.int32)
        rows_b = members[blocks[1] * B + offsets].astype(jnp.int32)
        spec_a = jnp.take(spectra, rows_a, axis=1).astype(jnp.float32)
        spec_b = jnp.take(spectra, rows_b, axis=1).astype(jnp.float32)
        a_real, a_imag = split_tiles(spec_a)
        b_real, b_imag = split_tiles(spec_b)
        mask_f = mask_row.astype(jnp.float32)
        day_count = jnp.sum(mask_f)
        masked_real = a_real * mask_f[:, None, None, None]
        masked_imag = a_imag * mask_f[:, None, None, None]
        cross_real = jnp.einsum('dakj,dbkj->dabkj', masked_real, b_real) + jnp.einsum('dakj,dbkj->dabkj', masked_imag, b_imag)
        cross_imag = jnp.einsum('dakj,dbkj->dabkj', masked_imag, b_real) - jnp.einsum('dakj,dbkj->dabkj', masked_real, b_imag)
        cross = join_tiles(cross_real, cross_imag).astype(jnp.bfloat16)
        correlation = jnp.einsum('dabc,cl->abl', cross.astype(jnp.float32), forward.astype(jnp.float32))
        stacked = correlation / day_count
        residual = weighted_residual(stacked, obs_pair.astype(jnp.float32), hilbert)
        response = jnp.dot(residual.reshape(B * B, L), backward_f, precision=lax.Precision.HIGHEST, preferred_element_type=jnp.float32)
        g_cos, g_sin = split_tiles(response.reshape(B, B, 2 * F))
        day_share = mask_f / day_count
        adj_a_real = jnp.einsum('abkj,dbkj->dakj', g_cos, b_real) + jnp.einsum('abkj,dbkj->dakj', g_sin, b_imag)
        adj_a_imag = jnp.einsum('abkj,dbkj->dakj', g_cos, b_imag) - jnp.einsum('abkj,dbkj->dakj', g_sin, b_real)
        adj_b_real = jnp.einsum('abkj,dakj->dbkj', g_cos, a_real) - jnp.einsum('abkj,dakj->dbkj', g_sin, a_imag)
        adj_b_imag = jnp.einsum('abkj,dakj->dbkj', g_cos, a_imag) + jnp.einsum('abkj,dakj->dbkj', g_sin, a_real)
        side_a = join_tiles(adj_a_real, adj_a_imag) * day_share[:, None, None]
        side_b = join_tiles(adj_b_real, adj_b_imag) * day_share[:, None, None]
        accum_total = accum_total.at[:, rows_a].add(side_a)
        accum_total = accum_total.at[:, rows_b].add(side_b)
        return (accum_total, None)
    start = jnp.zeros((DAYS, NSTA, 2 * F), jnp.float32)
    accum_total, _ = lax.scan(one_pair, start, (pair_blocks, observed, day_mask))
    return accum_total
```

```python
import functools
import math

import jax
import jax.numpy as jnp
import ml_dtypes
import numpy as np
from jax import lax
from jax.experimental import pallas as pl
from jax.experimental.pallas import tpu as pltpu
from jax.sharding import Mesh, PartitionSpec as P

HALF = 64
TILE = 128
CORES = 2
F32 = jnp.float32
BF16 = jnp.bfloat16


def dft_tables(columns, lags):
    freqs = columns // 2
    column = np.arange(columns)
    frequency = column // TILE * HALF + column % HALF
    is_real = column % TILE < HALF
    phase = frequency[:, None] * (np.arange(lags) - lags // 2)[None, :] % (2 * freqs)
    angles = np.float32(math.pi) * phase.astype(np.float32) / np.float32(freqs)
    scale = np.float32(1.0 / math.sqrt(freqs))
    cosine = np.cos(angles) * scale
    sine = np.sin(angles) * scale
    forward = np.where(is_real[:, None], cosine, -sine).astype(ml_dtypes.bfloat16)
    backward = np.where(is_real[:, None], cosine, sine).T.astype(ml_dtypes.bfloat16)
    return forward, backward


def hilbert_parts(lags):
    offset = (np.arange(lags)[None, :] - np.arange(lags)[:, None]) % lags
    angles = np.float32(math.pi) * offset.astype(np.float32) / np.float32(lags)
    odd = offset % 2 == 1
    safe = np.where(odd, np.sin(angles), np.float32(1.0))
    table = np.where(odd, np.float32(2.0 / lags) * np.cos(angles) / safe, np.float32(0.0))
    table = table.astype(np.float32)
    high = table.astype(ml_dtypes.bfloat16)
    low = (table - high.astype(np.float32)).astype(ml_dtypes.bfloat16)
    return high, low


def left_lanes(shape):
    return lax.broadcasted_iota(jnp.int32, shape, len(shape) - 1) % TILE < HALF


def swap_halves(x):
    return pltpu.roll(x, HALF, 1)


def dot(a, b):
    return jnp.dot(a, b, preferred_element_type=F32)


def dot_split(x, high, low):
    x_high = x.astype(BF16)
    x_low = (x - x_high.astype(F32)).astype(BF16)
    return dot(x_high, high) + (dot(x_high, low) + dot(x_low, high))


def pack_kernel(blocks_ref, members_ref, spectra_ref, out_ref, ordered):
    stations = spectra_ref.shape[1]
    b = out_ref.shape[1] // 2
    station = lax.broadcasted_iota(jnp.int32, (stations, stations), 0)
    chosen = (station == members_ref[...]).astype(F32).astype(BF16)
    ordered[...] = lax.dot_general(
        chosen, spectra_ref[0], (((0,), (0,)), ((), ())), preferred_element_type=F32
    ).astype(BF16)
    for p in range(out_ref.shape[0]):
        for side in range(2):
            row = pl.multiple_of(blocks_ref[p, side] * b, b)
            out_ref[p, side * b:(side + 1) * b, :] = ordered[pl.ds(row, b), :]


def pack(pair_blocks, members, spectra, b):
    _, stations, cols = spectra.shape
    n_pairs = pair_blocks.shape[0]
    return pl.pallas_call(
        pack_kernel,
        out_shape=jax.ShapeDtypeStruct((n_pairs, 2 * b, cols), BF16),
        in_specs=[
            pl.BlockSpec(memory_space=pltpu.SMEM),
            pl.BlockSpec(memory_space=pltpu.VMEM),
            pl.BlockSpec(memory_space=pltpu.VMEM),
        ],
        out_specs=pl.BlockSpec(memory_space=pltpu.VMEM),
        scratch_shapes=[pltpu.VMEM((stations, cols), BF16)],
        compiler_params=pltpu.CompilerParams(vmem_limit_bytes=32 << 20),
        name="pack",
    )(pair_blocks, members, spectra)


def unpack_kernel(blocks_ref, members_ref, got_ref, out_ref, total):
    stations = out_ref.shape[1]
    b = got_ref.shape[1] // 2
    total[...] = jnp.zeros_like(total)
    for p in range(got_ref.shape[0]):
        for side in range(2):
            rows = pl.ds(pl.multiple_of(blocks_ref[p, side] * b, b), b)
            total[rows, :] += got_ref[p, side * b:(side + 1) * b, :].astype(F32)
    station = lax.broadcasted_iota(jnp.int32, (stations, stations), 0)
    chosen = (station == members_ref[...]).astype(F32).astype(BF16)
    whole = total[...]
    high = whole.astype(BF16)
    rest = whole - high.astype(F32)
    mid = rest.astype(BF16)
    low = (rest - mid.astype(F32)).astype(BF16)
    out_ref[0] = dot(chosen, high) + (dot(chosen, mid) + dot(chosen, low))


def unpack(pair_blocks, members, got, stations):
    cols = got.shape[2]
    return pl.pallas_call(
        unpack_kernel,
        out_shape=jax.ShapeDtypeStruct((1, stations, cols), F32),
        in_specs=[
            pl.BlockSpec(memory_space=pltpu.SMEM),
            pl.BlockSpec(memory_space=pltpu.VMEM),
            pl.BlockSpec(memory_space=pltpu.VMEM),
        ],
        out_specs=pl.BlockSpec(memory_space=pltpu.VMEM),
        scratch_shapes=[pltpu.VMEM((stations, cols), F32)],
        compiler_params=pltpu.CompilerParams(vmem_limit_bytes=32 << 20),
        name="unpack",
    )(pair_blocks, members, got)


def forward_kernel(b, group, mask_ref, got_ref, table_ref, out_ref, rows_one, rows_two, cols_one, cols_two):
    days = got_ref.shape[0]
    cols = got_ref.shape[2]
    lanes = left_lanes((b, TILE))
    sign = jnp.where(lanes, F32(1.0), F32(-1.0))

    @pl.when(pl.program_id(0) == 0)
    def _():
        out_ref[...] = jnp.zeros_like(out_ref)

    for d in range(days):
        for t in range(cols // TILE):
            at = slice((d * (cols // TILE) + t) * TILE, (d * (cols // TILE) + t + 1) * TILE)
            u_a = got_ref[d, :b, t * TILE:(t + 1) * TILE].astype(F32) * mask_ref[d]
            u_b = got_ref[d, b:, t * TILE:(t + 1) * TILE].astype(F32)
            v_a = swap_halves(u_a)
            v_b = swap_halves(u_b)
            rows_one[:, at] = u_a
            rows_two[:, at] = v_a * sign
            cols_one[:, at] = jnp.where(lanes, u_b, v_b)
            cols_two[:, at] = jnp.where(lanes, v_b, u_b)

    def some_rows(step, carry):
        first = pl.multiple_of(step * group, group)
        sums = jnp.zeros((group * b, out_ref.shape[1]), F32)
        for d in range(days):
            pieces = []
            for t in range(cols // TILE):
                at = slice((d * (cols // TILE) + t) * TILE, (d * (cols // TILE) + t + 1) * TILE)
                b_one = cols_one[:, at]
                b_two = cols_two[:, at]
                a_one = rows_one[pl.ds(first, group), at]
                a_two = rows_two[pl.ds(first, group), at]
                pieces.append(
                    jnp.concatenate(
                        [
                            (a_one[k:k + 1] * b_one + a_two[k:k + 1] * b_two).astype(BF16)
                            for k in range(group)
                        ],
                        axis=0,
                    )
                )
            cross = jnp.concatenate(pieces, axis=1)
            sums = sums + dot(cross, table_ref[...])
        at_rows = pl.ds(pl.multiple_of(first * b, group * b), group * b)
        out_ref[at_rows, :] += sums
        return carry

    lax.fori_loop(0, b // group, some_rows, 0)


def forward_pass(mask, got, table, b):
    shares, days, rows, cols = got.shape
    lags = table.shape[1]
    group = 8
    return pl.pallas_call(
        functools.partial(forward_kernel, b, group),
        out_shape=jax.ShapeDtypeStruct((b * b, lags), F32),
        grid=(shares,),
        in_specs=[
            pl.BlockSpec(memory_space=pltpu.SMEM),
            pl.BlockSpec((None, days, rows, cols), lambda s: (s, 0, 0, 0)),
            pl.BlockSpec((cols, lags), lambda s: (s, 0)),
        ],
        out_specs=pl.BlockSpec((b * b, lags), lambda s: (0, 0)),
        scratch_shapes=[pltpu.VMEM((b, days * cols), F32)] * 4,
        compiler_params=pltpu.CompilerParams(vmem_limit_bytes=40 << 20),
        name="forward",
    )(mask, got, table)


def adjoint_kernel(
    b, group, scalars_ref, slot_ref, mine_ref, other_ref, observed_ref, hil_high, hil_low, got_ref, table_ref,
    out_ref, residual, u_one, u_two, part_p, part_q, side_a, response,
):
    days = got_ref.shape[0]
    cols = got_ref.shape[2]
    lags = mine_ref.shape[1]
    tiles = cols // TILE
    chunk = group * b

    @pl.when(pl.program_id(0) == 0)
    def _():
        def some(step, carry):
            at = pl.ds(pl.multiple_of(step * chunk, chunk), chunk)
            stacked = (mine_ref[at, :] + other_ref[at, :]) / scalars_ref[days]
            seen = observed_ref[at, :]
            seen_f = seen.astype(F32)
            hil_s = dot_split(stacked, hil_high[...], hil_low[...])
            hil_o = dot(seen, hil_high[...]) + dot(seen, hil_low[...])
            env_s = jnp.sqrt(stacked * stacked + hil_s * hil_s)
            env_o = jnp.sqrt(seen_f * seen_f + hil_o * hil_o)
            value = (stacked - seen_f) * ((1.0 + env_s) / (1.0 + env_s + env_o))
            high = value.astype(BF16)
            residual[at, :lags] = high
            residual[at, lags:] = (value - high.astype(F32)).astype(BF16)
            return carry

        lax.fori_loop(0, b * b // chunk, some, 0)

    for d in range(days):
        for t in range(tiles):
            at = slice((d * tiles + t) * TILE, (d * tiles + t + 1) * TILE)
            u = got_ref[d, :, t * TILE:(t + 1) * TILE].astype(F32)
            u_one[:, at] = u
            u_two[:, at] = swap_halves(u)
    part_p[...] = jnp.zeros_like(part_p)
    part_q[...] = jnp.zeros_like(part_q)
    lanes = left_lanes((group, TILE))
    table_two = jnp.concatenate([table_ref[...], table_ref[...]], axis=0)

    def some_rows(step, carry):
        first = pl.multiple_of(step * group, group)
        at_rows = pl.ds(pl.multiple_of(first * b, chunk), chunk)
        response[...] = dot(residual[at_rows, :], table_two)
        for t in range(tiles):
            for d in range(days):
                at = slice((d * tiles + t) * TILE, (d * tiles + t + 1) * TILE)
                b_one = u_one[b:, at]
                b_two = u_two[b:, at]
                a_one = u_one[pl.ds(first, group), at]
                a_two = u_two[pl.ds(first, group), at]
                p_b = part_p[:, at]
                q_b = part_q[:, at]
                p_rows = []
                q_rows = []
                for k in range(group):
                    g = response[k * b:(k + 1) * b, t * TILE:(t + 1) * TILE]
                    p_rows.append(jnp.sum(g * b_one, axis=0, keepdims=True))
                    q_rows.append(jnp.sum(g * b_two, axis=0, keepdims=True))
                    p_b = p_b + g * a_one[k:k + 1]
                    q_b = q_b + g * a_two[k:k + 1]
                part_p[:, at] = p_b
                part_q[:, at] = q_b
                p_a = jnp.concatenate(p_rows, axis=0)
                q_a = jnp.concatenate(q_rows, axis=0)
                value = jnp.where(lanes, p_a + swap_halves(p_a), swap_halves(q_a) - q_a)
                side_a[pl.ds(first, group), at] = value * scalars_ref[d]
        return carry

    lax.fori_loop(0, b // group, some_rows, 0)
    lanes_b = left_lanes((b, TILE))
    for d in range(days):
        for t in range(tiles):
            at = slice((d * tiles + t) * TILE, (d * tiles + t + 1) * TILE)
            here = slice(t * TILE, (t + 1) * TILE)
            p_b = part_p[:, at]
            q_b = part_q[:, at]
            value = jnp.where(lanes_b, p_b - swap_halves(p_b), q_b + swap_halves(q_b))
            out_ref[d, :b, here] = side_a[:, at].astype(BF16)
            out_ref[d, b:, here] = (value * scalars_ref[d]).astype(BF16)


def adjoint_pass(scalars, slot, mine, other, observed, hil_high, hil_low, got, table):
    shares, days, rows, cols = got.shape
    b = rows // 2
    lags = mine.shape[1]
    group = 8
    whole = lambda s, slot_ref: (0, 0)
    spec = pltpu.PrefetchScalarGridSpec(
        num_scalar_prefetch=1,
        grid=(shares,),
        in_specs=[
            pl.BlockSpec(memory_space=pltpu.SMEM),
            pl.BlockSpec((b * b, lags), whole),
            pl.BlockSpec((b * b, lags), whole),
            pl.BlockSpec((None, b * b, lags), lambda s, slot_ref: (slot_ref[0], 0, 0)),
            pl.BlockSpec((lags, lags), whole),
            pl.BlockSpec((lags, lags), whole),
            pl.BlockSpec((None, days, rows, cols), lambda s, slot_ref: (s, 0, 0, 0)),
            pl.BlockSpec((lags, cols), lambda s, slot_ref: (0, s)),
        ],
        out_specs=pl.BlockSpec((None, days, rows, cols), lambda s, slot_ref: (s, 0, 0, 0)),
        scratch_shapes=[
            pltpu.VMEM((b * b, 2 * lags), BF16),
            pltpu.VMEM((rows, days * cols), F32),
            pltpu.VMEM((rows, days * cols), F32),
            pltpu.VMEM((b, days * cols), F32),
            pltpu.VMEM((b, days * cols), F32),
            pltpu.VMEM((b, days * cols), F32),
            pltpu.VMEM((group * b, cols), F32),
        ],
    )

    def kernel(slot_ref, scalars_ref, *refs):
        adjoint_kernel(b, group, scalars_ref, slot_ref, *refs)

    return pl.pallas_call(
        kernel,
        out_shape=jax.ShapeDtypeStruct(got.shape, BF16),
        grid_spec=spec,
        compiler_params=pltpu.CompilerParams(vmem_limit_bytes=48 << 20),
        name="adjoint",
    )(slot, scalars, mine, other, observed, hil_high, hil_low, got, table)


def body(spectra, observed, pair_blocks, members, day_mask):
    shares = lax.axis_size("pairs")
    slots, b, _, lags = observed.shape
    _, stations, cols = spectra.shape
    forward, backward = dft_tables(shares * cols, lags)
    hil_high, hil_low = hilbert_parts(lags)
    slot = lax.axis_index("slot")
    members = members.reshape(1, stations)
    first_day = lax.axis_index("outer") * slots * CORES + lax.axis_index("core")
    mask = lax.dynamic_slice_in_dim(day_mask, slot, 1, 0)[0].astype(F32)
    mask_here = jnp.stack([lax.dynamic_index_in_dim(mask, first_day + k * CORES, 0, False) for k in range(slots)])
    count = jnp.sum(mask)
    scalars = jnp.concatenate([mask_here / count, count[None]])

    sent = pack(pair_blocks, members, spectra, b)
    got = lax.all_to_all(sent, ("pairs", "slot"), 0, 0, tiled=True)
    got = got.reshape(shares, slots, 2 * b, cols)
    mine = forward_pass(mask_here, got, forward, b)
    for axis in ("outer", "core"):
        n = lax.axis_size(axis)
        others = [lax.ppermute(mine, axis, [(i, (i + k) % n) for i in range(n)]) for k in range(1, n)]
        if axis == "outer":
            for other in others:
                mine = mine + other
    contrib = adjoint_pass(
        scalars, slot[None], mine, others[0], observed.reshape(slots, b * b, lags), hil_high, hil_low, got, backward
    )
    returned = lax.all_to_all(
        contrib.reshape(shares * slots, 2 * b, cols), ("pairs", "slot"), 0, 0, tiled=True
    )
    return unpack(pair_blocks, members, returned, stations)


def solution(mesh):
    shares, days = mesh.devices.shape
    names = ("pairs", "outer", "slot", "core")

    def run(spectra, observed, pair_blocks, members, day_mask):
        slots = observed.shape[0] // shares
        split = (shares, days // CORES // slots, slots, CORES)
        finer = Mesh(mesh.devices.reshape(split), names)
        day_axes = names[1:]
        return jax.shard_map(
            body,
            mesh=finer,
            in_specs=(
                P(day_axes, None, "pairs"),
                P("pairs", None, None, None),
                P(),
                P(),
                P("pairs", None),
            ),
            out_specs=P(day_axes, None, "pairs"),
            check_vma=False,
        )(spectra, observed, pair_blocks, members, day_mask)

    return run
```

```python
import functools
import math

import jax
import jax.numpy as jnp
import ml_dtypes
import numpy as np
from jax import lax
from jax.experimental import pallas as pl
from jax.experimental.pallas import tpu as pltpu
from jax.sharding import Mesh, PartitionSpec as P

HALF = 64
TILE = 128
CORES = 2
F32 = jnp.float32
BF16 = jnp.bfloat16


def dft_table(columns, lags):
    freqs = columns // 2
    column = np.arange(columns)
    frequency = column // TILE * HALF + column % HALF
    is_real = column % TILE < HALF
    phase = frequency[:, None] * (np.arange(lags) - lags // 2)[None, :] % (2 * freqs)
    angles = np.float32(math.pi) * phase.astype(np.float32) / np.float32(freqs)
    scale = np.float32(1.0 / math.sqrt(freqs))
    cosine = np.cos(angles) * scale
    sine = np.sin(angles) * scale
    return np.where(is_real[:, None], cosine, -sine).astype(ml_dtypes.bfloat16)


def hilbert_parts(lags):
    offset = (np.arange(lags)[None, :] - np.arange(lags)[:, None]) % lags
    angles = np.float32(math.pi) * offset.astype(np.float32) / np.float32(lags)
    odd = offset % 2 == 1
    safe = np.where(odd, np.sin(angles), np.float32(1.0))
    table = np.where(odd, np.float32(2.0 / lags) * np.cos(angles) / safe, np.float32(0.0))
    table = table.astype(np.float32)
    high = table.astype(ml_dtypes.bfloat16)
    low = (table - high.astype(np.float32)).astype(ml_dtypes.bfloat16)
    return high, low


def left_lanes(shape):
    return lax.broadcasted_iota(jnp.int32, shape, len(shape) - 1) % TILE < HALF


def swap_halves(x):
    return pltpu.roll(x, HALF, 1)


def dot(a, b):
    return jnp.dot(a, b, preferred_element_type=F32)


def dot_split(x, high, low):
    x_high = x.astype(BF16)
    x_low = (x - x_high.astype(F32)).astype(BF16)
    return dot(x_high, high) + (dot(x_high, low) + dot(x_low, high))


def pack_kernel(blocks_ref, members_ref, spectra_ref, out_ref, ordered):
    stations = spectra_ref.shape[1]
    b = out_ref.shape[1] // 2
    station = lax.broadcasted_iota(jnp.int32, (stations, stations), 0)
    chosen = (station == members_ref[...]).astype(F32).astype(BF16)
    ordered[...] = lax.dot_general(
        chosen, spectra_ref[0], (((0,), (0,)), ((), ())), preferred_element_type=F32
    ).astype(BF16)
    for p in range(out_ref.shape[0]):
        for side in range(2):
            row = pl.multiple_of(blocks_ref[p, side] * b, b)
            out_ref[p, side * b:(side + 1) * b, :] = ordered[pl.ds(row, b), :]


def pack(pair_blocks, members, spectra, b):
    _, stations, cols = spectra.shape
    n_pairs = pair_blocks.shape[0]
    return pl.pallas_call(
        pack_kernel,
        out_shape=jax.ShapeDtypeStruct((n_pairs, 2 * b, cols), BF16),
        in_specs=[
            pl.BlockSpec(memory_space=pltpu.SMEM),
            pl.BlockSpec(memory_space=pltpu.VMEM),
            pl.BlockSpec(memory_space=pltpu.VMEM),
        ],
        out_specs=pl.BlockSpec(memory_space=pltpu.VMEM),
        scratch_shapes=[pltpu.VMEM((stations, cols), BF16)],
        compiler_params=pltpu.CompilerParams(vmem_limit_bytes=32 << 20),
        name="pack",
    )(pair_blocks, members, spectra)


def unpack_kernel(blocks_ref, members_ref, got_ref, out_ref, total):
    stations = out_ref.shape[1]
    b = got_ref.shape[1] // 2
    total[...] = jnp.zeros_like(total)
    for p in range(got_ref.shape[0]):
        for side in range(2):
            rows = pl.ds(pl.multiple_of(blocks_ref[p, side] * b, b), b)
            total[rows, :] += got_ref[p, side * b:(side + 1) * b, :].astype(F32)
    station = lax.broadcasted_iota(jnp.int32, (stations, stations), 0)
    chosen = (station == members_ref[...]).astype(F32).astype(BF16)
    whole = total[...]
    high = whole.astype(BF16)
    rest = whole - high.astype(F32)
    mid = rest.astype(BF16)
    low = (rest - mid.astype(F32)).astype(BF16)
    out_ref[0] = dot(chosen, high) + (dot(chosen, mid) + dot(chosen, low))


def unpack(pair_blocks, members, got, stations):
    cols = got.shape[2]
    return pl.pallas_call(
        unpack_kernel,
        out_shape=jax.ShapeDtypeStruct((1, stations, cols), F32),
        in_specs=[
            pl.BlockSpec(memory_space=pltpu.SMEM),
            pl.BlockSpec(memory_space=pltpu.VMEM),
            pl.BlockSpec(memory_space=pltpu.VMEM),
        ],
        out_specs=pl.BlockSpec(memory_space=pltpu.VMEM),
        scratch_shapes=[pltpu.VMEM((stations, cols), F32)],
        compiler_params=pltpu.CompilerParams(vmem_limit_bytes=32 << 20),
        name="unpack",
    )(pair_blocks, members, got)


def forward_kernel(b, group, mask_ref, got_ref, table_ref, out_ref, rows_one, rows_two, cols_one, cols_two):
    days = got_ref.shape[0]
    cols = got_ref.shape[2]
    lanes = left_lanes((b, TILE))
    sign = jnp.where(lanes, F32(1.0), F32(-1.0))

    @pl.when(pl.program_id(0) == 0)
    def _():
        out_ref[...] = jnp.zeros_like(out_ref)

    for d in range(days):
        for t in range(cols // TILE):
            at = slice((d * (cols // TILE) + t) * TILE, (d * (cols // TILE) + t + 1) * TILE)
            u_a = got_ref[d, :b, t * TILE:(t + 1) * TILE].astype(F32) * mask_ref[d]
            u_b = got_ref[d, b:, t * TILE:(t + 1) * TILE].astype(F32)
            v_a = swap_halves(u_a)
            v_b = swap_halves(u_b)
            rows_one[:, at] = u_a
            rows_two[:, at] = v_a * sign
            cols_one[:, at] = jnp.where(lanes, u_b, v_b)
            cols_two[:, at] = jnp.where(lanes, v_b, u_b)

    def some_rows(step, carry):
        first = pl.multiple_of(step * group, group)
        sums = jnp.zeros((group * b, out_ref.shape[1]), F32)
        for d in range(days):
            pieces = []
            for t in range(cols // TILE):
                at = slice((d * (cols // TILE) + t) * TILE, (d * (cols // TILE) + t + 1) * TILE)
                b_one = cols_one[:, at]
                b_two = cols_two[:, at]
                a_one = rows_one[pl.ds(first, group), at]
                a_two = rows_two[pl.ds(first, group), at]
                pieces.append(
                    jnp.concatenate(
                        [
                            (a_one[k:k + 1] * b_one + a_two[k:k + 1] * b_two).astype(BF16)
                            for k in range(group)
                        ],
                        axis=0,
                    )
                )
            cross = jnp.concatenate(pieces, axis=1)
            sums = sums + dot(cross, table_ref[...])
        at_rows = pl.ds(pl.multiple_of(first * b, group * b), group * b)
        out_ref[at_rows, :] += sums
        return carry

    lax.fori_loop(0, b // group, some_rows, 0)


def forward_pass(mask, got, table, b):
    shares, days, rows, cols = got.shape
    lags = table.shape[1]
    group = 8
    return pl.pallas_call(
        functools.partial(forward_kernel, b, group),
        out_shape=jax.ShapeDtypeStruct((b * b, lags), F32),
        grid=(shares,),
        in_specs=[
            pl.BlockSpec(memory_space=pltpu.SMEM),
            pl.BlockSpec((None, days, rows, cols), lambda s: (s, 0, 0, 0)),
            pl.BlockSpec((cols, lags), lambda s: (s, 0)),
        ],
        out_specs=pl.BlockSpec((b * b, lags), lambda s: (0, 0)),
        scratch_shapes=[pltpu.VMEM((b, days * cols), F32)] * 4,
        compiler_params=pltpu.CompilerParams(vmem_limit_bytes=40 << 20),
        name="forward",
    )(mask, got, table)


def adjoint_kernel(
    sizes, scalars_ref, slot_ref, mine_ref, other_ref, observed_ref, hil_high, hil_low, got_ref, fine_ref, coarse_ref,
    out_ref, lagged, res_high, res_low, turned_a, turned_b, sums_a, sums_b,
):
    b, n_fine, n_coarse, scale = sizes
    shares, days, _, cols = got_ref.shape
    lags = mine_ref.shape[1]
    tiles = cols // TILE
    chunk = 8 * b
    pieces = [(d, t) for d in range(days) for t in range(tiles)]

    def lanes_of(d, t):
        return slice((d * tiles + t) * TILE, (d * tiles + t + 1) * TILE)

    def part(t):
        return slice(t * TILE, (t + 1) * TILE)

    def residual_rows(step, carry):
        at = pl.ds(pl.multiple_of(step * chunk, chunk), chunk)
        stacked = (mine_ref[at, :] + other_ref[at, :]) / scalars_ref[days]
        seen = observed_ref[at, :]
        seen_f = seen.astype(F32)
        hil_s = dot_split(stacked, hil_high[...], hil_low[...])
        hil_o = dot(seen, hil_high[...]) + dot(seen, hil_low[...])
        env_s = jnp.sqrt(stacked * stacked + hil_s * hil_s)
        env_o = jnp.sqrt(seen_f * seen_f + hil_o * hil_o)
        value = (stacked - seen_f) * ((1.0 + env_s) / (1.0 + env_s + env_o))
        for k in range(0, 8, 2):
            flipped = value[k * b:(k + 2) * b, :].T
            left = left_lanes((n_fine, 2 * b))
            for two in range(n_coarse // 2):
                even = flipped[2 * two * n_fine:(2 * two + 1) * n_fine, :]
                odd = flipped[(2 * two + 1) * n_fine:(2 * two + 2) * n_fine, :]
                first = jnp.where(left, even, swap_halves(odd))
                second = jnp.where(left, swap_halves(even), odd)
                lagged[two, pl.ds(step * 8 + k, n_fine, stride=b), :] = first
                lagged[two, pl.ds(step * 8 + k + 1, n_fine, stride=b), :] = second
        return carry

    lax.fori_loop(0, b // 8, residual_rows, 0)

    def split_rows(step, carry):
        at = pl.ds(pl.multiple_of(step * b, b), b)
        for two in range(n_coarse // 2):
            value = lagged[two, at, :]
            high = value.astype(BF16)
            res_high[at, part(two)] = high
            res_low[at, part(two)] = (value - high.astype(F32)).astype(BF16)
        return carry

    lax.fori_loop(0, n_fine, split_rows, 0)

    def turn(share, side, table, n, into):
        for d, t in pieces:
            u = got_ref[share, d, side * b:(side + 1) * b, part(t)].astype(F32)
            v = swap_halves(u)
            for k in range(n):
                value = u * table[share, k:k + 1, part(t)] + v * table[share, n + k:n + k + 1, part(t)]
                into[k * b:(k + 1) * b, lanes_of(d, t)] = value.astype(BF16)

    def collect(share, side, table, n, sums):
        for d, t in pieces:
            p = jnp.zeros((b, TILE), F32)
            q = jnp.zeros((b, TILE), F32)
            for k in range(n):
                h = sums[k * b:(k + 1) * b, lanes_of(d, t)]
                p = p + h * table[share, k:k + 1, part(t)]
                q = q + h * table[share, n + k:n + k + 1, part(t)]
            value = (p + swap_halves(q)) * (scalars_ref[d] * scale)
            out_ref[share, d, side * b:(side + 1) * b, part(t)] = value.astype(BF16)

    turn(0, 1, coarse_ref, n_coarse, turned_b)
    sums_b[...] = jnp.zeros_like(sums_b)
    first_dim = (((0,), (0,)), ((), ()))

    def one_share(share, carry):
        sums_a[...] = dot(res_high[...], turned_b[...]) + dot(res_low[...], turned_b[...])
        turn(share, 0, fine_ref, n_fine, turned_a)
        collect(jnp.maximum(share - 1, 0), 1, coarse_ref, n_coarse, sums_b)
        sums_b[...] = lax.dot_general(
            res_high[...], turned_a[...], first_dim, preferred_element_type=F32
        ) + lax.dot_general(res_low[...], turned_a[...], first_dim, preferred_element_type=F32)
        collect(share, 0, fine_ref, n_fine, sums_a)
        turn(jnp.minimum(share + 1, shares - 1), 1, coarse_ref, n_coarse, turned_b)
        return carry

    lax.fori_loop(0, shares, one_share, 0)
    collect(shares - 1, 1, coarse_ref, n_coarse, sums_b)


def turn_tables(columns, lags, shares):
    freqs = columns // 2
    n_fine = 16
    n_coarse = lags // n_fine
    column = np.arange(columns)
    frequency = column // TILE * HALF + column % HALF
    is_real = column % TILE < HALF

    def table(steps, sign):
        phase = frequency[None, :] * steps[:, None] % (2 * freqs)
        angles = np.pi * phase / freqs
        sine = np.where(is_real[None, :], -sign, sign) * np.sin(angles)
        rows = np.concatenate([np.cos(angles), sine]).astype(np.float32)
        return rows.reshape(rows.shape[0], shares, columns // shares).transpose(1, 0, 2)

    fine = table(np.arange(n_fine), 1)
    coarse = table(n_fine * np.arange(n_coarse) - lags // 2, -1)
    return np.ascontiguousarray(fine), np.ascontiguousarray(coarse)


def adjoint_pass(scalars, slot, mine, other, observed, hil_high, hil_low, got, fine, coarse):
    shares, days, rows, cols = got.shape
    b = rows // 2
    lags = mine.shape[1]
    n_fine = fine.shape[1] // 2
    n_coarse = coarse.shape[1] // 2
    scale = 1.0 / math.sqrt(shares * cols // 2)
    vmem = pl.BlockSpec(memory_space=pltpu.VMEM)
    spec = pltpu.PrefetchScalarGridSpec(
        num_scalar_prefetch=1,
        grid=(1,),
        in_specs=[
            pl.BlockSpec(memory_space=pltpu.SMEM),
            vmem,
            vmem,
            pl.BlockSpec((None, b * b, lags), lambda s, slot_ref: (slot_ref[0], 0, 0)),
            vmem,
            vmem,
            vmem,
            vmem,
            vmem,
        ],
        out_specs=vmem,
        scratch_shapes=[
            pltpu.VMEM((n_coarse // 2, n_fine * b, 2 * b), F32),
            pltpu.VMEM((n_fine * b, n_coarse * b), BF16),
            pltpu.VMEM((n_fine * b, n_coarse * b), BF16),
            pltpu.VMEM((n_fine * b, days * cols), BF16),
            pltpu.VMEM((n_coarse * b, days * cols), BF16),
            pltpu.VMEM((n_fine * b, days * cols), F32),
            pltpu.VMEM((n_coarse * b, days * cols), F32),
        ],
    )

    def kernel(slot_ref, scalars_ref, *refs):
        adjoint_kernel((b, n_fine, n_coarse, scale), scalars_ref, slot_ref, *refs)

    return pl.pallas_call(
        kernel,
        out_shape=jax.ShapeDtypeStruct(got.shape, BF16),
        grid_spec=spec,
        compiler_params=pltpu.CompilerParams(vmem_limit_bytes=48 << 20),
        name="adjoint",
    )(slot, scalars, mine, other, observed, hil_high, hil_low, got, fine, coarse)


def body(spectra, observed, pair_blocks, members, day_mask):
    shares = lax.axis_size("pairs")
    slots, b, _, lags = observed.shape
    _, stations, cols = spectra.shape
    forward = dft_table(shares * cols, lags)
    fine, coarse = turn_tables(shares * cols, lags, shares)
    hil_high, hil_low = hilbert_parts(lags)
    slot = lax.axis_index("slot")
    members = members.reshape(1, stations)
    first_day = lax.axis_index("outer") * slots * CORES + lax.axis_index("core")
    mask = lax.dynamic_slice_in_dim(day_mask, slot, 1, 0)[0].astype(F32)
    mask_here = jnp.stack([lax.dynamic_index_in_dim(mask, first_day + k * CORES, 0, False) for k in range(slots)])
    count = jnp.sum(mask)
    scalars = jnp.concatenate([mask_here / count, count[None]])

    sent = pack(pair_blocks, members, spectra, b)
    got = lax.all_to_all(sent, ("pairs", "slot"), 0, 0, tiled=True)
    got = got.reshape(shares, slots, 2 * b, cols)
    mine = forward_pass(mask_here, got, forward, b)
    for axis in ("outer", "core"):
        n = lax.axis_size(axis)
        others = [lax.ppermute(mine, axis, [(i, (i + k) % n) for i in range(n)]) for k in range(1, n)]
        if axis == "outer":
            for other in others:
                mine = mine + other
    contrib = adjoint_pass(
        scalars, slot[None], mine, others[0], observed.reshape(slots, b * b, lags), hil_high, hil_low, got, fine, coarse
    )
    returned = lax.all_to_all(
        contrib.reshape(shares * slots, 2 * b, cols), ("pairs", "slot"), 0, 0, tiled=True
    )
    return unpack(pair_blocks, members, returned, stations)


def solution(mesh):
    shares, days = mesh.devices.shape
    names = ("pairs", "outer", "slot", "core")

    def run(spectra, observed, pair_blocks, members, day_mask):
        slots = observed.shape[0] // shares
        split = (shares, days // CORES // slots, slots, CORES)
        finer = Mesh(mesh.devices.reshape(split), names)
        day_axes = names[1:]
        return jax.shard_map(
            body,
            mesh=finer,
            in_specs=(
                P(day_axes, None, "pairs"),
                P("pairs", None, None, None),
                P(),
                P(),
                P("pairs", None),
            ),
            out_specs=P(day_axes, None, "pairs"),
            check_vma=False,
        )(spectra, observed, pair_blocks, members, day_mask)

    return run
```

```python
import functools
import math

import jax
import jax.numpy as jnp
import ml_dtypes
import numpy as np
from jax import lax
from jax.experimental import pallas as pl
from jax.experimental.pallas import tpu as pltpu
from jax.sharding import Mesh, PartitionSpec as P

HALF = 64
TILE = 128
CORES = 2
F32 = jnp.float32
BF16 = jnp.bfloat16


def dft_table(columns, lags):
    freqs = columns // 2
    column = np.arange(columns)
    frequency = column // TILE * HALF + column % HALF
    is_real = column % TILE < HALF
    phase = frequency[:, None] * (np.arange(lags) - lags // 2)[None, :] % (2 * freqs)
    angles = np.float32(math.pi) * phase.astype(np.float32) / np.float32(freqs)
    scale = np.float32(1.0 / math.sqrt(freqs))
    cosine = np.cos(angles) * scale
    sine = np.sin(angles) * scale
    return np.where(is_real[:, None], cosine, -sine).astype(ml_dtypes.bfloat16)


def hilbert_parts(lags):
    offset = (np.arange(lags)[None, :] - np.arange(lags)[:, None]) % lags
    angles = np.float32(math.pi) * offset.astype(np.float32) / np.float32(lags)
    odd = offset % 2 == 1
    safe = np.where(odd, np.sin(angles), np.float32(1.0))
    table = np.where(odd, np.float32(2.0 / lags) * np.cos(angles) / safe, np.float32(0.0))
    table = table.astype(np.float32)
    high = table.astype(ml_dtypes.bfloat16)
    low = (table - high.astype(np.float32)).astype(ml_dtypes.bfloat16)
    return high, low


def left_lanes(shape):
    return lax.broadcasted_iota(jnp.int32, shape, len(shape) - 1) % TILE < HALF


def swap_halves(x):
    return pltpu.roll(x, HALF, 1)


def dot(a, b):
    return jnp.dot(a, b, preferred_element_type=F32)


def dot_split(x, high, low):
    x_high = x.astype(BF16)
    x_low = (x - x_high.astype(F32)).astype(BF16)
    return dot(x_high, high) + (dot(x_high, low) + dot(x_low, high))


def pack_kernel(blocks_ref, members_ref, spectra_ref, out_ref, ordered):
    stations = spectra_ref.shape[1]
    b = out_ref.shape[1] // 2
    station = lax.broadcasted_iota(jnp.int32, (stations, stations), 0)
    chosen = (station == members_ref[...]).astype(F32).astype(BF16)
    ordered[...] = lax.dot_general(
        chosen, spectra_ref[0], (((0,), (0,)), ((), ())), preferred_element_type=F32
    ).astype(BF16)
    for p in range(out_ref.shape[0]):
        for side in range(2):
            row = pl.multiple_of(blocks_ref[p, side] * b, b)
            out_ref[p, side * b:(side + 1) * b, :] = ordered[pl.ds(row, b), :]


def pack(pair_blocks, members, spectra, b):
    _, stations, cols = spectra.shape
    n_pairs = pair_blocks.shape[0]
    return pl.pallas_call(
        pack_kernel,
        out_shape=jax.ShapeDtypeStruct((n_pairs, 2 * b, cols), BF16),
        in_specs=[
            pl.BlockSpec(memory_space=pltpu.SMEM),
            pl.BlockSpec(memory_space=pltpu.VMEM),
            pl.BlockSpec(memory_space=pltpu.VMEM),
        ],
        out_specs=pl.BlockSpec(memory_space=pltpu.VMEM),
        scratch_shapes=[pltpu.VMEM((stations, cols), BF16)],
        compiler_params=pltpu.CompilerParams(vmem_limit_bytes=32 << 20),
        name="pack",
    )(pair_blocks, members, spectra)


def unpack_kernel(blocks_ref, members_ref, got_ref, out_ref, total):
    stations = out_ref.shape[1]
    b = got_ref.shape[1] // 2
    total[...] = jnp.zeros_like(total)
    for p in range(got_ref.shape[0]):
        for side in range(2):
            rows = pl.ds(pl.multiple_of(blocks_ref[p, side] * b, b), b)
            total[rows, :] += got_ref[p, side * b:(side + 1) * b, :].astype(F32)
    station = lax.broadcasted_iota(jnp.int32, (stations, stations), 0)
    chosen = (station == members_ref[...]).astype(F32).astype(BF16)
    whole = total[...]
    high = whole.astype(BF16)
    rest = whole - high.astype(F32)
    mid = rest.astype(BF16)
    low = (rest - mid.astype(F32)).astype(BF16)
    out_ref[0] = dot(chosen, high) + (dot(chosen, mid) + dot(chosen, low))


def unpack(pair_blocks, members, got, stations):
    cols = got.shape[2]
    return pl.pallas_call(
        unpack_kernel,
        out_shape=jax.ShapeDtypeStruct((1, stations, cols), F32),
        in_specs=[
            pl.BlockSpec(memory_space=pltpu.SMEM),
            pl.BlockSpec(memory_space=pltpu.VMEM),
            pl.BlockSpec(memory_space=pltpu.VMEM),
        ],
        out_specs=pl.BlockSpec(memory_space=pltpu.VMEM),
        scratch_shapes=[pltpu.VMEM((stations, cols), F32)],
        compiler_params=pltpu.CompilerParams(vmem_limit_bytes=32 << 20),
        name="unpack",
    )(pair_blocks, members, got)


def forward_kernel(b, group, mask_ref, got_ref, table_ref, out_ref, rows_one, rows_two, cols_one, cols_two):
    days = got_ref.shape[0]
    cols = got_ref.shape[2]
    lanes = left_lanes((b, TILE))
    sign = jnp.where(lanes, F32(1.0), F32(-1.0))

    @pl.when(pl.program_id(0) == 0)
    def _():
        out_ref[...] = jnp.zeros_like(out_ref)

    for d in range(days):
        for t in range(cols // TILE):
            at = slice((d * (cols // TILE) + t) * TILE, (d * (cols // TILE) + t + 1) * TILE)
            u_a = got_ref[d, :b, t * TILE:(t + 1) * TILE].astype(F32) * mask_ref[d]
            u_b = got_ref[d, b:, t * TILE:(t + 1) * TILE].astype(F32)
            v_a = swap_halves(u_a)
            v_b = swap_halves(u_b)
            rows_one[:, at] = u_a
            rows_two[:, at] = v_a * sign
            cols_one[:, at] = jnp.where(lanes, u_b, v_b)
            cols_two[:, at] = jnp.where(lanes, v_b, u_b)

    def some_rows(step, carry):
        first = pl.multiple_of(step * group, group)
        sums = jnp.zeros((group * b, out_ref.shape[1]), F32)
        for d in range(days):
            pieces = []
            for t in range(cols // TILE):
                at = slice((d * (cols // TILE) + t) * TILE, (d * (cols // TILE) + t + 1) * TILE)
                b_one = cols_one[:, at]
                b_two = cols_two[:, at]
                a_one = rows_one[pl.ds(first, group), at]
                a_two = rows_two[pl.ds(first, group), at]
                pieces.append(
                    jnp.concatenate(
                        [
                            (a_one[k:k + 1] * b_one + a_two[k:k + 1] * b_two).astype(BF16)
                            for k in range(group)
                        ],
                        axis=0,
                    )
                )
            cross = jnp.concatenate(pieces, axis=1)
            sums = sums + dot(cross, table_ref[...])
        at_rows = pl.ds(pl.multiple_of(first * b, group * b), group * b)
        out_ref[at_rows, :] += sums
        return carry

    lax.fori_loop(0, b // group, some_rows, 0)


def forward_pass(mask, got, table, b):
    shares, days, rows, cols = got.shape
    lags = table.shape[1]
    group = 8
    return pl.pallas_call(
        functools.partial(forward_kernel, b, group),
        out_shape=jax.ShapeDtypeStruct((b * b, lags), F32),
        grid=(shares,),
        in_specs=[
            pl.BlockSpec(memory_space=pltpu.SMEM),
            pl.BlockSpec((None, days, rows, cols), lambda s: (s, 0, 0, 0)),
            pl.BlockSpec((cols, lags), lambda s: (s, 0)),
        ],
        out_specs=pl.BlockSpec((b * b, lags), lambda s: (0, 0)),
        scratch_shapes=[pltpu.VMEM((b, days * cols), F32)] * 4,
        compiler_params=pltpu.CompilerParams(vmem_limit_bytes=40 << 20),
        name="forward",
    )(mask, got, table)


def adjoint_kernel(
    sizes, scalars_ref, slot_ref, mine_ref, other_ref, observed_ref, hil_high, hil_low, got_ref, fine_ref, coarse_ref,
    out_ref, lagged, res, res_t, turned_a, turned_b, sums_a, sums_b,
):
    b, n_fine, n_coarse, scale = sizes
    shares, days, _, cols = got_ref.shape
    lags = mine_ref.shape[1]
    tiles = cols // TILE
    chunk = 8 * b
    pieces = [(d, t) for d in range(days) for t in range(tiles)]

    def lanes_of(d, t):
        return slice((d * tiles + t) * TILE, (d * tiles + t + 1) * TILE)

    def part(t):
        return slice(t * TILE, (t + 1) * TILE)

    def residual_rows(step, carry):
        at = pl.ds(pl.multiple_of(step * chunk, chunk), chunk)
        stacked = (mine_ref[at, :] + other_ref[at, :]) / scalars_ref[days]
        seen = observed_ref[at, :]
        seen_f = seen.astype(F32)
        hil_s = dot_split(stacked, hil_high[...], hil_low[...])
        hil_o = dot(seen, hil_high[...]) + dot(seen, hil_low[...])
        env_s = jnp.sqrt(stacked * stacked + hil_s * hil_s)
        env_o = jnp.sqrt(seen_f * seen_f + hil_o * hil_o)
        value = (stacked - seen_f) * ((1.0 + env_s) / (1.0 + env_s + env_o))
        for k in range(0, 8, 2):
            flipped = value[k * b:(k + 2) * b, :].T
            left = left_lanes((n_fine, 2 * b))
            for two in range(n_coarse // 2):
                even = flipped[2 * two * n_fine:(2 * two + 1) * n_fine, :]
                odd = flipped[(2 * two + 1) * n_fine:(2 * two + 2) * n_fine, :]
                first = jnp.where(left, even, swap_halves(odd))
                second = jnp.where(left, swap_halves(even), odd)
                lagged[two, pl.ds(step * 8 + k, n_fine, stride=b), :] = first
                lagged[two, pl.ds(step * 8 + k + 1, n_fine, stride=b), :] = second
        return carry

    lax.fori_loop(0, b // 8, residual_rows, 0)

    def round_rows(step, carry):
        at = pl.ds(pl.multiple_of(step * 2 * b, 2 * b), 2 * b)
        for two in range(n_coarse // 2):
            value = lagged[two, at, :]
            res[at, part(two)] = value.astype(BF16)
            res_t[part(two), at] = value.T.astype(BF16)
        return carry

    lax.fori_loop(0, n_fine // 2, round_rows, 0)

    def turn(share, side, table, n, into):
        for d, t in pieces:
            u = got_ref[share, d, side * b:(side + 1) * b, part(t)].astype(F32)
            v = swap_halves(u)
            for k in range(n):
                value = u * table[share, k:k + 1, part(t)] + v * table[share, n + k:n + k + 1, part(t)]
                into[k * b:(k + 1) * b, lanes_of(d, t)] = value.astype(BF16)

    def collect(share, side, table, n, sums):
        for d, t in pieces:
            p = jnp.zeros((b, TILE), F32)
            q = jnp.zeros((b, TILE), F32)
            for k in range(n):
                h = sums[k * b:(k + 1) * b, lanes_of(d, t)]
                p = p + h * table[share, k:k + 1, part(t)]
                q = q + h * table[share, n + k:n + k + 1, part(t)]
            value = (p + swap_halves(q)) * (scalars_ref[d] * scale)
            out_ref[share, d, side * b:(side + 1) * b, part(t)] = value.astype(BF16)

    turn(0, 1, coarse_ref, n_coarse, turned_b)
    sums_b[...] = jnp.zeros_like(sums_b)

    def one_share(share, carry):
        sums_a[...] = dot(res[...], turned_b[...])
        turn(share, 0, fine_ref, n_fine, turned_a)
        collect(jnp.maximum(share - 1, 0), 1, coarse_ref, n_coarse, sums_b)
        sums_b[...] = dot(res_t[...], turned_a[...])
        collect(share, 0, fine_ref, n_fine, sums_a)
        turn(jnp.minimum(share + 1, shares - 1), 1, coarse_ref, n_coarse, turned_b)
        return carry

    lax.fori_loop(0, shares, one_share, 0)
    collect(shares - 1, 1, coarse_ref, n_coarse, sums_b)


def turn_tables(columns, lags, shares):
    freqs = columns // 2
    n_fine = 16
    n_coarse = lags // n_fine
    column = np.arange(columns)
    frequency = column // TILE * HALF + column % HALF
    is_real = column % TILE < HALF

    def table(steps, sign):
        phase = frequency[None, :] * steps[:, None] % (2 * freqs)
        angles = np.pi * phase / freqs
        sine = np.where(is_real[None, :], -sign, sign) * np.sin(angles)
        rows = np.concatenate([np.cos(angles), sine]).astype(np.float32)
        return rows.reshape(rows.shape[0], shares, columns // shares).transpose(1, 0, 2)

    fine = table(np.arange(n_fine), 1)
    coarse = table(n_fine * np.arange(n_coarse) - lags // 2, -1)
    return np.ascontiguousarray(fine), np.ascontiguousarray(coarse)


def adjoint_pass(scalars, slot, mine, other, observed, hil_high, hil_low, got, fine, coarse):
    shares, days, rows, cols = got.shape
    b = rows // 2
    lags = mine.shape[1]
    n_fine = fine.shape[1] // 2
    n_coarse = coarse.shape[1] // 2
    scale = 1.0 / math.sqrt(shares * cols // 2)
    vmem = pl.BlockSpec(memory_space=pltpu.VMEM)
    spec = pltpu.PrefetchScalarGridSpec(
        num_scalar_prefetch=1,
        grid=(1,),
        in_specs=[
            pl.BlockSpec(memory_space=pltpu.SMEM),
            vmem,
            vmem,
            pl.BlockSpec((None, b * b, lags), lambda s, slot_ref: (slot_ref[0], 0, 0)),
            vmem,
            vmem,
            vmem,
            vmem,
            vmem,
        ],
        out_specs=vmem,
        scratch_shapes=[
            pltpu.VMEM((n_coarse // 2, n_fine * b, 2 * b), F32),
            pltpu.VMEM((n_fine * b, n_coarse * b), BF16),
            pltpu.VMEM((n_coarse * b, n_fine * b), BF16),
            pltpu.VMEM((n_fine * b, days * cols), BF16),
            pltpu.VMEM((n_coarse * b, days * cols), BF16),
            pltpu.VMEM((n_fine * b, days * cols), F32),
            pltpu.VMEM((n_coarse * b, days * cols), F32),
        ],
    )

    def kernel(slot_ref, scalars_ref, *refs):
        adjoint_kernel((b, n_fine, n_coarse, scale), scalars_ref, slot_ref, *refs)

    return pl.pallas_call(
        kernel,
        out_shape=jax.ShapeDtypeStruct(got.shape, BF16),
        grid_spec=spec,
        compiler_params=pltpu.CompilerParams(vmem_limit_bytes=48 << 20),
        name="adjoint",
    )(slot, scalars, mine, other, observed, hil_high, hil_low, got, fine, coarse)


def body(spectra, observed, pair_blocks, members, day_mask):
    shares = lax.axis_size("pairs")
    slots, b, _, lags = observed.shape
    _, stations, cols = spectra.shape
    forward = dft_table(shares * cols, lags)
    fine, coarse = turn_tables(shares * cols, lags, shares)
    hil_high, hil_low = hilbert_parts(lags)
    slot = lax.axis_index("slot")
    members = members.reshape(1, stations)
    first_day = lax.axis_index("outer") * slots * CORES + lax.axis_index("core")
    mask = lax.dynamic_slice_in_dim(day_mask, slot, 1, 0)[0].astype(F32)
    mask_here = jnp.stack([lax.dynamic_index_in_dim(mask, first_day + k * CORES, 0, False) for k in range(slots)])
    count = jnp.sum(mask)
    scalars = jnp.concatenate([mask_here / count, count[None]])

    sent = pack(pair_blocks, members, spectra, b)
    got = lax.all_to_all(sent, ("pairs", "slot"), 0, 0, tiled=True)
    got = got.reshape(shares, slots, 2 * b, cols)
    mine = forward_pass(mask_here, got, forward, b)
    for axis in ("outer", "core"):
        n = lax.axis_size(axis)
        others = [lax.ppermute(mine, axis, [(i, (i + k) % n) for i in range(n)]) for k in range(1, n)]
        if axis == "outer":
            for other in others:
                mine = mine + other
    contrib = adjoint_pass(
        scalars, slot[None], mine, others[0], observed.reshape(slots, b * b, lags), hil_high, hil_low, got, fine, coarse
    )
    returned = lax.all_to_all(
        contrib.reshape(shares * slots, 2 * b, cols), ("pairs", "slot"), 0, 0, tiled=True
    )
    return unpack(pair_blocks, members, returned, stations)


def solution(mesh):
    shares, days = mesh.devices.shape
    names = ("pairs", "outer", "slot", "core")

    def run(spectra, observed, pair_blocks, members, day_mask):
        slots = observed.shape[0] // shares
        split = (shares, days // CORES // slots, slots, CORES)
        finer = Mesh(mesh.devices.reshape(split), names)
        day_axes = names[1:]
        return jax.shard_map(
            body,
            mesh=finer,
            in_specs=(
                P(day_axes, None, "pairs"),
                P("pairs", None, None, None),
                P(),
                P(),
                P("pairs", None),
            ),
            out_specs=P(day_axes, None, "pairs"),
            check_vma=False,
        )(spectra, observed, pair_blocks, members, day_mask)

    return run
```

```python
import functools
import math

import jax
import jax.numpy as jnp
import ml_dtypes
import numpy as np
from jax import lax
from jax.experimental import pallas as pl
from jax.experimental.pallas import tpu as pltpu
from jax.sharding import Mesh, PartitionSpec as P

HALF = 64
TILE = 128
CORES = 2
F32 = jnp.float32
BF16 = jnp.bfloat16


def hilbert_parts(lags):
    offset = (np.arange(lags)[None, :] - np.arange(lags)[:, None]) % lags
    angles = np.float32(math.pi) * offset.astype(np.float32) / np.float32(lags)
    odd = offset % 2 == 1
    safe = np.where(odd, np.sin(angles), np.float32(1.0))
    table = np.where(odd, np.float32(2.0 / lags) * np.cos(angles) / safe, np.float32(0.0))
    table = table.astype(np.float32).T
    high = table.astype(ml_dtypes.bfloat16)
    low = (table - high.astype(np.float32)).astype(ml_dtypes.bfloat16)
    return np.concatenate([high, low, high], axis=1)


def left_lanes(shape):
    return lax.broadcasted_iota(jnp.int32, shape, len(shape) - 1) % TILE < HALF


def swap_halves(x):
    return pltpu.roll(x, HALF, 1)


def dot(a, b):
    return jnp.dot(a, b, preferred_element_type=F32)


def pack_kernel(blocks_ref, members_ref, spectra_ref, out_ref, ordered):
    stations = spectra_ref.shape[1]
    b = out_ref.shape[1] // 2
    station = lax.broadcasted_iota(jnp.int32, (stations, stations), 0)
    chosen = (station == members_ref[...]).astype(F32).astype(BF16)
    ordered[...] = lax.dot_general(
        chosen, spectra_ref[0], (((0,), (0,)), ((), ())), preferred_element_type=F32
    ).astype(BF16)
    for p in range(out_ref.shape[0]):
        for side in range(2):
            row = pl.multiple_of(blocks_ref[p, side] * b, b)
            out_ref[p, side * b:(side + 1) * b, :] = ordered[pl.ds(row, b), :]


def pack(pair_blocks, members, spectra, b):
    _, stations, cols = spectra.shape
    n_pairs = pair_blocks.shape[0]
    return pl.pallas_call(
        pack_kernel,
        out_shape=jax.ShapeDtypeStruct((n_pairs, 2 * b, cols), BF16),
        in_specs=[
            pl.BlockSpec(memory_space=pltpu.SMEM),
            pl.BlockSpec(memory_space=pltpu.VMEM),
            pl.BlockSpec(memory_space=pltpu.VMEM),
        ],
        out_specs=pl.BlockSpec(memory_space=pltpu.VMEM),
        scratch_shapes=[pltpu.VMEM((stations, cols), BF16)],
        compiler_params=pltpu.CompilerParams(vmem_limit_bytes=32 << 20),
        name="pack",
    )(pair_blocks, members, spectra)


def unpack_kernel(blocks_ref, members_ref, got_ref, out_ref, total):
    stations = out_ref.shape[1]
    b = got_ref.shape[1] // 2
    total[...] = jnp.zeros_like(total)
    for p in range(got_ref.shape[0]):
        for side in range(2):
            rows = pl.ds(pl.multiple_of(blocks_ref[p, side] * b, b), b)
            total[rows, :] += got_ref[p, side * b:(side + 1) * b, :].astype(F32)
    station = lax.broadcasted_iota(jnp.int32, (stations, stations), 0)
    chosen = (station == members_ref[...]).astype(F32).astype(BF16)
    whole = total[...]
    high = whole.astype(BF16)
    rest = whole - high.astype(F32)
    mid = rest.astype(BF16)
    low = (rest - mid.astype(F32)).astype(BF16)
    out_ref[0] = dot(chosen, high) + (dot(chosen, mid) + dot(chosen, low))


def unpack(pair_blocks, members, got, stations):
    cols = got.shape[2]
    return pl.pallas_call(
        unpack_kernel,
        out_shape=jax.ShapeDtypeStruct((1, stations, cols), F32),
        in_specs=[
            pl.BlockSpec(memory_space=pltpu.SMEM),
            pl.BlockSpec(memory_space=pltpu.VMEM),
            pl.BlockSpec(memory_space=pltpu.VMEM),
        ],
        out_specs=pl.BlockSpec(memory_space=pltpu.VMEM),
        scratch_shapes=[pltpu.VMEM((stations, cols), F32)],
        compiler_params=pltpu.CompilerParams(vmem_limit_bytes=32 << 20),
        name="unpack",
    )(pair_blocks, members, got)


def prepare_kernel(b, slot_ref, observed_ref, hilbert_ref, seen_ref, env_ref):
    lags = observed_ref.shape[1]
    two = 2 * b

    def some(step, carry):
        seen = [
            observed_ref[pl.ds(pl.multiple_of((2 * step + k) * two, two), two), :].astype(F32).T for k in range(2)
        ]
        seen = jnp.concatenate(seen, axis=1)
        seen_b = seen.astype(BF16)
        hil = dot(hilbert_ref[:, :2 * lags], jnp.concatenate([seen_b, seen_b], axis=0))
        seen_ref[step] = seen_b
        env_ref[step] = 1.0 + jnp.sqrt(seen * seen + hil * hil)
        return carry

    lax.fori_loop(0, b // 4, some, 0, unroll=2)


def prepare(slot, observed, hilbert):
    _, rows, lags = observed.shape
    b = math.isqrt(rows)
    vmem = pl.BlockSpec(memory_space=pltpu.VMEM)
    spec = pltpu.PrefetchScalarGridSpec(
        num_scalar_prefetch=1,
        grid=(1,),
        in_specs=[pl.BlockSpec((None, rows, lags), lambda s, slot_ref: (slot_ref[0], 0, 0)), vmem],
        out_specs=[vmem, vmem],
    )
    shape = (b // 4, lags, 4 * b)
    return pl.pallas_call(
        functools.partial(prepare_kernel, b),
        out_shape=[jax.ShapeDtypeStruct(shape, BF16), jax.ShapeDtypeStruct(shape, F32)],
        grid_spec=spec,
        compiler_params=pltpu.CompilerParams(vmem_limit_bytes=16 << 20),
        cost_estimate=pl.CostEstimate(flops=2 * rows * lags * lags, bytes_accessed=8 * rows * lags, transcendentals=0),
        name="prepare",
    )(slot, observed, hilbert)


def tile_lanes(tiles, d, t):
    return slice((d * tiles + t) * TILE, (d * tiles + t + 1) * TILE)


def part(t):
    return slice(t * TILE, (t + 1) * TILE)


def forward_kernel(b, mask_ref, got_ref, fine_ref, coarse_ref, out_ref, turned_a, turned_b, masked):
    shares, days, _, cols = got_ref.shape
    tiles = cols // TILE
    n_fine = fine_ref.shape[1] // 2
    n_coarse = coarse_ref.shape[1] // 2
    slabs = out_ref.shape[0]
    out_ref[...] = jnp.zeros_like(out_ref)

    def turn(share, side, table, n, into):
        for d in range(days):
            for t in range(tiles):
                at = tile_lanes(tiles, d, t)
                u = got_ref[share, d, side * b:(side + 1) * b, part(t)].astype(F32)
                v = swap_halves(u)
                for k in range(n):
                    value = u * table[share, k:k + 1, part(t)] + v * table[share, n + k:n + k + 1, part(t)]
                    into[share, k * b:(k + 1) * b, at] = value.astype(BF16)

    def use(share):
        for d in range(days):
            at = slice(d * cols, (d + 1) * cols)
            masked[:, at] = turned_b[share, :, at] * mask_ref[d].astype(BF16)
        sums = lax.dot_general(
            turned_a[share], masked[...], (((1,), (1,)), ((), ())), preferred_element_type=F32
        )
        for k in range(slabs):
            out_ref[k] += sums[:, k * 2 * b:(k + 1) * 2 * b]

    turn(0, 1, coarse_ref, n_coarse, turned_b)
    turn(0, 0, fine_ref, n_fine, turned_a)

    def one_share(share, carry):
        use(share)
        turn(share + 1, 1, coarse_ref, n_coarse, turned_b)
        turn(share + 1, 0, fine_ref, n_fine, turned_a)
        return carry

    lax.fori_loop(0, shares - 1, one_share, 0)
    use(shares - 1)


def forward_pass(mask, got, fine, coarse):
    shares, days, rows, cols = got.shape
    b = rows // 2
    n_fine = fine.shape[1] // 2
    n_coarse = coarse.shape[1] // 2
    vmem = pl.BlockSpec(memory_space=pltpu.VMEM)
    return pl.pallas_call(
        functools.partial(forward_kernel, b),
        out_shape=[
            jax.ShapeDtypeStruct((n_coarse // 2, n_fine * b, 2 * b), F32),
            jax.ShapeDtypeStruct((shares, n_fine * b, days * cols), BF16),
            jax.ShapeDtypeStruct((shares, n_coarse * b, days * cols), BF16),
        ],
        in_specs=[pl.BlockSpec(memory_space=pltpu.SMEM), vmem, vmem, vmem],
        out_specs=[vmem] * 3,
        scratch_shapes=[pltpu.VMEM((n_coarse * b, days * cols), BF16)],
        compiler_params=pltpu.CompilerParams(vmem_limit_bytes=24 << 20),
        name="forward",
    )(mask, got, fine, coarse)


def adjoint_kernel(
    sizes, scalars_ref, mine_ref, other_ref, seen_ref, env_ref, hilbert_ref, turned_a, turned_b, fine_ref, coarse_ref,
    out_ref, lagged, res, res_t, sums_a, sums_b,
):
    b, scale = sizes
    shares, days, _, cols = out_ref.shape
    lags = seen_ref.shape[1]
    n_fine = fine_ref.shape[1] // 2
    n_coarse = coarse_ref.shape[1] // 2
    slabs = n_coarse // 2
    tiles = cols // TILE
    left = left_lanes((n_fine, 2 * b))

    def residual_rows(step, carry):
        halves = []
        for k in (0, 2):
            rows = []
            for slab in range(slabs):
                got = []
                for j in (0, 1):
                    at = pl.ds(4 * step + k + j, n_fine, stride=b)
                    got.append((mine_ref[slab, at, :] + other_ref[slab, at, :]) * scalars_ref[days])
                rows.append(jnp.where(left, got[0], swap_halves(got[1])))
                rows.append(jnp.where(left, swap_halves(got[0]), got[1]))
            halves.append(jnp.concatenate(rows, axis=0))
        stacked = jnp.concatenate(halves, axis=1)
        high = stacked.astype(BF16)
        low = (stacked - high.astype(F32)).astype(BF16)
        hil = dot(hilbert_ref[...], jnp.concatenate([high, high, low], axis=0))
        env_s = 1.0 + jnp.sqrt(stacked * stacked + hil * hil)
        env_o = env_ref[step]
        value = (stacked - seen_ref[step].astype(F32)) * (env_s / (env_s + env_o - 1.0))
        for k in (0, 2):
            lanes = slice(k * b, (k + 2) * b)
            for slab in range(slabs):
                even = value[2 * slab * n_fine:(2 * slab + 1) * n_fine, lanes]
                odd = value[(2 * slab + 1) * n_fine:(2 * slab + 2) * n_fine, lanes]
                first = jnp.where(left, even, swap_halves(odd))
                second = jnp.where(left, swap_halves(even), odd)
                lagged[slab, pl.ds(4 * step + k, n_fine, stride=b), :] = first
                lagged[slab, pl.ds(4 * step + k + 1, n_fine, stride=b), :] = second
        return carry

    lax.fori_loop(0, b // 4, residual_rows, 0, unroll=2)

    def round_rows(step, carry):
        at = pl.ds(pl.multiple_of(step * 2 * b, 2 * b), 2 * b)
        for slab in range(slabs):
            value = lagged[slab, at, :]
            here = slice(slab * 2 * b, (slab + 1) * 2 * b)
            res[at, here] = value.astype(BF16)
            res_t[here, at] = value.T.astype(BF16)
        return carry

    lax.fori_loop(0, n_fine // 2, round_rows, 0)

    def collect(share, side, table, n, sums):
        for d in range(days):
            for t in range(tiles):
                at = tile_lanes(tiles, d, t)
                p = jnp.zeros((b, TILE), F32)
                q = jnp.zeros((b, TILE), F32)
                for k in range(n):
                    h = sums[k * b:(k + 1) * b, at]
                    p = p + h * table[share, k:k + 1, part(t)]
                    q = q + h * table[share, n + k:n + k + 1, part(t)]
                value = (p + swap_halves(q)) * (scalars_ref[d] * scale)
                out_ref[share, d, side * b:(side + 1) * b, part(t)] = value.astype(BF16)

    sums_b[...] = jnp.zeros_like(sums_b)

    def one_share(share, carry):
        sums_a[...] = dot(res[...], turned_b[share])
        collect(jnp.maximum(share - 1, 0), 1, coarse_ref, n_coarse, sums_b)
        sums_b[...] = dot(res_t[...], turned_a[share])
        collect(share, 0, fine_ref, n_fine, sums_a)
        return carry

    lax.fori_loop(0, shares, one_share, 0)
    collect(shares - 1, 1, coarse_ref, n_coarse, sums_b)


def turn_tables(columns, lags, shares):
    freqs = columns // 2
    n_fine = 16
    n_coarse = lags // n_fine
    column = np.arange(columns)
    frequency = column // TILE * HALF + column % HALF
    is_real = column % TILE < HALF

    def table(steps, sign):
        phase = frequency[None, :] * steps[:, None] % (2 * freqs)
        angles = np.pi * phase / freqs
        sine = np.where(is_real[None, :], -sign, sign) * np.sin(angles)
        rows = np.concatenate([np.cos(angles), sine]).astype(np.float32)
        return rows.reshape(rows.shape[0], shares, columns // shares).transpose(1, 0, 2)

    fine = table(np.arange(n_fine), 1)
    coarse = table(n_fine * np.arange(n_coarse) - lags // 2, -1)
    return np.ascontiguousarray(fine), np.ascontiguousarray(coarse)


def adjoint_pass(scalars, mine, other, seen, env, hilbert, turned_a, turned_b, fine, coarse):
    shares, _, days_cols = turned_a.shape
    cols = fine.shape[2]
    n_fine = fine.shape[1] // 2
    n_coarse = coarse.shape[1] // 2
    b = turned_a.shape[1] // n_fine
    days = days_cols // cols
    scale = 1.0 / math.sqrt(shares * cols // 2)
    vmem = pl.BlockSpec(memory_space=pltpu.VMEM)
    return pl.pallas_call(
        functools.partial(adjoint_kernel, (b, scale)),
        out_shape=jax.ShapeDtypeStruct((shares, days, 2 * b, cols), BF16),
        in_specs=[pl.BlockSpec(memory_space=pltpu.SMEM)] + [vmem] * 9,
        out_specs=vmem,
        scratch_shapes=[
            pltpu.VMEM((n_coarse // 2, n_fine * b, 2 * b), F32),
            pltpu.VMEM((n_fine * b, n_coarse * b), BF16),
            pltpu.VMEM((n_coarse * b, n_fine * b), BF16),
            pltpu.VMEM((n_fine * b, days_cols), F32),
            pltpu.VMEM((n_coarse * b, days_cols), F32),
        ],
        compiler_params=pltpu.CompilerParams(vmem_limit_bytes=32 << 20),
        name="adjoint",
    )(scalars, mine, other, seen, env, hilbert, turned_a, turned_b, fine, coarse)


def body(spectra, observed, pair_blocks, members, day_mask):
    shares = lax.axis_size("pairs")
    slots, b, _, lags = observed.shape
    _, stations, cols = spectra.shape
    fine, coarse = turn_tables(shares * cols, lags, shares)
    hilbert = hilbert_parts(lags)
    slot = lax.axis_index("slot")
    members = members.reshape(1, stations)
    first_day = lax.axis_index("outer") * slots * CORES + lax.axis_index("core")
    mask = lax.dynamic_slice_in_dim(day_mask, slot, 1, 0)[0].astype(F32)
    mask_here = jnp.stack([lax.dynamic_index_in_dim(mask, first_day + k * CORES, 0, False) for k in range(slots)])
    count = jnp.sum(mask)
    scale = 1.0 / math.sqrt(shares * cols // 2)
    scalars = jnp.concatenate([mask_here / count, scale / count[None]])

    sent = pack(pair_blocks, members, spectra, b)
    got = lax.all_to_all(sent, ("pairs", "slot"), 0, 0, tiled=True)
    got = got.reshape(shares, slots, 2 * b, cols)
    seen, env = prepare(slot[None], observed.reshape(slots, b * b, lags), hilbert)
    mine, turned_a, turned_b = forward_pass(mask_here, got, fine, coarse)
    for axis in ("outer", "core"):
        n = lax.axis_size(axis)
        others = [lax.ppermute(mine, axis, [(i, (i + k) % n) for i in range(n)]) for k in range(1, n)]
        if axis == "outer":
            for other in others:
                mine = mine + other
    contrib = adjoint_pass(scalars, mine, others[0], seen, env, hilbert, turned_a, turned_b, fine, coarse)
    returned = lax.all_to_all(
        contrib.reshape(shares * slots, 2 * b, cols), ("pairs", "slot"), 0, 0, tiled=True
    )
    return unpack(pair_blocks, members, returned, stations)


def solution(mesh):
    shares, days = mesh.devices.shape
    names = ("pairs", "outer", "slot", "core")

    def run(spectra, observed, pair_blocks, members, day_mask):
        slots = observed.shape[0] // shares
        split = (shares, days // CORES // slots, slots, CORES)
        finer = Mesh(mesh.devices.reshape(split), names)
        day_axes = names[1:]
        return jax.shard_map(
            body,
            mesh=finer,
            in_specs=(
                P(day_axes, None, "pairs"),
                P("pairs", None, None, None),
                P(),
                P(),
                P("pairs", None),
            ),
            out_specs=P(day_axes, None, "pairs"),
            check_vma=False,
        )(spectra, observed, pair_blocks, members, day_mask)

    return run
```

```python
import functools
import math

import jax
import jax.numpy as jnp
import ml_dtypes
import numpy as np
from jax import lax
from jax.experimental import pallas as pl
from jax.experimental.pallas import tpu as pltpu
from jax.sharding import Mesh, PartitionSpec as P

HALF = 64
TILE = 128
CORES = 2
F32 = jnp.float32
BF16 = jnp.bfloat16


def hilbert_parts(lags):
    offset = (np.arange(lags)[None, :] - np.arange(lags)[:, None]) % lags
    angles = np.float32(math.pi) * offset.astype(np.float32) / np.float32(lags)
    odd = offset % 2 == 1
    safe = np.where(odd, np.sin(angles), np.float32(1.0))
    table = np.where(odd, np.float32(2.0 / lags) * np.cos(angles) / safe, np.float32(0.0))
    table = table.astype(np.float32).T
    high = table.astype(ml_dtypes.bfloat16)
    low = (table - high.astype(np.float32)).astype(ml_dtypes.bfloat16)
    return np.concatenate([high, low, high], axis=1)


def left_lanes(shape):
    return lax.broadcasted_iota(jnp.int32, shape, len(shape) - 1) % TILE < HALF


def swap_halves(x):
    return pltpu.roll(x, HALF, 1)


def dot(a, b):
    return jnp.dot(a, b, preferred_element_type=F32)


def pack_kernel(blocks_ref, members_ref, spectra_ref, out_ref, ordered):
    stations = spectra_ref.shape[1]
    b = out_ref.shape[1] // 2
    station = lax.broadcasted_iota(jnp.int32, (stations, stations), 0)
    chosen = (station == members_ref[...]).astype(F32).astype(BF16)
    ordered[...] = lax.dot_general(
        chosen, spectra_ref[0], (((0,), (0,)), ((), ())), preferred_element_type=F32
    ).astype(BF16)
    for p in range(out_ref.shape[0]):
        for side in range(2):
            row = pl.multiple_of(blocks_ref[p, side] * b, b)
            out_ref[p, side * b:(side + 1) * b, :] = ordered[pl.ds(row, b), :]


def pack(pair_blocks, members, spectra, b):
    _, stations, cols = spectra.shape
    n_pairs = pair_blocks.shape[0]
    return pl.pallas_call(
        pack_kernel,
        out_shape=jax.ShapeDtypeStruct((n_pairs, 2 * b, cols), BF16),
        in_specs=[
            pl.BlockSpec(memory_space=pltpu.SMEM),
            pl.BlockSpec(memory_space=pltpu.VMEM),
            pl.BlockSpec(memory_space=pltpu.VMEM),
        ],
        out_specs=pl.BlockSpec(memory_space=pltpu.VMEM),
        scratch_shapes=[pltpu.VMEM((stations, cols), BF16)],
        compiler_params=pltpu.CompilerParams(vmem_limit_bytes=32 << 20),
        name="pack",
    )(pair_blocks, members, spectra)


def unpack_kernel(blocks_ref, members_ref, got_ref, out_ref, total):
    stations = out_ref.shape[1]
    b = got_ref.shape[1] // 2
    total[...] = jnp.zeros_like(total)
    for p in range(got_ref.shape[0]):
        for side in range(2):
            rows = pl.ds(pl.multiple_of(blocks_ref[p, side] * b, b), b)
            total[rows, :] += got_ref[p, side * b:(side + 1) * b, :].astype(F32)
    station = lax.broadcasted_iota(jnp.int32, (stations, stations), 0)
    chosen = (station == members_ref[...]).astype(F32).astype(BF16)
    whole = total[...]
    high = whole.astype(BF16)
    rest = whole - high.astype(F32)
    mid = rest.astype(BF16)
    low = (rest - mid.astype(F32)).astype(BF16)
    out_ref[0] = dot(chosen, high) + (dot(chosen, mid) + dot(chosen, low))


def unpack(pair_blocks, members, got, stations):
    cols = got.shape[2]
    return pl.pallas_call(
        unpack_kernel,
        out_shape=jax.ShapeDtypeStruct((1, stations, cols), F32),
        in_specs=[
            pl.BlockSpec(memory_space=pltpu.SMEM),
            pl.BlockSpec(memory_space=pltpu.VMEM),
            pl.BlockSpec(memory_space=pltpu.VMEM),
        ],
        out_specs=pl.BlockSpec(memory_space=pltpu.VMEM),
        scratch_shapes=[pltpu.VMEM((stations, cols), F32)],
        compiler_params=pltpu.CompilerParams(vmem_limit_bytes=32 << 20),
        name="unpack",
    )(pair_blocks, members, got)


def prepare_kernel(b, slot_ref, observed_ref, hilbert_ref, seen_ref, env_ref):
    lags = observed_ref.shape[1]
    two = 2 * b

    def some(step, carry):
        seen = [
            observed_ref[pl.ds(pl.multiple_of((2 * step + k) * two, two), two), :].astype(F32).T for k in range(2)
        ]
        seen = jnp.concatenate(seen, axis=1)
        seen_b = seen.astype(BF16)
        hil = dot(hilbert_ref[:, :2 * lags], jnp.concatenate([seen_b, seen_b], axis=0))
        seen_ref[step] = seen_b
        env_ref[step] = 1.0 + jnp.sqrt(seen * seen + hil * hil)
        return carry

    lax.fori_loop(0, b // 4, some, 0, unroll=2)


def prepare(slot, observed, hilbert):
    _, rows, lags = observed.shape
    b = math.isqrt(rows)
    vmem = pl.BlockSpec(memory_space=pltpu.VMEM)
    spec = pltpu.PrefetchScalarGridSpec(
        num_scalar_prefetch=1,
        grid=(1,),
        in_specs=[pl.BlockSpec((None, rows, lags), lambda s, slot_ref: (slot_ref[0], 0, 0)), vmem],
        out_specs=[vmem, vmem],
    )
    shape = (b // 4, lags, 4 * b)
    return pl.pallas_call(
        functools.partial(prepare_kernel, b),
        out_shape=[pltpu.VMEM(shape, BF16), pltpu.VMEM(shape, F32)],
        grid_spec=spec,
        compiler_params=pltpu.CompilerParams(vmem_limit_bytes=16 << 20),
        cost_estimate=pl.CostEstimate(flops=2 * rows * lags * lags, bytes_accessed=8 * rows * lags, transcendentals=0),
        name="prepare",
    )(slot, observed, hilbert)


def tile_lanes(tiles, d, t):
    return slice((d * tiles + t) * TILE, (d * tiles + t + 1) * TILE)


def part(t):
    return slice(t * TILE, (t + 1) * TILE)


def forward_kernel(
    b, mask_ref, got_ref, fine_ref, coarse_ref, out_ref, kept_a, kept_b, turned_a, turned_b, rows_u, rows_v, sems_a, sems_b
):
    shares, days, _, cols = got_ref.shape
    tiles = cols // TILE
    n_fine = fine_ref.shape[1] // 2
    n_coarse = coarse_ref.shape[1] // 2
    pieces = [(d, t) for d in range(days) for t in range(tiles)]
    out_ref[...] = jnp.zeros_like(out_ref)

    def make(share):
        for d, t in pieces:
            at = tile_lanes(tiles, d, t)
            u = got_ref[share, d, b:, part(t)].astype(F32)
            v = swap_halves(u)
            for k in range(n_coarse):
                cosine = coarse_ref[share, k:k + 1, part(t)]
                sine = coarse_ref[share, n_coarse + k:n_coarse + k + 1, part(t)]
                turned_b[share, k * b:(k + 1) * b, at] = (u * cosine + v * sine).astype(BF16)
        for d, t in pieces:
            at = tile_lanes(tiles, d, t)
            u = got_ref[share, d, :b, part(t)].astype(F32) * mask_ref[d]
            rows_u[:, at] = u
            rows_v[:, at] = swap_halves(u)
        for d, t in pieces:
            at = tile_lanes(tiles, d, t)
            cosine = fine_ref[share, :n_fine, part(t)]
            sine = fine_ref[share, n_fine:, part(t)]
            for k in range(b):
                value = rows_u[k:k + 1, at] * cosine + rows_v[k:k + 1, at] * sine
                turned_a[share, k * n_fine:(k + 1) * n_fine, at] = value.astype(BF16)

    def use(share):
        out_ref[...] += lax.dot_general(
            turned_a[share], turned_b[share], (((1,), (1,)), ((), ())), preferred_element_type=F32
        )

    def keep(share):
        return (
            pltpu.make_async_copy(turned_a.at[share], kept_a.at[share], sems_a.at[share]),
            pltpu.make_async_copy(turned_b.at[share], kept_b.at[share], sems_b.at[share]),
        )

    make(0)

    def one_share(share, carry):
        for copy in keep(share):
            copy.start()
        use(share)
        make(share + 1)
        return carry

    lax.fori_loop(0, shares - 1, one_share, 0)
    for copy in keep(shares - 1):
        copy.start()
    use(shares - 1)

    def finish(share, carry):
        for copy in keep(share):
            copy.wait()
        return carry

    lax.fori_loop(0, shares, finish, 0)


def forward_pass(mask, got, fine, coarse):
    shares, days, rows, cols = got.shape
    b = rows // 2
    n_fine = fine.shape[1] // 2
    n_coarse = coarse.shape[1] // 2
    vmem = pl.BlockSpec(memory_space=pltpu.VMEM)
    return pl.pallas_call(
        functools.partial(forward_kernel, b),
        out_shape=[
            jax.ShapeDtypeStruct((n_fine * b, n_coarse * b), F32),
            pltpu.HBM((shares, n_fine * b, days * cols), BF16),
            pltpu.HBM((shares, n_coarse * b, days * cols), BF16),
        ],
        in_specs=[pl.BlockSpec(memory_space=pltpu.SMEM), vmem, vmem, vmem],
        out_specs=[vmem] + [pl.BlockSpec(memory_space=pltpu.HBM)] * 2,
        scratch_shapes=[
            pltpu.VMEM((shares, n_fine * b, days * cols), BF16),
            pltpu.VMEM((shares, n_coarse * b, days * cols), BF16),
            pltpu.VMEM((b, days * cols), F32),
            pltpu.VMEM((b, days * cols), F32),
            pltpu.SemaphoreType.DMA((shares,)),
            pltpu.SemaphoreType.DMA((shares,)),
        ],
        compiler_params=pltpu.CompilerParams(vmem_limit_bytes=28 << 20),
        name="forward",
    )(mask, got, fine, coarse)


def adjoint_kernel(
    sizes, scalars_ref, mine_ref, other_ref, seen_ref, env_ref, hilbert_ref, kept_a, kept_b, fine_ref, coarse_ref,
    out_ref, lagged, back, res, res_t, sums_a, sums_b, turned_a, turned_b, sems_a, sems_b,
):
    b, scale = sizes
    shares, days, _, cols = out_ref.shape
    n_fine = fine_ref.shape[1] // 2
    n_coarse = coarse_ref.shape[1] // 2
    slabs = n_coarse // 2
    tiles = cols // TILE
    group = 8
    block = group * n_fine
    left = left_lanes((n_fine, 2 * b))

    def fetch(share):
        return (
            pltpu.make_async_copy(kept_b.at[share], turned_b.at[share], sems_b.at[share]),
            pltpu.make_async_copy(kept_a.at[share], turned_a.at[share], sems_a.at[share]),
        )

    def begin(share, carry):
        for copy in fetch(share):
            copy.start()
        return carry

    lax.fori_loop(0, shares, begin, 0)

    def residual_rows(step, carry):
        for quad in range(group // 4):
            stacked = []
            for two in (0, 2):
                rows = []
                for slab in range(slabs):
                    got = []
                    for k in (two, two + 1):
                        at = pl.ds(pl.multiple_of(step * block + (4 * quad + k) * n_fine, n_fine), n_fine)
                        got.append((mine_ref[at, part(slab)] + other_ref[at, part(slab)]) * scalars_ref[days])
                    rows.append(jnp.where(left, got[0], swap_halves(got[1])))
                    rows.append(jnp.where(left, swap_halves(got[0]), got[1]))
                stacked.append(jnp.concatenate(rows, axis=0))
            stacked = jnp.concatenate(stacked, axis=1)
            high = stacked.astype(BF16)
            low = (stacked - high.astype(F32)).astype(BF16)
            hil = dot(hilbert_ref[...], jnp.concatenate([high, high, low], axis=0))
            env_s = 1.0 + jnp.sqrt(stacked * stacked + hil * hil)
            env_o = env_ref[2 * step + quad]
            value = (stacked - seen_ref[2 * step + quad].astype(F32)) * (env_s / (env_s + env_o - 1.0))
            for two in (0, 2):
                lanes = slice(two * b, (two + 2) * b)
                for slab in range(slabs):
                    even = value[2 * slab * n_fine:(2 * slab + 1) * n_fine, lanes]
                    odd = value[(2 * slab + 1) * n_fine:(2 * slab + 2) * n_fine, lanes]
                    first = jnp.where(left, even, swap_halves(odd))
                    second = jnp.where(left, swap_halves(even), odd)
                    for k, rows in ((0, first), (1, second)):
                        a = step * group + 4 * quad + two + k
                        lagged[slab, pl.ds(a, n_fine, stride=b), :] = rows
                        at = (4 * quad + two + k) * n_fine
                        back[at:at + n_fine, part(slab)] = rows
        at = pl.ds(pl.multiple_of(step * block, block), block)
        for slab in range(slabs):
            res_t[part(slab), at] = back[:, part(slab)].T.astype(BF16)
        return carry

    lax.fori_loop(0, b // group, residual_rows, 0)

    def round_rows(step, carry):
        at = pl.ds(pl.multiple_of(step * b, b), b)
        for slab in range(slabs):
            res[at, part(slab)] = lagged[slab, at, :].astype(BF16)
        return carry

    lax.fori_loop(0, n_fine, round_rows, 0)

    def collect(share, side, table, n, sums):
        for d in range(days):
            for t in range(tiles):
                at = tile_lanes(tiles, d, t)
                p = jnp.zeros((b, TILE), F32)
                q = jnp.zeros((b, TILE), F32)
                for k in range(n):
                    h = sums[k * b:(k + 1) * b, at]
                    p = p + h * table[share, k:k + 1, part(t)]
                    q = q + h * table[share, n + k:n + k + 1, part(t)]
                value = (p + swap_halves(q)) * (scalars_ref[d] * scale)
                out_ref[share, d, side * b:(side + 1) * b, part(t)] = value.astype(BF16)

    sums_b[...] = jnp.zeros_like(sums_b)

    def one_share(share, carry):
        for copy in fetch(share):
            copy.wait()
        sums_a[...] = dot(res[...], turned_b[share])
        collect(jnp.maximum(share - 1, 0), 1, coarse_ref, n_coarse, sums_b)
        sums_b[...] = dot(res_t[...], turned_a[share])
        collect(share, 0, fine_ref, n_fine, sums_a)
        return carry

    lax.fori_loop(0, shares, one_share, 0)
    collect(shares - 1, 1, coarse_ref, n_coarse, sums_b)


def turn_tables(columns, lags, shares):
    freqs = columns // 2
    n_fine = 16
    n_coarse = lags // n_fine
    column = np.arange(columns)
    frequency = column // TILE * HALF + column % HALF
    is_real = column % TILE < HALF

    def table(steps, sign):
        phase = frequency[None, :] * steps[:, None] % (2 * freqs)
        angles = np.pi * phase / freqs
        sine = np.where(is_real[None, :], -sign, sign) * np.sin(angles)
        rows = np.concatenate([np.cos(angles), sine]).astype(np.float32)
        return rows.reshape(rows.shape[0], shares, columns // shares).transpose(1, 0, 2)

    fine = table(np.arange(n_fine), 1)
    coarse = table(n_fine * np.arange(n_coarse) - lags // 2, -1)
    return np.ascontiguousarray(fine), np.ascontiguousarray(coarse)


def adjoint_pass(scalars, mine, other, seen, env, hilbert, turned_a, turned_b, fine, coarse):
    shares, _, days_cols = turned_a.shape
    cols = fine.shape[2]
    n_fine = fine.shape[1] // 2
    n_coarse = coarse.shape[1] // 2
    b = turned_a.shape[1] // n_fine
    days = days_cols // cols
    scale = 1.0 / math.sqrt(shares * cols // 2)
    vmem = pl.BlockSpec(memory_space=pltpu.VMEM)
    hbm = pl.BlockSpec(memory_space=pltpu.HBM)
    turned_a = pltpu.with_memory_space_constraint(turned_a, pltpu.HBM)
    turned_b = pltpu.with_memory_space_constraint(turned_b, pltpu.HBM)
    return pl.pallas_call(
        functools.partial(adjoint_kernel, (b, scale)),
        out_shape=jax.ShapeDtypeStruct((shares, days, 2 * b, cols), BF16),
        in_specs=[pl.BlockSpec(memory_space=pltpu.SMEM)] + [vmem] * 5 + [hbm] * 2 + [vmem] * 2,
        out_specs=vmem,
        scratch_shapes=[
            pltpu.VMEM((n_coarse // 2, n_fine * b, 2 * b), F32),
            pltpu.VMEM((8 * n_fine, n_coarse * b), F32),
            pltpu.VMEM((n_fine * b, n_coarse * b), BF16),
            pltpu.VMEM((n_coarse * b, n_fine * b), BF16),
            pltpu.VMEM((n_fine * b, days_cols), F32),
            pltpu.VMEM((n_coarse * b, days_cols), F32),
            pltpu.VMEM(turned_a.shape, BF16),
            pltpu.VMEM(turned_b.shape, BF16),
            pltpu.SemaphoreType.DMA((shares,)),
            pltpu.SemaphoreType.DMA((shares,)),
        ],
        compiler_params=pltpu.CompilerParams(vmem_limit_bytes=36 << 20),
        name="adjoint",
    )(scalars, mine, other, seen, env, hilbert, turned_a, turned_b, fine, coarse)


def body(spectra, observed, pair_blocks, members, day_mask):
    shares = lax.axis_size("pairs")
    slots, b, _, lags = observed.shape
    _, stations, cols = spectra.shape
    fine, coarse = turn_tables(shares * cols, lags, shares)
    hilbert = hilbert_parts(lags)
    slot = lax.axis_index("slot")
    members = members.reshape(1, stations)
    first_day = lax.axis_index("outer") * slots * CORES + lax.axis_index("core")
    mask = lax.dynamic_slice_in_dim(day_mask, slot, 1, 0)[0].astype(F32)
    mask_here = jnp.stack([lax.dynamic_index_in_dim(mask, first_day + k * CORES, 0, False) for k in range(slots)])
    count = jnp.sum(mask)
    scale = 1.0 / math.sqrt(shares * cols // 2)
    scalars = jnp.concatenate([mask_here / count, scale / count[None]])

    sent = pack(pair_blocks, members, spectra, b)
    got = lax.all_to_all(sent, ("pairs", "slot"), 0, 0, tiled=True)
    got = got.reshape(shares, slots, 2 * b, cols)
    hilbert = pltpu.with_memory_space_constraint(jnp.asarray(hilbert), pltpu.VMEM)
    seen, env = prepare(slot[None], observed.reshape(slots, b * b, lags), hilbert)
    got, seen, env = lax.optimization_barrier((got, seen, env))
    mine, turned_a, turned_b = forward_pass(mask_here, got, fine, coarse)
    for axis in ("outer", "core"):
        n = lax.axis_size(axis)
        others = [lax.ppermute(mine, axis, [(i, (i + k) % n) for i in range(n)]) for k in range(1, n)]
        if axis == "outer":
            for other in others:
                mine = mine + other
    contrib = adjoint_pass(scalars, mine, others[0], seen, env, hilbert, turned_a, turned_b, fine, coarse)
    returned = lax.all_to_all(
        contrib.reshape(shares * slots, 2 * b, cols), ("pairs", "slot"), 0, 0, tiled=True
    )
    return unpack(pair_blocks, members, returned, stations)


def solution(mesh):
    shares, days = mesh.devices.shape
    names = ("pairs", "outer", "slot", "core")

    def run(spectra, observed, pair_blocks, members, day_mask):
        slots = observed.shape[0] // shares
        split = (shares, days // CORES // slots, slots, CORES)
        finer = Mesh(mesh.devices.reshape(split), names)
        day_axes = names[1:]
        return jax.shard_map(
            body,
            mesh=finer,
            in_specs=(
                P(day_axes, None, "pairs"),
                P("pairs", None, None, None),
                P(),
                P(),
                P("pairs", None),
            ),
            out_specs=P(day_axes, None, "pairs"),
            check_vma=False,
        )(spectra, observed, pair_blocks, members, day_mask)

    return run
```

```python
import functools
import math

import jax
import jax.numpy as jnp
import ml_dtypes
import numpy as np
from jax import lax
from jax.experimental import pallas as pl
from jax.experimental.pallas import tpu as pltpu
from jax.sharding import Mesh, PartitionSpec as P

HALF = 64
TILE = 128
CORES = 2
F32 = jnp.float32
BF16 = jnp.bfloat16


def hilbert_parts(lags):
    offset = (np.arange(lags)[None, :] - np.arange(lags)[:, None]) % lags
    angles = np.float32(math.pi) * offset.astype(np.float32) / np.float32(lags)
    odd = offset % 2 == 1
    safe = np.where(odd, np.sin(angles), np.float32(1.0))
    table = np.where(odd, np.float32(2.0 / lags) * np.cos(angles) / safe, np.float32(0.0))
    table = table.astype(np.float32).T
    high = table.astype(ml_dtypes.bfloat16)
    low = (table - high.astype(np.float32)).astype(ml_dtypes.bfloat16)
    return np.concatenate([high, low, high], axis=1)


def left_lanes(shape):
    return lax.broadcasted_iota(jnp.int32, shape, len(shape) - 1) % TILE < HALF


def swap_halves(x):
    return pltpu.roll(x, HALF, 1)


def dot(a, b):
    return jnp.dot(a, b, preferred_element_type=F32)


def pack_kernel(blocks_ref, members_ref, spectra_ref, out_ref, ordered):
    stations = spectra_ref.shape[1]
    b = out_ref.shape[1] // 2
    station = lax.broadcasted_iota(jnp.int32, (stations, stations), 0)
    chosen = (station == members_ref[...]).astype(F32).astype(BF16)
    ordered[...] = lax.dot_general(
        chosen, spectra_ref[0], (((0,), (0,)), ((), ())), preferred_element_type=F32
    ).astype(BF16)
    for p in range(out_ref.shape[0]):
        for side in range(2):
            row = pl.multiple_of(blocks_ref[p, side] * b, b)
            out_ref[p, side * b:(side + 1) * b, :] = ordered[pl.ds(row, b), :]


def pack(pair_blocks, members, spectra, b):
    _, stations, cols = spectra.shape
    n_pairs = pair_blocks.shape[0]
    return pl.pallas_call(
        pack_kernel,
        out_shape=jax.ShapeDtypeStruct((n_pairs, 2 * b, cols), BF16),
        in_specs=[
            pl.BlockSpec(memory_space=pltpu.SMEM),
            pl.BlockSpec(memory_space=pltpu.VMEM),
            pl.BlockSpec(memory_space=pltpu.VMEM),
        ],
        out_specs=pl.BlockSpec(memory_space=pltpu.VMEM),
        scratch_shapes=[pltpu.VMEM((stations, cols), BF16)],
        compiler_params=pltpu.CompilerParams(vmem_limit_bytes=8 << 20),
        name="pack",
    )(pair_blocks, members, spectra)


def unpack_kernel(blocks_ref, members_ref, got_ref, out_ref, total):
    stations = out_ref.shape[1]
    b = got_ref.shape[1] // 2
    total[...] = jnp.zeros_like(total)
    for p in range(got_ref.shape[0]):
        for side in range(2):
            rows = pl.ds(pl.multiple_of(blocks_ref[p, side] * b, b), b)
            total[rows, :] += got_ref[p, side * b:(side + 1) * b, :].astype(F32)
    station = lax.broadcasted_iota(jnp.int32, (stations, stations), 0)
    chosen = (station == members_ref[...]).astype(F32).astype(BF16)
    whole = total[...]
    high = whole.astype(BF16)
    rest = whole - high.astype(F32)
    mid = rest.astype(BF16)
    low = (rest - mid.astype(F32)).astype(BF16)
    out_ref[0] = dot(chosen, high) + (dot(chosen, mid) + dot(chosen, low))


def unpack(pair_blocks, members, got, stations):
    cols = got.shape[2]
    return pl.pallas_call(
        unpack_kernel,
        out_shape=jax.ShapeDtypeStruct((1, stations, cols), F32),
        in_specs=[
            pl.BlockSpec(memory_space=pltpu.SMEM),
            pl.BlockSpec(memory_space=pltpu.VMEM),
            pl.BlockSpec(memory_space=pltpu.VMEM),
        ],
        out_specs=pl.BlockSpec(memory_space=pltpu.VMEM),
        scratch_shapes=[pltpu.VMEM((stations, cols), F32)],
        compiler_params=pltpu.CompilerParams(vmem_limit_bytes=8 << 20),
        name="unpack",
    )(pair_blocks, members, got)


def prepare_kernel(b, slot_ref, observed_ref, hilbert_ref, seen_ref, env_ref):
    lags = observed_ref.shape[1]
    two = 2 * b

    def some(step, carry):
        seen = observed_ref[pl.ds(pl.multiple_of(step * two, two), two), :].astype(F32).T
        seen_b = seen.astype(BF16)
        hil = dot(hilbert_ref[:, :2 * lags], jnp.concatenate([seen_b, seen_b], axis=0))
        seen_ref[step] = seen_b
        env_ref[step] = 1.0 + jnp.sqrt(seen * seen + hil * hil)
        return carry

    lax.fori_loop(0, seen_ref.shape[0], some, 0, unroll=4)


def prepare(slot, observed, hilbert, parts):
    _, rows, lags = observed.shape
    b = math.isqrt(rows)
    shape = (b // 2, lags, 2 * b)
    block = (b // 2 // parts, lags, 2 * b)
    spec = pltpu.PrefetchScalarGridSpec(
        num_scalar_prefetch=1,
        grid=(parts,),
        in_specs=[
            pl.BlockSpec((None, rows // parts, lags), lambda s, slot_ref: (slot_ref[0], s, 0)),
            pl.BlockSpec(hilbert.shape, lambda s, slot_ref: (0, 0)),
        ],
        out_specs=[pl.BlockSpec(block, lambda s, slot_ref: (s, 0, 0))] * 2,
    )
    return pl.pallas_call(
        functools.partial(prepare_kernel, b),
        out_shape=[pltpu.HBM(shape, BF16), pltpu.HBM(shape, F32)],
        grid_spec=spec,
        compiler_params=pltpu.CompilerParams(vmem_limit_bytes=8 << 20),
        cost_estimate=pl.CostEstimate(flops=2 * rows * lags * lags, bytes_accessed=8 * rows * lags, transcendentals=0),
        name="prepare",
    )(slot, observed, hilbert)


def tile_lanes(tiles, d, t):
    return slice((d * tiles + t) * TILE, (d * tiles + t + 1) * TILE)


def part(t):
    return slice(t * TILE, (t + 1) * TILE)


def turn_columns(got_ref, share, b, table_ref, into):
    _, days, _, cols = got_ref.shape
    tiles = cols // TILE
    n = table_ref.shape[1] // 2
    for d in range(days):
        for t in range(tiles):
            at = tile_lanes(tiles, d, t)
            u = got_ref[share, d, b:, part(t)].astype(F32)
            v = swap_halves(u)
            for k in range(n):
                cosine = table_ref[share, k:k + 1, part(t)]
                sine = table_ref[share, n + k:n + k + 1, part(t)]
                into[k * b:(k + 1) * b, at] = (u * cosine + v * sine).astype(BF16)


def turn_rows(got_ref, share, b, table_ref, into, rows_u, rows_v, mask_ref=None):
    _, days, _, cols = got_ref.shape
    tiles = cols // TILE
    n = table_ref.shape[1] // 2
    pieces = [(d, t) for d in range(days) for t in range(tiles)]
    for d, t in pieces:
        at = tile_lanes(tiles, d, t)
        u = got_ref[share, d, :b, part(t)].astype(F32)
        if mask_ref is not None:
            u = u * mask_ref[d]
        rows_u[:, at] = u
        rows_v[:, at] = swap_halves(u)
    for d, t in pieces:
        at = tile_lanes(tiles, d, t)
        cosine = table_ref[share, :n, part(t)]
        sine = table_ref[share, n:, part(t)]
        for k in range(b):
            value = rows_u[k:k + 1, at] * cosine + rows_v[k:k + 1, at] * sine
            into[k * n:(k + 1) * n, at] = value.astype(BF16)


def forward_kernel(
    b, mask_ref, got_ref, fine_ref, coarse_ref, out_ref, sent_ref, kept_ref, even_a, even_b, odd_a, odd_b, rows_u, rows_v,
    sem,
):
    shares = got_ref.shape[0]
    even = (even_a, even_b)
    odd = (odd_a, odd_b)
    keep = pltpu.make_async_copy(got_ref, kept_ref, sem)
    keep.start()

    def make(share, into):
        turn_columns(got_ref, share, b, coarse_ref, into[1])
        turn_rows(got_ref, share, b, fine_ref, into[0], rows_u, rows_v, mask_ref)

    def product(made):
        return lax.dot_general(made[0][...], made[1][...], (((1,), (1,)), ((), ())), preferred_element_type=F32)

    make(0, even)
    out_ref[...] = product(even)
    make(1, odd)

    def two_shares(step, carry):
        out_ref[...] += product(odd)
        make(2 * step + 2, even)
        out_ref[...] += product(even)
        make(2 * step + 3, odd)
        return carry

    lax.fori_loop(0, shares // 2 - 1, two_shares, 0)
    total = out_ref[...] + product(odd)
    out_ref[...] = total
    sent_ref[...] = total.astype(sent_ref.dtype)
    keep.wait()


def forward_pass(mask, got, fine, coarse):
    shares, days, rows, cols = got.shape
    assert shares % 2 == 0
    b = rows // 2
    n_fine = fine.shape[1] // 2
    n_coarse = coarse.shape[1] // 2
    vmem = pl.BlockSpec(memory_space=pltpu.VMEM)
    return pl.pallas_call(
        functools.partial(forward_kernel, b),
        out_shape=[
            pltpu.VMEM((n_fine * b, n_coarse * b), F32),
            jax.ShapeDtypeStruct((n_fine * b, n_coarse * b), BF16),
            pltpu.HBM(got.shape, BF16),
        ],
        in_specs=[pl.BlockSpec(memory_space=pltpu.SMEM), vmem, vmem, vmem],
        out_specs=[vmem, vmem, pl.BlockSpec(memory_space=pltpu.HBM)],
        scratch_shapes=[
            pltpu.VMEM((n_fine * b, days * cols), BF16),
            pltpu.VMEM((n_coarse * b, days * cols), BF16),
            pltpu.VMEM((n_fine * b, days * cols), BF16),
            pltpu.VMEM((n_coarse * b, days * cols), BF16),
            pltpu.VMEM((b, days * cols), F32),
            pltpu.VMEM((b, days * cols), F32),
            pltpu.SemaphoreType.DMA,
        ],
        compiler_params=pltpu.CompilerParams(vmem_limit_bytes=16 << 20),
        name="forward",
    )(mask, got, fine, coarse)


def adjoint_kernel(
    sizes, scalars_ref, mine_ref, other_hbm, seen_hbm, env_hbm, hilbert_hbm, kept_ref, fine_hbm, coarse_hbm, out_ref,
    other_ref, seen_ref, env_ref, hilbert_ref, got_ref, fine_ref, coarse_ref, lagged, back, res, res_t, sums_a, sums_b,
    turned_a, turned_b, rows_u, rows_v, sems_o, sems_s, sems_e, sems,
):
    b, scale, group = sizes
    shares, days, _, cols = out_ref.shape
    n_fine = fine_ref.shape[1] // 2
    n_coarse = coarse_ref.shape[1] // 2
    slabs = n_coarse // 2
    tiles = cols // TILE
    block = group * n_fine
    left = left_lanes((n_fine, 2 * b))

    def bring(step):
        at = pl.ds(pl.multiple_of(step * block, block), block)
        some = pl.ds(step * (group // 2), group // 2)
        return (
            pltpu.make_async_copy(other_hbm.at[at], other_ref.at[at], sems_o.at[step]),
            pltpu.make_async_copy(seen_hbm.at[some], seen_ref.at[some], sems_s.at[step]),
            pltpu.make_async_copy(env_hbm.at[some], env_ref.at[some], sems_e.at[step]),
        )

    first = pltpu.make_async_copy(hilbert_hbm, hilbert_ref, sems.at[0])
    later = (
        pltpu.make_async_copy(kept_ref, got_ref, sems.at[1]),
        pltpu.make_async_copy(fine_hbm, fine_ref, sems.at[2]),
        pltpu.make_async_copy(coarse_hbm, coarse_ref, sems.at[3]),
    )
    first.start()
    for step in range(b // group):
        for copy in bring(step):
            copy.start()
    for copy in later:
        copy.start()
    first.wait()

    def residual_rows(step, carry):
        for copy in bring(step):
            copy.wait()
        for two in range(0, group, 2):
            rows = []
            for slab in range(slabs):
                got = []
                for k in (two, two + 1):
                    at = pl.ds(pl.multiple_of(step * block + k * n_fine, n_fine), n_fine)
                    got.append((mine_ref[at, part(slab)] + other_ref[at, part(slab)].astype(F32)) * scalars_ref[days])
                rows.append(jnp.where(left, got[0], swap_halves(got[1])))
                rows.append(jnp.where(left, swap_halves(got[0]), got[1]))
            stacked = jnp.concatenate(rows, axis=0)
            high = stacked.astype(BF16)
            low = (stacked - high.astype(F32)).astype(BF16)
            hil = dot(hilbert_ref[...], jnp.concatenate([high, high, low], axis=0))
            env_s = 1.0 + jnp.sqrt(stacked * stacked + hil * hil)
            env_o = env_ref[step * (group // 2) + two // 2]
            value = (stacked - seen_ref[step * (group // 2) + two // 2].astype(F32)) * (env_s / (env_s + env_o - 1.0))
            for slab in range(slabs):
                even = value[2 * slab * n_fine:(2 * slab + 1) * n_fine, :]
                odd = value[(2 * slab + 1) * n_fine:(2 * slab + 2) * n_fine, :]
                first = jnp.where(left, even, swap_halves(odd))
                second = jnp.where(left, swap_halves(even), odd)
                for k, rows in ((two, first), (two + 1, second)):
                    lagged[slab, pl.ds(step * group + k, n_fine, stride=b), :] = rows
                    back[k * n_fine:(k + 1) * n_fine, part(slab)] = rows
        at = pl.ds(pl.multiple_of(step * block, block), block)
        for slab in range(slabs):
            res_t[part(slab), at] = back[:, part(slab)].T.astype(BF16)
        return carry

    lax.fori_loop(0, b // group, residual_rows, 0)

    def round_rows(step, carry):
        at = pl.ds(pl.multiple_of(step * b, b), b)
        for slab in range(slabs):
            res[at, part(slab)] = lagged[slab, at, :].astype(BF16)
        return carry

    lax.fori_loop(0, n_fine, round_rows, 0)

    def collect(share, side, table, n, sums):
        for d in range(days):
            for t in range(tiles):
                at = tile_lanes(tiles, d, t)
                p = jnp.zeros((b, TILE), F32)
                q = jnp.zeros((b, TILE), F32)
                for k in range(n):
                    h = sums[k * b:(k + 1) * b, at]
                    p = p + h * table[share, k:k + 1, part(t)]
                    q = q + h * table[share, n + k:n + k + 1, part(t)]
                value = (p + swap_halves(q)) * (scalars_ref[d] * scale)
                out_ref[share, d, side * b:(side + 1) * b, part(t)] = value.astype(BF16)

    for copy in later:
        copy.wait()
    sums_b[...] = jnp.zeros_like(sums_b)
    turn_columns(got_ref, 0, b, coarse_ref, turned_b)

    def one_share(share, carry):
        sums_a[...] = dot(res[...], turned_b[...])
        turn_rows(got_ref, share, b, fine_ref, turned_a, rows_u, rows_v)
        collect(jnp.maximum(share - 1, 0), 1, coarse_ref, n_coarse, sums_b)
        sums_b[...] = dot(res_t[...], turned_a[...])
        collect(share, 0, fine_ref, n_fine, sums_a)
        turn_columns(got_ref, jnp.minimum(share + 1, shares - 1), b, coarse_ref, turned_b)
        return carry

    lax.fori_loop(0, shares, one_share, 0)
    collect(shares - 1, 1, coarse_ref, n_coarse, sums_b)


def turn_tables(columns, lags, shares):
    freqs = columns // 2
    n_fine = 16
    n_coarse = lags // n_fine
    column = np.arange(columns)
    frequency = column // TILE * HALF + column % HALF
    is_real = column % TILE < HALF

    def table(steps, sign):
        phase = frequency[None, :] * steps[:, None] % (2 * freqs)
        angles = np.pi * phase / freqs
        sine = np.where(is_real[None, :], -sign, sign) * np.sin(angles)
        rows = np.concatenate([np.cos(angles), sine]).astype(np.float32)
        return rows.reshape(rows.shape[0], shares, columns // shares).transpose(1, 0, 2)

    fine = table(np.arange(n_fine), 1)
    coarse = table(n_fine * np.arange(n_coarse) - lags // 2, -1)
    return np.ascontiguousarray(fine), np.ascontiguousarray(coarse)


def adjoint_pass(scalars, mine, other, seen, env, hilbert, kept, fine, coarse, parts):
    shares, days, rows, cols = kept.shape
    b = rows // 2
    n_fine = fine.shape[1] // 2
    n_coarse = coarse.shape[1] // 2
    scale = 1.0 / math.sqrt(shares * cols // 2)
    group = b // parts
    lanes = days * cols
    vmem = pl.BlockSpec(memory_space=pltpu.VMEM)
    hbm = pl.BlockSpec(memory_space=pltpu.HBM)
    apart = [pltpu.with_memory_space_constraint(x, pltpu.HBM) for x in (other, seen, env, hilbert, kept, fine, coarse)]
    return pl.pallas_call(
        functools.partial(adjoint_kernel, (b, scale, group)),
        out_shape=jax.ShapeDtypeStruct(kept.shape, BF16),
        in_specs=[pl.BlockSpec(memory_space=pltpu.SMEM), vmem] + [hbm] * len(apart),
        out_specs=vmem,
        scratch_shapes=[pltpu.VMEM(x.shape, x.dtype) for x in apart]
        + [
            pltpu.VMEM((n_coarse // 2, n_fine * b, 2 * b), F32),
            pltpu.VMEM((group * n_fine, n_coarse * b), F32),
            pltpu.VMEM((n_fine * b, n_coarse * b), BF16),
            pltpu.VMEM((n_coarse * b, n_fine * b), BF16),
            pltpu.VMEM((n_fine * b, lanes), F32),
            pltpu.VMEM((n_coarse * b, lanes), F32),
            pltpu.VMEM((n_fine * b, lanes), BF16),
            pltpu.VMEM((n_coarse * b, lanes), BF16),
            pltpu.VMEM((b, lanes), F32),
            pltpu.VMEM((b, lanes), F32),
            pltpu.SemaphoreType.DMA((parts,)),
            pltpu.SemaphoreType.DMA((parts,)),
            pltpu.SemaphoreType.DMA((parts,)),
            pltpu.SemaphoreType.DMA((4,)),
        ],
        compiler_params=pltpu.CompilerParams(vmem_limit_bytes=24 << 20),
        name="adjoint",
    )(scalars, mine, *apart)


def body(spectra, observed, pair_blocks, members, day_mask):
    shares = lax.axis_size("pairs")
    slots, b, _, lags = observed.shape
    _, stations, cols = spectra.shape
    fine, coarse = turn_tables(shares * cols, lags, shares)
    hilbert = hilbert_parts(lags)
    slot = lax.axis_index("slot")
    members = members.reshape(1, stations)
    first_day = lax.axis_index("outer") * slots * CORES + lax.axis_index("core")
    mask = lax.dynamic_slice_in_dim(day_mask, slot, 1, 0)[0].astype(F32)
    mask_here = jnp.stack([lax.dynamic_index_in_dim(mask, first_day + k * CORES, 0, False) for k in range(slots)])
    count = jnp.sum(mask)
    scale = 1.0 / math.sqrt(shares * cols // 2)
    scalars = jnp.concatenate([mask_here / count, scale / count[None]])

    sent = pack(pair_blocks, members, spectra, b)
    got = lax.all_to_all(sent, ("pairs", "slot"), 0, 0, tiled=True)
    got = got.reshape(shares, slots, 2 * b, cols)
    parts = 4
    hilbert, fine, coarse = [jnp.asarray(x) for x in (hilbert, fine, coarse)]
    seen, env = prepare(slot[None], observed.reshape(slots, b * b, lags), hilbert, parts)
    got, seen, env = lax.optimization_barrier((got, seen, env))
    mine, sent, kept = forward_pass(mask_here, got, fine, coarse)
    for axis in ("outer", "core"):
        n = lax.axis_size(axis)
        others = [lax.ppermute(sent, axis, [(i, (i + k) % n) for i in range(n)]) for k in range(1, n)]
        if axis == "outer" and others:
            for other in others:
                mine = mine + other.astype(F32)
            sent = mine.astype(BF16)
    contrib = adjoint_pass(scalars, mine, others[0], seen, env, hilbert, kept, fine, coarse, parts)
    returned = lax.all_to_all(
        contrib.reshape(shares * slots, 2 * b, cols), ("pairs", "slot"), 0, 0, tiled=True
    )
    return unpack(pair_blocks, members, returned, stations)


def solution(mesh):
    shares, days = mesh.devices.shape
    names = ("pairs", "outer", "slot", "core")

    def run(spectra, observed, pair_blocks, members, day_mask):
        slots = observed.shape[0] // shares
        split = (shares, days // CORES // slots, slots, CORES)
        finer = Mesh(mesh.devices.reshape(split), names)
        day_axes = names[1:]
        return jax.shard_map(
            body,
            mesh=finer,
            in_specs=(
                P(day_axes, None, "pairs"),
                P("pairs", None, None, None),
                P(),
                P(),
                P("pairs", None),
            ),
            out_specs=P(day_axes, None, "pairs"),
            check_vma=False,
        )(spectra, observed, pair_blocks, members, day_mask)

    return run
```

```python
import functools
import math

import jax
import jax.numpy as jnp
import ml_dtypes
import numpy as np
from jax import lax
from jax.experimental import pallas as pl
from jax.experimental.pallas import tpu as pltpu
from jax.sharding import Mesh, PartitionSpec as P

HALF = 64
TILE = 128
CORES = 2
F32 = jnp.float32
BF16 = jnp.bfloat16


def hilbert_parts(lags):
    offset = (np.arange(lags)[None, :] - np.arange(lags)[:, None]) % lags
    angles = np.float32(math.pi) * offset.astype(np.float32) / np.float32(lags)
    odd = offset % 2 == 1
    safe = np.where(odd, np.sin(angles), np.float32(1.0))
    table = np.where(odd, np.float32(2.0 / lags) * np.cos(angles) / safe, np.float32(0.0))
    table = table.astype(np.float32).T
    high = table.astype(ml_dtypes.bfloat16)
    low = (table - high.astype(np.float32)).astype(ml_dtypes.bfloat16)
    return np.concatenate([high, low, high], axis=1)


def left_lanes(shape):
    return lax.broadcasted_iota(jnp.int32, shape, len(shape) - 1) % TILE < HALF


def swap_halves(x):
    return pltpu.roll(x, HALF, 1)


def dot(a, b):
    return jnp.dot(a, b, preferred_element_type=F32)


def pack_kernel(blocks_hbm, members_hbm, spectra_hbm, out_ref, blocks_ref, members_ref, spectra_ref, ordered, sems):
    stations = spectra_ref.shape[1]
    b = out_ref.shape[1] // 2
    copies = (
        pltpu.make_async_copy(spectra_hbm, spectra_ref, sems.at[0]),
        pltpu.make_async_copy(members_hbm, members_ref, sems.at[1]),
        pltpu.make_async_copy(blocks_hbm, blocks_ref, sems.at[2]),
    )
    for copy in copies:
        copy.start()
    station = lax.broadcasted_iota(jnp.int32, (stations, stations), 0)
    copies[1].wait()
    chosen = (station == members_ref[...]).astype(F32).astype(BF16)
    copies[0].wait()
    ordered[...] = lax.dot_general(
        chosen, spectra_ref[0], (((0,), (0,)), ((), ())), preferred_element_type=F32
    ).astype(BF16)
    copies[2].wait()
    for p in range(out_ref.shape[0]):
        for side in range(2):
            row = pl.multiple_of(blocks_ref[side, p] * b, b)
            out_ref[p, side * b:(side + 1) * b, :] = ordered[pl.ds(row, b), :]


def pack(pair_blocks, members, spectra, b):
    _, stations, cols = spectra.shape
    n_pairs = pair_blocks.shape[1]
    arrays = [pltpu.with_memory_space_constraint(x, pltpu.HBM) for x in (pair_blocks, members, spectra)]
    return pl.pallas_call(
        pack_kernel,
        out_shape=jax.ShapeDtypeStruct((n_pairs, 2 * b, cols), BF16),
        in_specs=[pl.BlockSpec(memory_space=pltpu.HBM)] * 3,
        out_specs=pl.BlockSpec(memory_space=pltpu.VMEM),
        scratch_shapes=[
            pltpu.SMEM(pair_blocks.shape, pair_blocks.dtype),
            pltpu.VMEM(members.shape, members.dtype),
            pltpu.VMEM(spectra.shape, BF16),
            pltpu.VMEM((stations, cols), BF16),
            pltpu.SemaphoreType.DMA((3,)),
        ],
        compiler_params=pltpu.CompilerParams(vmem_limit_bytes=8 << 20),
        name="pack",
    )(*arrays)


def unpack_kernel(blocks_ref, members_ref, got_ref, out_ref, total):
    stations = out_ref.shape[1]
    b = got_ref.shape[1] // 2
    total[...] = jnp.zeros_like(total)
    for p in range(got_ref.shape[0]):
        for side in range(2):
            rows = pl.ds(pl.multiple_of(blocks_ref[side, p] * b, b), b)
            total[rows, :] += got_ref[p, side * b:(side + 1) * b, :].astype(F32)
    station = lax.broadcasted_iota(jnp.int32, (stations, stations), 0)
    chosen = (station == members_ref[...]).astype(F32).astype(BF16)
    whole = total[...]
    high = whole.astype(BF16)
    rest = whole - high.astype(F32)
    mid = rest.astype(BF16)
    low = (rest - mid.astype(F32)).astype(BF16)
    out_ref[0] = dot(chosen, high) + (dot(chosen, mid) + dot(chosen, low))


def unpack(pair_blocks, members, got, stations):
    cols = got.shape[2]
    return pl.pallas_call(
        unpack_kernel,
        out_shape=jax.ShapeDtypeStruct((1, stations, cols), F32),
        in_specs=[
            pl.BlockSpec(memory_space=pltpu.SMEM),
            pl.BlockSpec(memory_space=pltpu.VMEM),
            pl.BlockSpec(memory_space=pltpu.VMEM),
        ],
        out_specs=pl.BlockSpec(memory_space=pltpu.VMEM),
        scratch_shapes=[pltpu.VMEM((stations, cols), F32)],
        compiler_params=pltpu.CompilerParams(vmem_limit_bytes=8 << 20),
        name="unpack",
    )(pair_blocks, members, got)


def prepare_kernel(b, slot_ref, observed_ref, hilbert_ref, seen_ref, env_ref):
    lags = observed_ref.shape[1]
    two = 2 * b

    def some(step, carry):
        seen = observed_ref[pl.ds(pl.multiple_of(step * two, two), two), :].astype(F32).T
        seen_b = seen.astype(BF16)
        hil = dot(hilbert_ref[:, :2 * lags], jnp.concatenate([seen_b, seen_b], axis=0))
        seen_ref[step] = seen_b
        env_ref[step] = 1.0 + jnp.sqrt(seen * seen + hil * hil)
        return carry

    lax.fori_loop(0, seen_ref.shape[0], some, 0, unroll=4)


def prepare(slot, observed, hilbert, parts):
    _, rows, lags = observed.shape
    b = math.isqrt(rows)
    shape = (b // 2, lags, 2 * b)
    block = (b // 2 // parts, lags, 2 * b)
    spec = pltpu.PrefetchScalarGridSpec(
        num_scalar_prefetch=1,
        grid=(parts,),
        in_specs=[
            pl.BlockSpec((None, rows // parts, lags), lambda s, slot_ref: (slot_ref[0], s, 0)),
            pl.BlockSpec(hilbert.shape, lambda s, slot_ref: (0, 0)),
        ],
        out_specs=[pl.BlockSpec(block, lambda s, slot_ref: (s, 0, 0))] * 2,
    )
    return pl.pallas_call(
        functools.partial(prepare_kernel, b),
        out_shape=[pltpu.HBM(shape, BF16), pltpu.HBM(shape, F32)],
        grid_spec=spec,
        compiler_params=pltpu.CompilerParams(vmem_limit_bytes=8 << 20),
        cost_estimate=pl.CostEstimate(flops=2 * rows * lags * lags, bytes_accessed=8 * rows * lags, transcendentals=0),
        name="prepare",
    )(slot, observed, hilbert)


def tile_lanes(tiles, d, t):
    return slice((d * tiles + t) * TILE, (d * tiles + t + 1) * TILE)


def part(t):
    return slice(t * TILE, (t + 1) * TILE)


def turn_columns(got_ref, share, b, table_ref, into):
    _, days, _, cols = got_ref.shape
    tiles = cols // TILE
    n = table_ref.shape[1] // 2
    for d in range(days):
        for t in range(tiles):
            at = tile_lanes(tiles, d, t)
            u = got_ref[share, d, b:, part(t)].astype(F32)
            v = swap_halves(u)
            for k in range(n):
                cosine = table_ref[share, k:k + 1, part(t)]
                sine = table_ref[share, n + k:n + k + 1, part(t)]
                into[k * b:(k + 1) * b, at] = (u * cosine + v * sine).astype(BF16)


def turn_rows(got_ref, share, b, table_ref, into, rows_u, rows_v, mask_ref=None):
    _, days, _, cols = got_ref.shape
    tiles = cols // TILE
    n = table_ref.shape[1] // 2
    pieces = [(d, t) for d in range(days) for t in range(tiles)]
    for d, t in pieces:
        at = tile_lanes(tiles, d, t)
        u = got_ref[share, d, :b, part(t)].astype(F32)
        if mask_ref is not None:
            u = u * mask_ref[d]
        rows_u[:, at] = u
        rows_v[:, at] = swap_halves(u)
    for d, t in pieces:
        at = tile_lanes(tiles, d, t)
        cosine = table_ref[share, :n, part(t)]
        sine = table_ref[share, n:, part(t)]
        for k in range(b):
            value = rows_u[k:k + 1, at] * cosine + rows_v[k:k + 1, at] * sine
            into[k * n:(k + 1) * n, at] = value.astype(BF16)


def forward_kernel(
    b, mask_ref, got_ref, fine_ref, coarse_ref, out_ref, sent_ref, kept_ref, even_a, even_b, odd_a, odd_b, rows_u, rows_v,
    sem,
):
    shares = got_ref.shape[0]
    even = (even_a, even_b)
    odd = (odd_a, odd_b)
    keep = pltpu.make_async_copy(got_ref, kept_ref, sem)
    keep.start()

    def make(share, into):
        turn_columns(got_ref, share, b, coarse_ref, into[1])
        turn_rows(got_ref, share, b, fine_ref, into[0], rows_u, rows_v, mask_ref)

    def product(made):
        return lax.dot_general(made[0][...], made[1][...], (((1,), (1,)), ((), ())), preferred_element_type=F32)

    make(0, even)
    out_ref[...] = product(even)
    make(1, odd)

    def two_shares(step, carry):
        out_ref[...] += product(odd)
        make(2 * step + 2, even)
        out_ref[...] += product(even)
        make(2 * step + 3, odd)
        return carry

    lax.fori_loop(0, shares // 2 - 1, two_shares, 0)
    total = out_ref[...] + product(odd)
    out_ref[...] = total
    sent_ref[...] = total.astype(sent_ref.dtype)
    keep.wait()


def forward_pass(mask, got, fine, coarse):
    shares, days, rows, cols = got.shape
    assert shares % 2 == 0
    b = rows // 2
    n_fine = fine.shape[1] // 2
    n_coarse = coarse.shape[1] // 2
    vmem = pl.BlockSpec(memory_space=pltpu.VMEM)
    return pl.pallas_call(
        functools.partial(forward_kernel, b),
        out_shape=[
            pltpu.VMEM((n_fine * b, n_coarse * b), F32),
            jax.ShapeDtypeStruct((n_fine * b, n_coarse * b), BF16),
            pltpu.HBM(got.shape, BF16),
        ],
        in_specs=[pl.BlockSpec(memory_space=pltpu.SMEM), vmem, vmem, vmem],
        out_specs=[vmem, vmem, pl.BlockSpec(memory_space=pltpu.HBM)],
        scratch_shapes=[
            pltpu.VMEM((n_fine * b, days * cols), BF16),
            pltpu.VMEM((n_coarse * b, days * cols), BF16),
            pltpu.VMEM((n_fine * b, days * cols), BF16),
            pltpu.VMEM((n_coarse * b, days * cols), BF16),
            pltpu.VMEM((b, days * cols), F32),
            pltpu.VMEM((b, days * cols), F32),
            pltpu.SemaphoreType.DMA,
        ],
        compiler_params=pltpu.CompilerParams(vmem_limit_bytes=16 << 20),
        name="forward",
    )(mask, got, fine, coarse)


def adjoint_kernel(
    sizes, scalars_ref, mine_ref, other_ref, seen_hbm, env_hbm, hilbert_hbm, kept_ref, fine_hbm, coarse_hbm, out_ref,
    seen_ref, env_ref, hilbert_ref, got_ref, fine_ref, coarse_ref, lagged, back, res, res_t, sums_a, sums_b,
    turned_a, turned_b, rows_u, rows_v, sems_s, sems_e, sems,
):
    b, scale, group = sizes
    shares, days, _, cols = out_ref.shape
    n_fine = fine_ref.shape[1] // 2
    n_coarse = coarse_ref.shape[1] // 2
    slabs = n_coarse // 2
    tiles = cols // TILE
    block = group * n_fine
    left = left_lanes((n_fine, 2 * b))

    def bring(step):
        some = pl.ds(step * (group // 2), group // 2)
        return (
            pltpu.make_async_copy(seen_hbm.at[some], seen_ref.at[some], sems_s.at[step]),
            pltpu.make_async_copy(env_hbm.at[some], env_ref.at[some], sems_e.at[step]),
        )

    first = pltpu.make_async_copy(hilbert_hbm, hilbert_ref, sems.at[0])
    later = (
        pltpu.make_async_copy(kept_ref, got_ref, sems.at[1]),
        pltpu.make_async_copy(fine_hbm, fine_ref, sems.at[2]),
        pltpu.make_async_copy(coarse_hbm, coarse_ref, sems.at[3]),
    )
    first.start()
    for step in range(b // group):
        for copy in bring(step):
            copy.start()
    for copy in later:
        copy.start()
    first.wait()

    def residual_rows(step, carry):
        for copy in bring(step):
            copy.wait()
        for two in range(0, group, 2):
            rows = []
            for slab in range(slabs):
                got = []
                for k in (two, two + 1):
                    at = pl.ds(pl.multiple_of(step * block + k * n_fine, n_fine), n_fine)
                    got.append((mine_ref[at, part(slab)] + other_ref[at, part(slab)].astype(F32)) * scalars_ref[days])
                rows.append(jnp.where(left, got[0], swap_halves(got[1])))
                rows.append(jnp.where(left, swap_halves(got[0]), got[1]))
            stacked = jnp.concatenate(rows, axis=0)
            high = stacked.astype(BF16)
            low = (stacked - high.astype(F32)).astype(BF16)
            hil = dot(hilbert_ref[...], jnp.concatenate([high, high, low], axis=0))
            env_s = 1.0 + jnp.sqrt(stacked * stacked + hil * hil)
            env_o = env_ref[step * (group // 2) + two // 2]
            value = (stacked - seen_ref[step * (group // 2) + two // 2].astype(F32)) * (env_s / (env_s + env_o - 1.0))
            for slab in range(slabs):
                even = value[2 * slab * n_fine:(2 * slab + 1) * n_fine, :]
                odd = value[(2 * slab + 1) * n_fine:(2 * slab + 2) * n_fine, :]
                first = jnp.where(left, even, swap_halves(odd))
                second = jnp.where(left, swap_halves(even), odd)
                for k, rows in ((two, first), (two + 1, second)):
                    lagged[slab, pl.ds(step * group + k, n_fine, stride=b), :] = rows
                    back[k * n_fine:(k + 1) * n_fine, part(slab)] = rows
        at = pl.ds(pl.multiple_of(step * block, block), block)
        for slab in range(slabs):
            res_t[part(slab), at] = back[:, part(slab)].T.astype(BF16)
        return carry

    lax.fori_loop(0, b // group, residual_rows, 0)

    def round_rows(step, carry):
        at = pl.ds(pl.multiple_of(step * b, b), b)
        for slab in range(slabs):
            res[at, part(slab)] = lagged[slab, at, :].astype(BF16)
        return carry

    lax.fori_loop(0, n_fine, round_rows, 0)

    def collect(share, side, table, n, sums):
        for d in range(days):
            for t in range(tiles):
                at = tile_lanes(tiles, d, t)
                p = jnp.zeros((b, TILE), F32)
                q = jnp.zeros((b, TILE), F32)
                for k in range(n):
                    h = sums[k * b:(k + 1) * b, at]
                    p = p + h * table[share, k:k + 1, part(t)]
                    q = q + h * table[share, n + k:n + k + 1, part(t)]
                value = (p + swap_halves(q)) * (scalars_ref[d] * scale)
                out_ref[share, d, side * b:(side + 1) * b, part(t)] = value.astype(BF16)

    for copy in later:
        copy.wait()
    sums_b[...] = jnp.zeros_like(sums_b)
    turn_columns(got_ref, 0, b, coarse_ref, turned_b)

    def one_share(share, carry):
        sums_a[...] = dot(res[...], turned_b[...])
        turn_rows(got_ref, share, b, fine_ref, turned_a, rows_u, rows_v)
        collect(jnp.maximum(share - 1, 0), 1, coarse_ref, n_coarse, sums_b)
        sums_b[...] = dot(res_t[...], turned_a[...])
        collect(share, 0, fine_ref, n_fine, sums_a)
        turn_columns(got_ref, jnp.minimum(share + 1, shares - 1), b, coarse_ref, turned_b)
        return carry

    lax.fori_loop(0, shares, one_share, 0)
    collect(shares - 1, 1, coarse_ref, n_coarse, sums_b)


def turn_tables(columns, lags, shares):
    freqs = columns // 2
    n_fine = 16
    n_coarse = lags // n_fine
    column = np.arange(columns)
    frequency = column // TILE * HALF + column % HALF
    is_real = column % TILE < HALF

    def table(steps, sign):
        phase = frequency[None, :] * steps[:, None] % (2 * freqs)
        angles = np.pi * phase / freqs
        sine = np.where(is_real[None, :], -sign, sign) * np.sin(angles)
        rows = np.concatenate([np.cos(angles), sine]).astype(np.float32)
        return rows.reshape(rows.shape[0], shares, columns // shares).transpose(1, 0, 2)

    fine = table(np.arange(n_fine), 1)
    coarse = table(n_fine * np.arange(n_coarse) - lags // 2, -1)
    return np.ascontiguousarray(fine), np.ascontiguousarray(coarse)


def adjoint_pass(scalars, mine, other, seen, env, hilbert, kept, fine, coarse, parts):
    shares, days, rows, cols = kept.shape
    b = rows // 2
    n_fine = fine.shape[1] // 2
    n_coarse = coarse.shape[1] // 2
    scale = 1.0 / math.sqrt(shares * cols // 2)
    group = b // parts
    lanes = days * cols
    vmem = pl.BlockSpec(memory_space=pltpu.VMEM)
    hbm = pl.BlockSpec(memory_space=pltpu.HBM)
    apart = [pltpu.with_memory_space_constraint(x, pltpu.HBM) for x in (seen, env, hilbert, kept, fine, coarse)]
    return pl.pallas_call(
        functools.partial(adjoint_kernel, (b, scale, group)),
        out_shape=jax.ShapeDtypeStruct(kept.shape, BF16),
        in_specs=[pl.BlockSpec(memory_space=pltpu.SMEM), vmem, vmem] + [hbm] * len(apart),
        out_specs=vmem,
        scratch_shapes=[pltpu.VMEM(x.shape, x.dtype) for x in apart]
        + [
            pltpu.VMEM((n_coarse // 2, n_fine * b, 2 * b), F32),
            pltpu.VMEM((group * n_fine, n_coarse * b), F32),
            pltpu.VMEM((n_fine * b, n_coarse * b), BF16),
            pltpu.VMEM((n_coarse * b, n_fine * b), BF16),
            pltpu.VMEM((n_fine * b, lanes), F32),
            pltpu.VMEM((n_coarse * b, lanes), F32),
            pltpu.VMEM((n_fine * b, lanes), BF16),
            pltpu.VMEM((n_coarse * b, lanes), BF16),
            pltpu.VMEM((b, lanes), F32),
            pltpu.VMEM((b, lanes), F32),
            pltpu.SemaphoreType.DMA((parts,)),
            pltpu.SemaphoreType.DMA((parts,)),
            pltpu.SemaphoreType.DMA((4,)),
        ],
        compiler_params=pltpu.CompilerParams(vmem_limit_bytes=24 << 20),
        name="adjoint",
    )(scalars, mine, other, *apart)


def body(spectra, observed, pair_blocks, members, day_mask):
    shares = lax.axis_size("pairs")
    slots, b, _, lags = observed.shape
    _, stations, cols = spectra.shape
    fine, coarse = turn_tables(shares * cols, lags, shares)
    hilbert = hilbert_parts(lags)
    slot = lax.axis_index("slot")
    members = members.reshape(1, stations)
    pair_blocks = pair_blocks.T
    first_day = lax.axis_index("outer") * slots * CORES + lax.axis_index("core")
    mask = lax.dynamic_slice_in_dim(day_mask, slot, 1, 0)[0].astype(F32)
    mask_here = jnp.stack([lax.dynamic_index_in_dim(mask, first_day + k * CORES, 0, False) for k in range(slots)])
    count = jnp.sum(mask)
    scale = 1.0 / math.sqrt(shares * cols // 2)
    scalars = jnp.concatenate([mask_here / count, scale / count[None]])

    sent = pack(pair_blocks, members, spectra, b)
    got = lax.all_to_all(sent, ("pairs", "slot"), 0, 0, tiled=True)
    got = got.reshape(shares, slots, 2 * b, cols)
    parts = 4
    hilbert, fine, coarse = [jnp.asarray(x) for x in (hilbert, fine, coarse)]
    seen, env = prepare(slot[None], observed.reshape(slots, b * b, lags), hilbert, parts)
    got, seen, env = lax.optimization_barrier((got, seen, env))
    mine, sent, kept = forward_pass(mask_here, got, fine, coarse)
    for axis in ("outer", "core"):
        n = lax.axis_size(axis)
        others = [lax.ppermute(sent, axis, [(i, (i + k) % n) for i in range(n)]) for k in range(1, n)]
        if axis == "outer" and others:
            for other in others:
                mine = mine + other.astype(F32)
            sent = mine.astype(BF16)
    contrib = adjoint_pass(scalars, mine, others[0], seen, env, hilbert, kept, fine, coarse, parts)
    returned = lax.all_to_all(
        contrib.reshape(shares * slots, 2 * b, cols), ("pairs", "slot"), 0, 0, tiled=True
    )
    return unpack(pair_blocks, members, returned, stations)


def solution(mesh):
    shares, days = mesh.devices.shape
    names = ("pairs", "outer", "slot", "core")

    def run(spectra, observed, pair_blocks, members, day_mask):
        slots = observed.shape[0] // shares
        split = (shares, days // CORES // slots, slots, CORES)
        finer = Mesh(mesh.devices.reshape(split), names)
        day_axes = names[1:]
        return jax.shard_map(
            body,
            mesh=finer,
            in_specs=(
                P(day_axes, None, "pairs"),
                P("pairs", None, None, None),
                P(),
                P(),
                P("pairs", None),
            ),
            out_specs=P(day_axes, None, "pairs"),
            check_vma=False,
        )(spectra, observed, pair_blocks, members, day_mask)

    return run
```

```python
import functools
import math

import jax
import jax.numpy as jnp
import ml_dtypes
import numpy as np
from jax import lax
from jax.experimental import pallas as pl
from jax.experimental.pallas import tpu as pltpu
from jax.sharding import Mesh, PartitionSpec as P

HALF = 64
TILE = 128
CORES = 2
F32 = jnp.float32
BF16 = jnp.bfloat16


def lag_order(lags, n_fine):
    n_coarse = lags // n_fine
    half_f, half_c = n_fine // 2, n_coarse // 2
    fine = np.concatenate([half_f + np.arange(half_f), half_f - 1 - np.arange(half_f)])
    coarse = np.concatenate([half_c + np.arange(half_c), half_c - 1 - np.arange(half_c)])
    return (n_fine * coarse[:, None] + fine[None, :]).reshape(-1)


def split_bf16(table):
    high = table.astype(ml_dtypes.bfloat16)
    return high, (table - high.astype(np.float32)).astype(ml_dtypes.bfloat16)


def hilbert_parts(lags, n_fine):
    offset = (np.arange(lags)[None, :] - np.arange(lags)[:, None]) % lags
    angles = np.float32(math.pi) * offset.astype(np.float32) / np.float32(lags)
    odd = offset % 2 == 1
    safe = np.where(odd, np.sin(angles), np.float32(1.0))
    table = np.where(odd, np.float32(2.0 / lags) * np.cos(angles) / safe, np.float32(0.0))
    table = table.astype(np.float32).T
    order = lag_order(lags, n_fine)
    high, low = split_bf16(table[order])
    chosen = np.eye(lags, dtype=np.float32)[order].astype(ml_dtypes.bfloat16)
    high_both, low_both = split_bf16(table[order][:, order])
    return (
        np.concatenate([chosen, high, low], axis=0),
        np.concatenate([high_both, low_both, high_both], axis=1),
    )


def left_lanes(shape):
    return lax.broadcasted_iota(jnp.int32, shape, len(shape) - 1) % TILE < HALF


def swap_halves(x):
    return pltpu.roll(x, HALF, 1)


def dot(a, b):
    return jnp.dot(a, b, preferred_element_type=F32)


def pack_kernel(blocks_hbm, members_hbm, spectra_hbm, out_ref, blocks_ref, members_ref, spectra_ref, ordered, sems):
    stations = spectra_ref.shape[1]
    b = out_ref.shape[1] // 2
    copies = (
        pltpu.make_async_copy(spectra_hbm, spectra_ref, sems.at[0]),
        pltpu.make_async_copy(members_hbm, members_ref, sems.at[1]),
        pltpu.make_async_copy(blocks_hbm, blocks_ref, sems.at[2]),
    )
    for copy in copies:
        copy.start()
    station = lax.broadcasted_iota(jnp.int32, (stations, stations), 0)
    copies[1].wait()
    chosen = (station == members_ref[...]).astype(F32).astype(BF16)
    copies[0].wait()
    ordered[...] = lax.dot_general(
        chosen, spectra_ref[0], (((0,), (0,)), ((), ())), preferred_element_type=F32
    ).astype(BF16)
    copies[2].wait()
    for p in range(out_ref.shape[0]):
        for side in range(2):
            row = pl.multiple_of(blocks_ref[side, p] * b, b)
            out_ref[p, side * b:(side + 1) * b, :] = ordered[pl.ds(row, b), :]


def pack(pair_blocks, members, spectra, b):
    _, stations, cols = spectra.shape
    n_pairs = pair_blocks.shape[1]
    arrays = [pltpu.with_memory_space_constraint(x, pltpu.HBM) for x in (pair_blocks, members, spectra)]
    return pl.pallas_call(
        pack_kernel,
        out_shape=jax.ShapeDtypeStruct((n_pairs, 2 * b, cols), BF16),
        in_specs=[pl.BlockSpec(memory_space=pltpu.HBM)] * 3,
        out_specs=pl.BlockSpec(memory_space=pltpu.VMEM),
        scratch_shapes=[
            pltpu.SMEM(pair_blocks.shape, pair_blocks.dtype),
            pltpu.VMEM(members.shape, members.dtype),
            pltpu.VMEM(spectra.shape, BF16),
            pltpu.VMEM((stations, cols), BF16),
            pltpu.SemaphoreType.DMA((3,)),
        ],
        compiler_params=pltpu.CompilerParams(vmem_limit_bytes=8 << 20),
        name="pack",
    )(*arrays)


def unpack_kernel(blocks_ref, members_ref, got_ref, out_ref, total):
    stations = out_ref.shape[1]
    b = got_ref.shape[1] // 2
    total[...] = jnp.zeros_like(total)
    for p in range(got_ref.shape[0]):
        for side in range(2):
            rows = pl.ds(pl.multiple_of(blocks_ref[side, p] * b, b), b)
            total[rows, :] += got_ref[p, side * b:(side + 1) * b, :].astype(F32)
    station = lax.broadcasted_iota(jnp.int32, (stations, stations), 0)
    chosen = (station == members_ref[...]).astype(F32).astype(BF16)
    whole = total[...]
    high = whole.astype(BF16)
    rest = whole - high.astype(F32)
    mid = rest.astype(BF16)
    low = (rest - mid.astype(F32)).astype(BF16)
    out_ref[0] = dot(chosen, high) + (dot(chosen, mid) + dot(chosen, low))


def unpack(pair_blocks, members, got, stations):
    cols = got.shape[2]
    return pl.pallas_call(
        unpack_kernel,
        out_shape=jax.ShapeDtypeStruct((1, stations, cols), F32),
        in_specs=[
            pl.BlockSpec(memory_space=pltpu.SMEM),
            pl.BlockSpec(memory_space=pltpu.VMEM),
            pl.BlockSpec(memory_space=pltpu.VMEM),
        ],
        out_specs=pl.BlockSpec(memory_space=pltpu.VMEM),
        scratch_shapes=[pltpu.VMEM((stations, cols), F32)],
        compiler_params=pltpu.CompilerParams(vmem_limit_bytes=8 << 20),
        name="unpack",
    )(pair_blocks, members, got)


def prepare_kernel(b, slot_ref, observed_ref, orders_ref, seen_ref, env_ref):
    lags = observed_ref.shape[1]
    two = 2 * b

    def some(step, carry):
        rows = observed_ref[pl.ds(pl.multiple_of(step * two, two), two), :]
        turned = lax.dot_general(orders_ref[...], rows, (((1,), (1,)), ((), ())), preferred_element_type=F32)
        seen = turned[:lags]
        hil = turned[lags:2 * lags] + turned[2 * lags:]
        seen_ref[step] = seen.astype(BF16)
        env_ref[step] = 1.0 + jnp.sqrt(seen * seen + hil * hil)
        return carry

    lax.fori_loop(0, seen_ref.shape[0], some, 0, unroll=4)


def prepare(slot, observed, orders, parts):
    _, rows, lags = observed.shape
    b = math.isqrt(rows)
    shape = (b // 2, lags, 2 * b)
    block = (b // 2 // parts, lags, 2 * b)
    spec = pltpu.PrefetchScalarGridSpec(
        num_scalar_prefetch=1,
        grid=(parts,),
        in_specs=[
            pl.BlockSpec((None, rows // parts, lags), lambda s, slot_ref: (slot_ref[0], s, 0)),
            pl.BlockSpec(orders.shape, lambda s, slot_ref: (0, 0)),
        ],
        out_specs=[pl.BlockSpec(block, lambda s, slot_ref: (s, 0, 0))] * 2,
    )
    return pl.pallas_call(
        functools.partial(prepare_kernel, b),
        out_shape=[pltpu.HBM(shape, BF16), pltpu.HBM(shape, F32)],
        grid_spec=spec,
        compiler_params=pltpu.CompilerParams(vmem_limit_bytes=8 << 20),
        cost_estimate=pl.CostEstimate(flops=2 * rows * lags * lags, bytes_accessed=8 * rows * lags, transcendentals=0),
        name="prepare",
    )(slot, observed, orders)


def tile_lanes(tiles, d, t):
    return slice((d * tiles + t) * TILE, (d * tiles + t + 1) * TILE)


def part(t):
    return slice(t * TILE, (t + 1) * TILE)


def turn_columns(got_ref, share, b, table_ref, into):
    _, days, _, cols = got_ref.shape
    tiles = cols // TILE
    half = table_ref.shape[1] // 2
    for d in range(days):
        for t in range(tiles):
            at = tile_lanes(tiles, d, t)
            u = got_ref[share, d, b:, part(t)].astype(F32)
            v = swap_halves(u)
            for k in range(half):
                one = u * table_ref[share, k:k + 1, part(t)]
                two = v * table_ref[share, half + k:half + k + 1, part(t)]
                into[k * b:(k + 1) * b, at] = (one + two).astype(BF16)
                into[(half + k) * b:(half + k + 1) * b, at] = (one - two).astype(BF16)


def turn_rows(got_ref, share, b, table_ref, into, rows_u, rows_v, mask_ref=None):
    _, days, _, cols = got_ref.shape
    tiles = cols // TILE
    half = table_ref.shape[1] // 2 - 1
    pieces = [(d, t) for d in range(days) for t in range(tiles)]
    for d, t in pieces:
        at = tile_lanes(tiles, d, t)
        u = got_ref[share, d, :b, part(t)].astype(F32)
        if mask_ref is not None:
            u = u * mask_ref[d]
        u = turn_half(u, table_ref, share, t, 1)
        rows_u[:, at] = u
        rows_v[:, at] = swap_halves(u)
    for d, t in pieces:
        at = tile_lanes(tiles, d, t)
        cosine = table_ref[share, :half, part(t)]
        sine = table_ref[share, half:2 * half, part(t)]
        for k in range(b):
            one = rows_u[k:k + 1, at] * cosine
            two = rows_v[k:k + 1, at] * sine
            into[2 * k * half:2 * (k + 1) * half, at] = jnp.concatenate([one + two, one - two], axis=0).astype(BF16)


def turn_half(u, table_ref, share, t, sign):
    at = table_ref.shape[1] - 2
    one = u * table_ref[share, at:at + 1, part(t)]
    two = swap_halves(u) * table_ref[share, at + 1:at + 2, part(t)]
    return one + two if sign > 0 else one - two


def forward_kernel(
    b, mask_ref, got_ref, fine_ref, coarse_ref, out_ref, sent_ref, kept_ref, even_a, even_b, odd_a, odd_b, rows_u, rows_v,
    sem,
):
    shares = got_ref.shape[0]
    even = (even_a, even_b)
    odd = (odd_a, odd_b)
    keep = pltpu.make_async_copy(got_ref, kept_ref, sem)
    keep.start()

    def make(share, into):
        turn_columns(got_ref, share, b, coarse_ref, into[1])
        turn_rows(got_ref, share, b, fine_ref, into[0], rows_u, rows_v, mask_ref)

    def product(made):
        return lax.dot_general(made[0][...], made[1][...], (((1,), (1,)), ((), ())), preferred_element_type=F32)

    make(0, even)
    out_ref[...] = product(even)
    make(1, odd)

    def two_shares(step, carry):
        out_ref[...] += product(odd)
        make(2 * step + 2, even)
        out_ref[...] += product(even)
        make(2 * step + 3, odd)
        return carry

    lax.fori_loop(0, shares // 2 - 1, two_shares, 0)
    total = out_ref[...] + product(odd)
    out_ref[...] = total
    sent_ref[...] = total.astype(sent_ref.dtype)
    keep.wait()


def forward_pass(mask, got, fine, coarse):
    shares, days, rows, cols = got.shape
    assert shares % 2 == 0
    b = rows // 2
    n_fine = fine.shape[1] - 2
    n_coarse = coarse.shape[1]
    vmem = pl.BlockSpec(memory_space=pltpu.VMEM)
    return pl.pallas_call(
        functools.partial(forward_kernel, b),
        out_shape=[
            pltpu.VMEM((n_fine * b, n_coarse * b), F32),
            jax.ShapeDtypeStruct((n_fine * b, n_coarse * b), BF16),
            pltpu.HBM(got.shape, BF16),
        ],
        in_specs=[pl.BlockSpec(memory_space=pltpu.SMEM), vmem, vmem, vmem],
        out_specs=[vmem, vmem, pl.BlockSpec(memory_space=pltpu.HBM)],
        scratch_shapes=[
            pltpu.VMEM((n_fine * b, days * cols), BF16),
            pltpu.VMEM((n_coarse * b, days * cols), BF16),
            pltpu.VMEM((n_fine * b, days * cols), BF16),
            pltpu.VMEM((n_coarse * b, days * cols), BF16),
            pltpu.VMEM((b, days * cols), F32),
            pltpu.VMEM((b, days * cols), F32),
            pltpu.SemaphoreType.DMA,
        ],
        compiler_params=pltpu.CompilerParams(vmem_limit_bytes=16 << 20),
        name="forward",
    )(mask, got, fine, coarse)


def adjoint_kernel(
    sizes, scalars_ref, mine_ref, other_ref, seen_hbm, env_hbm, hilbert_hbm, kept_ref, fine_hbm, coarse_hbm, out_ref,
    seen_ref, env_ref, hilbert_ref, got_ref, fine_ref, coarse_ref, lagged, back, res, res_t, sums_a, sums_b,
    turned_a, turned_b, rows_u, rows_v, sems_s, sems_e, sems,
):
    b, scale, group = sizes
    shares, days, _, cols = out_ref.shape
    n_fine = fine_ref.shape[1] - 2
    n_coarse = coarse_ref.shape[1]
    slabs = n_coarse // 2
    tiles = cols // TILE
    block = group * n_fine
    left = left_lanes((n_fine, 2 * b))

    def bring(step):
        some = pl.ds(step * (group // 2), group // 2)
        return (
            pltpu.make_async_copy(seen_hbm.at[some], seen_ref.at[some], sems_s.at[step]),
            pltpu.make_async_copy(env_hbm.at[some], env_ref.at[some], sems_e.at[step]),
        )

    first = pltpu.make_async_copy(hilbert_hbm, hilbert_ref, sems.at[0])
    later = (
        pltpu.make_async_copy(kept_ref, got_ref, sems.at[1]),
        pltpu.make_async_copy(fine_hbm, fine_ref, sems.at[2]),
        pltpu.make_async_copy(coarse_hbm, coarse_ref, sems.at[3]),
    )
    first.start()
    for step in range(b // group):
        for copy in bring(step):
            copy.start()
    for copy in later:
        copy.start()
    first.wait()

    def residual_rows(step, carry):
        for copy in bring(step):
            copy.wait()
        for two in range(0, group, 2):
            rows = []
            for slab in range(slabs):
                got = []
                for k in (two, two + 1):
                    at = pl.ds(pl.multiple_of(step * block + k * n_fine, n_fine), n_fine)
                    got.append((mine_ref[at, part(slab)] + other_ref[at, part(slab)].astype(F32)) * scalars_ref[days])
                rows.append(jnp.where(left, got[0], swap_halves(got[1])))
                rows.append(jnp.where(left, swap_halves(got[0]), got[1]))
            stacked = jnp.concatenate(rows, axis=0)
            high = stacked.astype(BF16)
            low = (stacked - high.astype(F32)).astype(BF16)
            hil = dot(hilbert_ref[...], jnp.concatenate([high, high, low], axis=0))
            env_s = 1.0 + jnp.sqrt(stacked * stacked + hil * hil)
            env_o = env_ref[step * (group // 2) + two // 2]
            value = (stacked - seen_ref[step * (group // 2) + two // 2].astype(F32)) * (env_s / (env_s + env_o - 1.0))
            for slab in range(slabs):
                even = value[2 * slab * n_fine:(2 * slab + 1) * n_fine, :]
                odd = value[(2 * slab + 1) * n_fine:(2 * slab + 2) * n_fine, :]
                first = jnp.where(left, even, swap_halves(odd))
                second = jnp.where(left, swap_halves(even), odd)
                for k, rows in ((two, first), (two + 1, second)):
                    lagged[slab, pl.ds(step * group + k, n_fine, stride=b), :] = rows
                    back[k * n_fine:(k + 1) * n_fine, part(slab)] = rows
        at = pl.ds(pl.multiple_of(step * block, block), block)
        for slab in range(slabs):
            res_t[part(slab), at] = back[:, part(slab)].T.astype(BF16)
        return carry

    lax.fori_loop(0, b // group, residual_rows, 0)

    def round_rows(step, carry):
        at = pl.ds(pl.multiple_of(step * b, b), b)
        for slab in range(slabs):
            res[at, part(slab)] = lagged[slab, at, :].astype(BF16)
        return carry

    lax.fori_loop(0, n_fine, round_rows, 0)

    def collect(share, side, table, n, sums):
        half = n // 2
        for d in range(days):
            for t in range(tiles):
                at = tile_lanes(tiles, d, t)
                p = jnp.zeros((b, TILE), F32)
                q = jnp.zeros((b, TILE), F32)
                for k in range(half):
                    one = sums[k * b:(k + 1) * b, at]
                    two = sums[(half + k) * b:(half + k + 1) * b, at]
                    p = p + (one + two) * table[share, k:k + 1, part(t)]
                    q = q + (one - two) * table[share, half + k:half + k + 1, part(t)]
                value = p + swap_halves(q)
                if side == 0:
                    value = turn_half(value, table, share, t, -1)
                out_ref[share, d, side * b:(side + 1) * b, part(t)] = (value * (scalars_ref[d] * scale)).astype(BF16)

    for copy in later:
        copy.wait()
    sums_b[...] = jnp.zeros_like(sums_b)
    turn_columns(got_ref, 0, b, coarse_ref, turned_b)

    def one_share(share, carry):
        sums_a[...] = dot(res[...], turned_b[...])
        turn_rows(got_ref, share, b, fine_ref, turned_a, rows_u, rows_v)
        collect(jnp.maximum(share - 1, 0), 1, coarse_ref, n_coarse, sums_b)
        sums_b[...] = dot(res_t[...], turned_a[...])
        collect(share, 0, fine_ref, n_fine, sums_a)
        turn_columns(got_ref, jnp.minimum(share + 1, shares - 1), b, coarse_ref, turned_b)
        return carry

    lax.fori_loop(0, shares, one_share, 0)
    collect(shares - 1, 1, coarse_ref, n_coarse, sums_b)


def turn_tables(columns, lags, shares, n_fine):
    freqs = columns // 2
    n_coarse = lags // n_fine
    column = np.arange(columns)
    frequency = column // TILE * HALF + column % HALF
    is_real = column % TILE < HALF

    def table(halves, sign):
        phase = frequency[None, :] * halves[:, None] % (4 * freqs)
        angles = np.pi * phase / (2 * freqs)
        sine = np.where(is_real[None, :], -sign, sign) * np.sin(angles)
        return np.concatenate([np.cos(angles), sine])

    def place(rows):
        rows = rows.astype(np.float32).reshape(rows.shape[0], shares, columns // shares)
        return np.ascontiguousarray(rows.transpose(1, 0, 2))

    fine = table(2 * np.arange(n_fine // 2) + 1, 1)
    coarse = table(n_fine * (2 * np.arange(n_coarse // 2) + 1), -1)
    return place(np.concatenate([fine, table(np.array([1]), -1)])), place(coarse)


def adjoint_pass(scalars, mine, other, seen, env, hilbert, kept, fine, coarse, parts):
    shares, days, rows, cols = kept.shape
    b = rows // 2
    n_fine = fine.shape[1] - 2
    n_coarse = coarse.shape[1]
    scale = 1.0 / math.sqrt(shares * cols // 2)
    group = b // parts
    lanes = days * cols
    vmem = pl.BlockSpec(memory_space=pltpu.VMEM)
    hbm = pl.BlockSpec(memory_space=pltpu.HBM)
    apart = [pltpu.with_memory_space_constraint(x, pltpu.HBM) for x in (seen, env, hilbert, kept, fine, coarse)]
    return pl.pallas_call(
        functools.partial(adjoint_kernel, (b, scale, group)),
        out_shape=jax.ShapeDtypeStruct(kept.shape, BF16),
        in_specs=[pl.BlockSpec(memory_space=pltpu.SMEM), vmem, vmem] + [hbm] * len(apart),
        out_specs=vmem,
        scratch_shapes=[pltpu.VMEM(x.shape, x.dtype) for x in apart]
        + [
            pltpu.VMEM((n_coarse // 2, n_fine * b, 2 * b), F32),
            pltpu.VMEM((group * n_fine, n_coarse * b), F32),
            pltpu.VMEM((n_fine * b, n_coarse * b), BF16),
            pltpu.VMEM((n_coarse * b, n_fine * b), BF16),
            pltpu.VMEM((n_fine * b, lanes), F32),
            pltpu.VMEM((n_coarse * b, lanes), F32),
            pltpu.VMEM((n_fine * b, lanes), BF16),
            pltpu.VMEM((n_coarse * b, lanes), BF16),
            pltpu.VMEM((b, lanes), F32),
            pltpu.VMEM((b, lanes), F32),
            pltpu.SemaphoreType.DMA((parts,)),
            pltpu.SemaphoreType.DMA((parts,)),
            pltpu.SemaphoreType.DMA((4,)),
        ],
        compiler_params=pltpu.CompilerParams(vmem_limit_bytes=24 << 20),
        name="adjoint",
    )(scalars, mine, other, *apart)


def body(spectra, observed, pair_blocks, members, day_mask):
    shares = lax.axis_size("pairs")
    slots, b, _, lags = observed.shape
    _, stations, cols = spectra.shape
    n_fine = 16
    fine, coarse = turn_tables(shares * cols, lags, shares, n_fine)
    orders, hilbert = hilbert_parts(lags, n_fine)
    slot = lax.axis_index("slot")
    members = members.reshape(1, stations)
    pair_blocks = pair_blocks.T
    first_day = lax.axis_index("outer") * slots * CORES + lax.axis_index("core")
    mask = lax.dynamic_slice_in_dim(day_mask, slot, 1, 0)[0].astype(F32)
    mask_here = jnp.stack([lax.dynamic_index_in_dim(mask, first_day + k * CORES, 0, False) for k in range(slots)])
    count = jnp.sum(mask)
    scale = 1.0 / math.sqrt(shares * cols // 2)
    scalars = jnp.concatenate([mask_here / count, scale / count[None]])

    sent = pack(pair_blocks, members, spectra, b)
    got = lax.all_to_all(sent, ("pairs", "slot"), 0, 0, tiled=True)
    got = got.reshape(shares, slots, 2 * b, cols)
    parts = 4
    orders, hilbert, fine, coarse = [jnp.asarray(x) for x in (orders, hilbert, fine, coarse)]
    seen, env = prepare(slot[None], observed.reshape(slots, b * b, lags), orders, parts)
    got, seen, env = lax.optimization_barrier((got, seen, env))
    mine, sent, kept = forward_pass(mask_here, got, fine, coarse)
    for axis in ("outer", "core"):
        n = lax.axis_size(axis)
        others = [lax.ppermute(sent, axis, [(i, (i + k) % n) for i in range(n)]) for k in range(1, n)]
        if axis == "outer" and others:
            for other in others:
                mine = mine + other.astype(F32)
            sent = mine.astype(BF16)
    contrib = adjoint_pass(scalars, mine, others[0], seen, env, hilbert, kept, fine, coarse, parts)
    returned = lax.all_to_all(
        contrib.reshape(shares * slots, 2 * b, cols), ("pairs", "slot"), 0, 0, tiled=True
    )
    return unpack(pair_blocks, members, returned, stations)


def solution(mesh):
    shares, days = mesh.devices.shape
    names = ("pairs", "outer", "slot", "core")

    def run(spectra, observed, pair_blocks, members, day_mask):
        slots = observed.shape[0] // shares
        split = (shares, days // CORES // slots, slots, CORES)
        finer = Mesh(mesh.devices.reshape(split), names)
        day_axes = names[1:]
        return jax.shard_map(
            body,
            mesh=finer,
            in_specs=(
                P(day_axes, None, "pairs"),
                P("pairs", None, None, None),
                P(),
                P(),
                P("pairs", None),
            ),
            out_specs=P(day_axes, None, "pairs"),
            check_vma=False,
        )(spectra, observed, pair_blocks, members, day_mask)

    return run
```

```python
import functools
import math

import jax
import jax.numpy as jnp
import ml_dtypes
import numpy as np
from jax import lax
from jax.experimental import pallas as pl
from jax.experimental.pallas import tpu as pltpu
from jax.sharding import Mesh, PartitionSpec as P

HALF = 64
TILE = 128
CORES = 2
F32 = jnp.float32
BF16 = jnp.bfloat16


def lag_order(lags, n_fine):
    n_coarse = lags // n_fine
    half_f, half_c = n_fine // 2, n_coarse // 2
    fine = np.concatenate([half_f + np.arange(half_f), half_f - 1 - np.arange(half_f)])
    coarse = np.concatenate([half_c + np.arange(half_c), half_c - 1 - np.arange(half_c)])
    return (n_fine * coarse[:, None] + fine[None, :]).reshape(-1)


def split_bf16(table):
    high = table.astype(ml_dtypes.bfloat16)
    return high, (table - high.astype(np.float32)).astype(ml_dtypes.bfloat16)


def hilbert_parts(lags, n_fine):
    offset = (np.arange(lags)[None, :] - np.arange(lags)[:, None]) % lags
    angles = np.float32(math.pi) * offset.astype(np.float32) / np.float32(lags)
    odd = offset % 2 == 1
    safe = np.where(odd, np.sin(angles), np.float32(1.0))
    table = np.where(odd, np.float32(2.0 / lags) * np.cos(angles) / safe, np.float32(0.0))
    table = table.astype(np.float32).T
    order = lag_order(lags, n_fine)
    high, low = split_bf16(table[order])
    chosen = np.eye(lags, dtype=np.float32)[order].astype(ml_dtypes.bfloat16)
    high_both, low_both = split_bf16(table[order][:, order])
    return (
        np.concatenate([chosen, high, low], axis=0),
        np.concatenate([high_both, low_both, high_both], axis=1),
    )


def left_lanes(shape):
    return lax.broadcasted_iota(jnp.int32, shape, len(shape) - 1) % TILE < HALF


def swap_halves(x):
    return pltpu.roll(x, HALF, 1)


def dot(a, b):
    return jnp.dot(a, b, preferred_element_type=F32)


def pack_kernel(blocks_hbm, members_hbm, spectra_hbm, out_ref, blocks_ref, members_ref, spectra_ref, ordered, sems):
    stations = spectra_ref.shape[1]
    b = out_ref.shape[1] // 2
    copies = (
        pltpu.make_async_copy(spectra_hbm, spectra_ref, sems.at[0]),
        pltpu.make_async_copy(members_hbm, members_ref, sems.at[1]),
        pltpu.make_async_copy(blocks_hbm, blocks_ref, sems.at[2]),
    )
    for copy in copies:
        copy.start()
    station = lax.broadcasted_iota(jnp.int32, (stations, stations), 0)
    copies[1].wait()
    chosen = (station == members_ref[...]).astype(F32).astype(BF16)
    copies[0].wait()
    ordered[...] = lax.dot_general(
        chosen, spectra_ref[0], (((0,), (0,)), ((), ())), preferred_element_type=F32
    ).astype(BF16)
    copies[2].wait()
    for p in range(out_ref.shape[0]):
        for side in range(2):
            row = pl.multiple_of(blocks_ref[side, p] * b, b)
            out_ref[p, side * b:(side + 1) * b, :] = ordered[pl.ds(row, b), :]


def pack(pair_blocks, members, spectra, b):
    _, stations, cols = spectra.shape
    n_pairs = pair_blocks.shape[1]
    arrays = [pltpu.with_memory_space_constraint(x, pltpu.HBM) for x in (pair_blocks, members, spectra)]
    return pl.pallas_call(
        pack_kernel,
        out_shape=pltpu.VMEM((n_pairs, 2 * b, cols), BF16),
        in_specs=[pl.BlockSpec(memory_space=pltpu.HBM)] * 3,
        out_specs=pl.BlockSpec(memory_space=pltpu.VMEM),
        scratch_shapes=[
            pltpu.SMEM(pair_blocks.shape, pair_blocks.dtype),
            pltpu.VMEM(members.shape, members.dtype),
            pltpu.VMEM(spectra.shape, BF16),
            pltpu.VMEM((stations, cols), BF16),
            pltpu.SemaphoreType.DMA((3,)),
        ],
        compiler_params=pltpu.CompilerParams(vmem_limit_bytes=8 << 20),
        name="pack",
    )(*arrays)


def add_blocks(blocks_ref, got_ref, total):
    b = got_ref.shape[1] // 2
    for p in range(got_ref.shape[0]):
        for side in range(2):
            rows = pl.ds(pl.multiple_of(blocks_ref[side, p] * b, b), b)
            total[rows, :] += got_ref[p, side * b:(side + 1) * b, :].astype(F32)


def gather_kernel(blocks_ref, got_ref, out_ref, total):
    total[...] = jnp.zeros_like(total)
    add_blocks(blocks_ref, got_ref, total)
    out_ref[...] = total[...].astype(out_ref.dtype)


def gather(pair_blocks, got, stations):
    cols = got.shape[2]
    vmem = pl.BlockSpec(memory_space=pltpu.VMEM)
    return pl.pallas_call(
        gather_kernel,
        out_shape=jax.ShapeDtypeStruct((stations, cols), BF16),
        in_specs=[pl.BlockSpec(memory_space=pltpu.SMEM), vmem],
        out_specs=vmem,
        scratch_shapes=[pltpu.VMEM((stations, cols), F32)],
        compiler_params=pltpu.CompilerParams(vmem_limit_bytes=8 << 20),
        name="gather",
    )(pair_blocks, got)


def unpack_kernel(blocks_ref, members_ref, got_ref, far_ref, out_ref, total):
    stations = out_ref.shape[1]
    total[...] = far_ref[...].astype(F32)
    add_blocks(blocks_ref, got_ref, total)
    station = lax.broadcasted_iota(jnp.int32, (stations, stations), 0)
    chosen = (station == members_ref[...]).astype(F32).astype(BF16)
    whole = total[...]
    high = whole.astype(BF16)
    low = (whole - high.astype(F32)).astype(BF16)
    out_ref[0] = dot(chosen, high) + dot(chosen, low)


def unpack(pair_blocks, members, got, far):
    stations, cols = far.shape
    vmem = pl.BlockSpec(memory_space=pltpu.VMEM)
    return pl.pallas_call(
        unpack_kernel,
        out_shape=jax.ShapeDtypeStruct((1, stations, cols), F32),
        in_specs=[pl.BlockSpec(memory_space=pltpu.SMEM)] + [vmem] * 3,
        out_specs=vmem,
        scratch_shapes=[pltpu.VMEM((stations, cols), F32)],
        compiler_params=pltpu.CompilerParams(vmem_limit_bytes=8 << 20),
        name="unpack",
    )(pair_blocks, members, got, far)


def prepare_kernel(b, slot_ref, observed_ref, orders_ref, seen_ref, env_ref):
    lags = observed_ref.shape[1]
    two = 2 * b

    def some(step, carry):
        rows = observed_ref[pl.ds(pl.multiple_of(step * two, two), two), :]
        turned = lax.dot_general(orders_ref[...], rows, (((1,), (1,)), ((), ())), preferred_element_type=F32)
        seen = turned[:lags]
        hil = turned[lags:2 * lags] + turned[2 * lags:]
        seen_ref[step] = seen.astype(BF16)
        env_ref[step] = 1.0 + jnp.sqrt(seen * seen + hil * hil)
        return carry

    lax.fori_loop(0, seen_ref.shape[0], some, 0, unroll=4)


def prepare(slot, observed, orders, parts):
    _, rows, lags = observed.shape
    b = math.isqrt(rows)
    shape = (b // 2, lags, 2 * b)
    block = (b // 2 // parts, lags, 2 * b)
    spec = pltpu.PrefetchScalarGridSpec(
        num_scalar_prefetch=1,
        grid=(parts,),
        in_specs=[
            pl.BlockSpec((None, rows // parts, lags), lambda s, slot_ref: (slot_ref[0], s, 0)),
            pl.BlockSpec(orders.shape, lambda s, slot_ref: (0, 0)),
        ],
        out_specs=[pl.BlockSpec(block, lambda s, slot_ref: (s, 0, 0))] * 2,
    )
    return pl.pallas_call(
        functools.partial(prepare_kernel, b),
        out_shape=[pltpu.HBM(shape, BF16), pltpu.HBM(shape, F32)],
        grid_spec=spec,
        compiler_params=pltpu.CompilerParams(vmem_limit_bytes=8 << 20),
        cost_estimate=pl.CostEstimate(flops=2 * rows * lags * lags, bytes_accessed=8 * rows * lags, transcendentals=0),
        name="prepare",
    )(slot, observed, orders)


def tile_lanes(tiles, d, t):
    return slice((d * tiles + t) * TILE, (d * tiles + t + 1) * TILE)


def part(t):
    return slice(t * TILE, (t + 1) * TILE)


def turn_columns(got_ref, share, b, table_ref, into):
    _, days, _, cols = got_ref.shape
    tiles = cols // TILE
    half = table_ref.shape[1] // 2
    for d in range(days):
        for t in range(tiles):
            at = tile_lanes(tiles, d, t)
            u = got_ref[share, d, b:, part(t)].astype(F32)
            v = swap_halves(u)
            for k in range(half):
                one = u * table_ref[share, k:k + 1, part(t)]
                two = v * table_ref[share, half + k:half + k + 1, part(t)]
                into[k * b:(k + 1) * b, at] = (one + two).astype(BF16)
                into[(half + k) * b:(half + k + 1) * b, at] = (one - two).astype(BF16)


def turn_rows(got_ref, share, b, table_ref, into, rows_u, rows_v, mask_ref=None):
    _, days, _, cols = got_ref.shape
    tiles = cols // TILE
    half = table_ref.shape[1] // 2 - 1
    pieces = [(d, t) for d in range(days) for t in range(tiles)]
    for d, t in pieces:
        at = tile_lanes(tiles, d, t)
        u = got_ref[share, d, :b, part(t)].astype(F32)
        if mask_ref is not None:
            u = u * mask_ref[d]
        u = turn_half(u, table_ref, share, t, 1)
        rows_u[:, at] = u
        rows_v[:, at] = swap_halves(u)
    for d, t in pieces:
        at = tile_lanes(tiles, d, t)
        cosine = table_ref[share, :half, part(t)]
        sine = table_ref[share, half:2 * half, part(t)]
        for k in range(b):
            one = rows_u[k:k + 1, at] * cosine
            two = rows_v[k:k + 1, at] * sine
            into[2 * k * half:2 * (k + 1) * half, at] = jnp.concatenate([one + two, one - two], axis=0).astype(BF16)


def turn_half(u, table_ref, share, t, sign):
    at = table_ref.shape[1] - 2
    one = u * table_ref[share, at:at + 1, part(t)]
    two = swap_halves(u) * table_ref[share, at + 1:at + 2, part(t)]
    return one + two if sign > 0 else one - two


def forward_kernel(
    b, mask_ref, got_ref, fine_ref, coarse_ref, out_ref, sent_ref, kept_ref, even_a, even_b, odd_a, odd_b, rows_u, rows_v,
    sem,
):
    shares = got_ref.shape[0]
    even = (even_a, even_b)
    odd = (odd_a, odd_b)
    keep = pltpu.make_async_copy(got_ref, kept_ref, sem)
    keep.start()

    def make(share, into):
        turn_columns(got_ref, share, b, coarse_ref, into[1])
        turn_rows(got_ref, share, b, fine_ref, into[0], rows_u, rows_v, mask_ref)

    def product(made):
        return lax.dot_general(made[0][...], made[1][...], (((1,), (1,)), ((), ())), preferred_element_type=F32)

    make(0, even)
    out_ref[...] = product(even)
    make(1, odd)

    def two_shares(step, carry):
        out_ref[...] += product(odd)
        make(2 * step + 2, even)
        out_ref[...] += product(even)
        make(2 * step + 3, odd)
        return carry

    lax.fori_loop(0, shares // 2 - 1, two_shares, 0)
    total = out_ref[...] + product(odd)
    out_ref[...] = total
    sent_ref[...] = total.astype(sent_ref.dtype)
    keep.wait()


def forward_pass(mask, got, fine, coarse):
    shares, days, rows, cols = got.shape
    assert shares % 2 == 0
    b = rows // 2
    n_fine = fine.shape[1] - 2
    n_coarse = coarse.shape[1]
    vmem = pl.BlockSpec(memory_space=pltpu.VMEM)
    return pl.pallas_call(
        functools.partial(forward_kernel, b),
        out_shape=[
            pltpu.VMEM((n_fine * b, n_coarse * b), F32),
            jax.ShapeDtypeStruct((n_fine * b, n_coarse * b), BF16),
            pltpu.HBM(got.shape, BF16),
        ],
        in_specs=[pl.BlockSpec(memory_space=pltpu.SMEM), vmem, vmem, vmem],
        out_specs=[vmem, vmem, pl.BlockSpec(memory_space=pltpu.HBM)],
        scratch_shapes=[
            pltpu.VMEM((n_fine * b, days * cols), BF16),
            pltpu.VMEM((n_coarse * b, days * cols), BF16),
            pltpu.VMEM((n_fine * b, days * cols), BF16),
            pltpu.VMEM((n_coarse * b, days * cols), BF16),
            pltpu.VMEM((b, days * cols), F32),
            pltpu.VMEM((b, days * cols), F32),
            pltpu.SemaphoreType.DMA,
        ],
        compiler_params=pltpu.CompilerParams(vmem_limit_bytes=16 << 20),
        name="forward",
    )(mask, got, fine, coarse)


def residual_stage(
    b, group, scalars_ref, mine_ref, other_ref, seen_hbm, env_hbm, hilbert_hbm, seen_ref, env_ref, hilbert_ref, lagged,
    back, res, res_t, sems_s, sems_e, sem, begin,
):
    n_fine = mine_ref.shape[0] // b
    slabs = mine_ref.shape[1] // TILE
    days = scalars_ref.shape[0] - 1
    block = group * n_fine
    left = left_lanes((n_fine, 2 * b))

    def bring(step):
        some = pl.ds(step * (group // 2), group // 2)
        return (
            pltpu.make_async_copy(seen_hbm.at[some], seen_ref.at[some], sems_s.at[step]),
            pltpu.make_async_copy(env_hbm.at[some], env_ref.at[some], sems_e.at[step]),
        )

    first = pltpu.make_async_copy(hilbert_hbm, hilbert_ref, sem)
    first.start()
    for step in range(b // group):
        for copy in bring(step):
            copy.start()
    begin()
    first.wait()

    def residual_rows(step, carry):
        for copy in bring(step):
            copy.wait()
        for two in range(0, group, 2):
            rows = []
            for slab in range(slabs):
                got = []
                for k in (two, two + 1):
                    at = pl.ds(pl.multiple_of(step * block + k * n_fine, n_fine), n_fine)
                    got.append((mine_ref[at, part(slab)] + other_ref[at, part(slab)].astype(F32)) * scalars_ref[days])
                rows.append(jnp.where(left, got[0], swap_halves(got[1])))
                rows.append(jnp.where(left, swap_halves(got[0]), got[1]))
            stacked = jnp.concatenate(rows, axis=0)
            high = stacked.astype(BF16)
            low = (stacked - high.astype(F32)).astype(BF16)
            hil = dot(hilbert_ref[...], jnp.concatenate([high, high, low], axis=0))
            env_s = 1.0 + jnp.sqrt(stacked * stacked + hil * hil)
            env_o = env_ref[step * (group // 2) + two // 2]
            value = (stacked - seen_ref[step * (group // 2) + two // 2].astype(F32)) * (env_s / (env_s + env_o - 1.0))
            for slab in range(slabs):
                even = value[2 * slab * n_fine:(2 * slab + 1) * n_fine, :]
                odd = value[(2 * slab + 1) * n_fine:(2 * slab + 2) * n_fine, :]
                first = jnp.where(left, even, swap_halves(odd))
                second = jnp.where(left, swap_halves(even), odd)
                for k, rows in ((two, first), (two + 1, second)):
                    lagged[slab, pl.ds(step * group + k, n_fine, stride=b), :] = rows
                    back[k * n_fine:(k + 1) * n_fine, part(slab)] = rows
        at = pl.ds(pl.multiple_of(step * block, block), block)
        for slab in range(slabs):
            res_t[part(slab), at] = back[:, part(slab)].T.astype(BF16)
        return carry

    lax.fori_loop(0, b // group, residual_rows, 0)

    def round_rows(step, carry):
        at = pl.ds(pl.multiple_of(step * b, b), b)
        for slab in range(slabs):
            res[at, part(slab)] = lagged[slab, at, :].astype(BF16)
        return carry

    lax.fori_loop(0, n_fine, round_rows, 0)


def adjoint_stage(
    sizes, offset, scalars_ref, kept_ref, fine_hbm, coarse_hbm, out_ref, got_ref, fine_ref, coarse_ref, res, res_t,
    sums_a, sums_b, turned_a, turned_b, rows_u, rows_v, sems, before,
):
    b, scale = sizes
    shares, days, _, cols = out_ref.shape
    n_fine = fine_ref.shape[1] - 2
    n_coarse = coarse_ref.shape[1]
    tiles = cols // TILE
    some = pl.ds(offset, shares)
    later = (
        pltpu.make_async_copy(kept_ref.at[some], got_ref, sems.at[0]),
        pltpu.make_async_copy(fine_hbm.at[some], fine_ref, sems.at[1]),
        pltpu.make_async_copy(coarse_hbm.at[some], coarse_ref, sems.at[2]),
    )

    def begin():
        for copy in later:
            copy.start()

    before(begin)

    def collect(share, side, table, n, sums):
        half = n // 2
        for d in range(days):
            for t in range(tiles):
                at = tile_lanes(tiles, d, t)
                p = jnp.zeros((b, TILE), F32)
                q = jnp.zeros((b, TILE), F32)
                for k in range(half):
                    one = sums[k * b:(k + 1) * b, at]
                    two = sums[(half + k) * b:(half + k + 1) * b, at]
                    p = p + (one + two) * table[share, k:k + 1, part(t)]
                    q = q + (one - two) * table[share, half + k:half + k + 1, part(t)]
                value = p + swap_halves(q)
                if side == 0:
                    value = turn_half(value, table, share, t, -1)
                out_ref[share, d, side * b:(side + 1) * b, part(t)] = (value * (scalars_ref[d] * scale)).astype(BF16)

    for copy in later:
        copy.wait()
    sums_b[...] = jnp.zeros_like(sums_b)
    turn_columns(got_ref, 0, b, coarse_ref, turned_b)

    def one_share(share, carry):
        sums_a[...] = dot(res[...], turned_b[...])
        turn_rows(got_ref, share, b, fine_ref, turned_a, rows_u, rows_v)
        collect(jnp.maximum(share - 1, 0), 1, coarse_ref, n_coarse, sums_b)
        sums_b[...] = dot(res_t[...], turned_a[...])
        collect(share, 0, fine_ref, n_fine, sums_a)
        turn_columns(got_ref, jnp.minimum(share + 1, shares - 1), b, coarse_ref, turned_b)
        return carry

    lax.fori_loop(0, shares, one_share, 0)
    collect(shares - 1, 1, coarse_ref, n_coarse, sums_b)


def far_kernel(
    sizes, offset_ref, scalars_ref, mine_ref, other_ref, seen_hbm, env_hbm, hilbert_hbm, kept_ref, fine_hbm, coarse_hbm,
    out_ref, res_hbm, res_t_hbm, seen_ref, env_ref, hilbert_ref, lagged, back, got_ref, fine_ref, coarse_ref, res, res_t,
    sums_a, sums_b, turned_a, turned_b, rows_u, rows_v, sems_s, sems_e, sems,
):
    b, scale, group = sizes
    out = (
        pltpu.make_async_copy(res, res_hbm, sems.at[4]),
        pltpu.make_async_copy(res_t, res_t_hbm, sems.at[5]),
    )

    def before(begin):
        residual_stage(
            b, group, scalars_ref, mine_ref, other_ref, seen_hbm, env_hbm, hilbert_hbm, seen_ref, env_ref, hilbert_ref,
            lagged, back, res, res_t, sems_s, sems_e, sems.at[3], begin,
        )
        for copy in out:
            copy.start()

    adjoint_stage(
        (b, scale), offset_ref[0], scalars_ref, kept_ref, fine_hbm, coarse_hbm, out_ref, got_ref, fine_ref, coarse_ref,
        res, res_t, sums_a, sums_b, turned_a, turned_b, rows_u, rows_v, sems, before,
    )
    for copy in out:
        copy.wait()


def near_kernel(
    sizes, offset_ref, scalars_ref, res_hbm, res_t_hbm, kept_ref, fine_hbm, coarse_hbm, out_ref, got_ref, fine_ref,
    coarse_ref, res, res_t, sums_a, sums_b, turned_a, turned_b, rows_u, rows_v, sems,
):
    copies = (
        pltpu.make_async_copy(res_hbm, res, sems.at[3]),
        pltpu.make_async_copy(res_t_hbm, res_t, sems.at[4]),
    )

    def before(begin):
        for copy in copies:
            copy.start()
        begin()
        for copy in copies:
            copy.wait()

    adjoint_stage(
        sizes, offset_ref[0], scalars_ref, kept_ref, fine_hbm, coarse_hbm, out_ref, got_ref, fine_ref, coarse_ref, res,
        res_t, sums_a, sums_b, turned_a, turned_b, rows_u, rows_v, sems, before,
    )


def turn_tables(columns, lags, shares, n_fine):
    freqs = columns // 2
    n_coarse = lags // n_fine
    column = np.arange(columns)
    frequency = column // TILE * HALF + column % HALF
    is_real = column % TILE < HALF

    def table(halves, sign):
        phase = frequency[None, :] * halves[:, None] % (4 * freqs)
        angles = np.pi * phase / (2 * freqs)
        sine = np.where(is_real[None, :], -sign, sign) * np.sin(angles)
        return np.concatenate([np.cos(angles), sine])

    def place(rows):
        rows = rows.astype(np.float32).reshape(rows.shape[0], shares, columns // shares)
        return np.ascontiguousarray(rows.transpose(1, 0, 2))

    fine = table(2 * np.arange(n_fine // 2) + 1, 1)
    coarse = table(n_fine * (2 * np.arange(n_coarse // 2) + 1), -1)
    return place(np.concatenate([fine, table(np.array([1]), -1)])), place(coarse)


def adjoint_scratch(kept, fine, coarse, part_shares):
    _, days, rows, cols = kept.shape
    b = rows // 2
    n_fine = fine.shape[1] - 2
    n_coarse = coarse.shape[1]
    lanes = days * cols
    return [pltpu.VMEM((part_shares,) + x.shape[1:], x.dtype) for x in (kept, fine, coarse)] + [
        pltpu.VMEM((n_fine * b, n_coarse * b), BF16),
        pltpu.VMEM((n_coarse * b, n_fine * b), BF16),
        pltpu.VMEM((n_fine * b, lanes), F32),
        pltpu.VMEM((n_coarse * b, lanes), F32),
        pltpu.VMEM((n_fine * b, lanes), BF16),
        pltpu.VMEM((n_coarse * b, lanes), BF16),
        pltpu.VMEM((b, lanes), F32),
        pltpu.VMEM((b, lanes), F32),
    ]


def far_pass(offset, scalars, mine, other, seen, env, hilbert, kept, fine, coarse, parts):
    shares, days, rows, cols = kept.shape
    b = rows // 2
    n_fine = fine.shape[1] - 2
    n_coarse = coarse.shape[1]
    scale = 1.0 / math.sqrt(shares * cols // 2)
    group = b // parts
    vmem = pl.BlockSpec(memory_space=pltpu.VMEM)
    hbm = pl.BlockSpec(memory_space=pltpu.HBM)
    smem = pl.BlockSpec(memory_space=pltpu.SMEM)
    apart = [pltpu.with_memory_space_constraint(x, pltpu.HBM) for x in (seen, env, hilbert, kept, fine, coarse)]
    return pl.pallas_call(
        functools.partial(far_kernel, (b, scale, group)),
        out_shape=[
            jax.ShapeDtypeStruct((shares // 2,) + kept.shape[1:], BF16),
            pltpu.HBM((n_fine * b, n_coarse * b), BF16),
            pltpu.HBM((n_coarse * b, n_fine * b), BF16),
        ],
        in_specs=[smem, smem, vmem, vmem] + [hbm] * len(apart),
        out_specs=[vmem, hbm, hbm],
        scratch_shapes=[pltpu.VMEM(x.shape, x.dtype) for x in apart[:3]]
        + [
            pltpu.VMEM((n_coarse // 2, n_fine * b, 2 * b), F32),
            pltpu.VMEM((group * n_fine, n_coarse * b), F32),
        ]
        + adjoint_scratch(kept, fine, coarse, shares // 2)
        + [
            pltpu.SemaphoreType.DMA((parts,)),
            pltpu.SemaphoreType.DMA((parts,)),
            pltpu.SemaphoreType.DMA((6,)),
        ],
        compiler_params=pltpu.CompilerParams(vmem_limit_bytes=24 << 20),
        name="far",
    )(offset, scalars, mine, other, *apart)


def near_pass(offset, scalars, res, res_t, kept, fine, coarse):
    shares, days, rows, cols = kept.shape
    scale = 1.0 / math.sqrt(shares * cols // 2)
    hbm = pl.BlockSpec(memory_space=pltpu.HBM)
    smem = pl.BlockSpec(memory_space=pltpu.SMEM)
    apart = [pltpu.with_memory_space_constraint(x, pltpu.HBM) for x in (res, res_t, kept, fine, coarse)]
    return pl.pallas_call(
        functools.partial(near_kernel, (rows // 2, scale)),
        out_shape=jax.ShapeDtypeStruct((shares // 2,) + kept.shape[1:], BF16),
        in_specs=[smem, smem] + [hbm] * len(apart),
        out_specs=pl.BlockSpec(memory_space=pltpu.VMEM),
        scratch_shapes=adjoint_scratch(kept, fine, coarse, shares // 2) + [pltpu.SemaphoreType.DMA((5,))],
        compiler_params=pltpu.CompilerParams(vmem_limit_bytes=24 << 20),
        name="near",
    )(offset, scalars, *apart)


def body(spectra, observed, pair_blocks, members, day_mask):
    half_shares = lax.axis_size("near")
    shares = 2 * half_shares
    slots, b, _, lags = observed.shape
    _, stations, cols = spectra.shape
    n_fine = 16
    fine, coarse = turn_tables(shares * cols, lags, shares, n_fine)
    orders, hilbert = hilbert_parts(lags, n_fine)
    slot = lax.axis_index("slot")
    members = members.reshape(1, stations)
    pair_blocks = pair_blocks.T
    first_day = lax.axis_index("outer") * slots * CORES + lax.axis_index("core")
    mask = lax.dynamic_slice_in_dim(day_mask, slot, 1, 0)[0].astype(F32)
    mask_here = jnp.stack([lax.dynamic_index_in_dim(mask, first_day + k * CORES, 0, False) for k in range(slots)])
    count = jnp.sum(mask)
    scale = 1.0 / math.sqrt(shares * cols // 2)
    scalars = jnp.concatenate([mask_here / count, scale / count[None]])

    sent = pack(pair_blocks, members, spectra, b)
    got = lax.all_to_all(sent, ("half", "near", "slot"), 0, 0, tiled=True)
    got = got.reshape(shares, slots, 2 * b, cols)
    parts = 4
    orders, hilbert, fine, coarse = [jnp.asarray(x) for x in (orders, hilbert, fine, coarse)]
    seen, env = prepare(slot[None], observed.reshape(slots, b * b, lags), orders, parts)
    got, seen, env = lax.optimization_barrier((got, seen, env))
    mine, sent, kept = forward_pass(mask_here, got, fine, coarse)
    for axis in ("outer", "core"):
        n = lax.axis_size(axis)
        others = [lax.ppermute(sent, axis, [(i, (i + k) % n) for i in range(n)]) for k in range(1, n)]
        if axis == "outer" and others:
            for other in others:
                mine = mine + other.astype(F32)
            sent = mine.astype(BF16)
    half = lax.axis_index("half")
    own_blocks = lax.dynamic_slice_in_dim(pair_blocks, half * half_shares * slots, half_shares * slots, 1)

    def exchange(contrib):
        flat = contrib.reshape(half_shares * slots, 2 * b, cols)
        return lax.all_to_all(flat, ("near", "slot"), 0, 0, tiled=True)

    start_far = ((1 - half) * half_shares)[None]
    start_near = (half * half_shares)[None]
    contrib, res, res_t = far_pass(
        start_far, scalars, mine, others[0], seen, env, hilbert, kept, fine, coarse, parts
    )
    got_far = exchange(contrib)
    contrib = near_pass(start_near, scalars, res, res_t, kept, fine, coarse)
    across = gather(own_blocks, got_far, stations)
    contrib, across = lax.optimization_barrier((contrib, across))
    across = lax.ppermute(across, "half", [(0, 1), (1, 0)])
    got_near = exchange(contrib)
    return unpack(own_blocks, members, got_near, across)


def solution(mesh):
    shares, days = mesh.devices.shape
    names = ("half", "near", "outer", "slot", "core")

    def run(spectra, observed, pair_blocks, members, day_mask):
        slots = observed.shape[0] // shares
        split = (2, shares // 2, days // CORES // slots, slots, CORES)
        finer = Mesh(mesh.devices.reshape(split), names)
        day_axes = names[2:]
        pair_axes = names[:2]
        return jax.shard_map(
            body,
            mesh=finer,
            in_specs=(
                P(day_axes, None, pair_axes),
                P(pair_axes, None, None, None),
                P(),
                P(),
                P(pair_axes, None),
            ),
            out_specs=P(day_axes, None, pair_axes),
            check_vma=False,
        )(spectra, observed, pair_blocks, members, day_mask)

    return run
```

```python
import functools
import math

import jax
import jax.numpy as jnp
import ml_dtypes
import numpy as np
from jax import lax
from jax.experimental import pallas as pl
from jax.experimental.pallas import tpu as pltpu
from jax.sharding import Mesh, PartitionSpec as P

HALF = 64
TILE = 128
CORES = 2
F32 = jnp.float32
BF16 = jnp.bfloat16


def lag_order(lags, n_fine):
    n_coarse = lags // n_fine
    half_f, half_c = n_fine // 2, n_coarse // 2
    fine = np.concatenate([half_f + np.arange(half_f), half_f - 1 - np.arange(half_f)])
    coarse = np.concatenate([half_c + np.arange(half_c), half_c - 1 - np.arange(half_c)])
    return (n_fine * coarse[:, None] + fine[None, :]).reshape(-1)


def split_bf16(table):
    high = table.astype(ml_dtypes.bfloat16)
    return high, (table - high.astype(np.float32)).astype(ml_dtypes.bfloat16)


def hilbert_parts(lags, n_fine):
    offset = (np.arange(lags)[None, :] - np.arange(lags)[:, None]) % lags
    angles = np.float32(math.pi) * offset.astype(np.float32) / np.float32(lags)
    odd = offset % 2 == 1
    safe = np.where(odd, np.sin(angles), np.float32(1.0))
    table = np.where(odd, np.float32(2.0 / lags) * np.cos(angles) / safe, np.float32(0.0))
    table = table.astype(np.float32).T
    order = lag_order(lags, n_fine)
    high, low = split_bf16(table[order])
    chosen = np.eye(lags, dtype=np.float32)[order].astype(ml_dtypes.bfloat16)
    high_both, low_both = split_bf16(table[order][:, order])
    return (
        np.concatenate([chosen, high, low], axis=0),
        np.concatenate([high_both, low_both, high_both], axis=1),
    )


def left_lanes(shape):
    return lax.broadcasted_iota(jnp.int32, shape, len(shape) - 1) % TILE < HALF


def swap_halves(x):
    return pltpu.roll(x, HALF, 1)


def dot(a, b):
    return jnp.dot(a, b, preferred_element_type=F32)


def pack_kernel(first_ref, blocks_hbm, members_hbm, spectra_hbm, out_ref, blocks_ref, members_ref, spectra_ref, ordered, sems):
    stations = spectra_ref.shape[1]
    b = out_ref.shape[1] // 2
    copies = (
        pltpu.make_async_copy(spectra_hbm, spectra_ref, sems.at[0]),
        pltpu.make_async_copy(members_hbm, members_ref, sems.at[1]),
        pltpu.make_async_copy(blocks_hbm, blocks_ref, sems.at[2]),
    )
    for copy in copies:
        copy.start()
    station = lax.broadcasted_iota(jnp.int32, (stations, stations), 0)
    copies[1].wait()
    chosen = (station == members_ref[...]).astype(F32).astype(BF16)
    copies[0].wait()
    ordered[...] = lax.dot_general(
        chosen, spectra_ref[0], (((0,), (0,)), ((), ())), preferred_element_type=F32
    ).astype(BF16)
    copies[2].wait()
    for p in range(out_ref.shape[0]):
        for side in range(2):
            row = pl.multiple_of(blocks_ref[side, first_ref[0] + p] * b, b)
            out_ref[p, side * b:(side + 1) * b, :] = ordered[pl.ds(row, b), :]


def pack(first, pair_blocks, members, spectra, b):
    _, stations, cols = spectra.shape
    n_pairs = pair_blocks.shape[1] // 2
    arrays = [pltpu.with_memory_space_constraint(x, pltpu.HBM) for x in (pair_blocks, members, spectra)]
    return pl.pallas_call(
        pack_kernel,
        out_shape=pltpu.VMEM((n_pairs, 2 * b, cols), BF16),
        in_specs=[pl.BlockSpec(memory_space=pltpu.SMEM)] + [pl.BlockSpec(memory_space=pltpu.HBM)] * 3,
        out_specs=pl.BlockSpec(memory_space=pltpu.VMEM),
        scratch_shapes=[
            pltpu.SMEM(pair_blocks.shape, pair_blocks.dtype),
            pltpu.VMEM(members.shape, members.dtype),
            pltpu.VMEM(spectra.shape, BF16),
            pltpu.VMEM((stations, cols), BF16),
            pltpu.SemaphoreType.DMA((3,)),
        ],
        compiler_params=pltpu.CompilerParams(vmem_limit_bytes=8 << 20),
        name="pack",
    )(first, *arrays)


def unpack_kernel(blocks_ref, members_ref, got_ref, out_ref, total):
    stations = out_ref.shape[1]
    b = got_ref.shape[1] // 2
    total[...] = jnp.zeros_like(total)
    for p in range(got_ref.shape[0]):
        for side in range(2):
            rows = pl.ds(pl.multiple_of(blocks_ref[side, p] * b, b), b)
            total[rows, :] += got_ref[p, side * b:(side + 1) * b, :].astype(F32)
    station = lax.broadcasted_iota(jnp.int32, (stations, stations), 0)
    chosen = (station == members_ref[...]).astype(F32).astype(BF16)
    whole = total[...]
    high = whole.astype(BF16)
    rest = whole - high.astype(F32)
    mid = rest.astype(BF16)
    low = (rest - mid.astype(F32)).astype(BF16)
    out_ref[0] = dot(chosen, high) + (dot(chosen, mid) + dot(chosen, low))


def unpack(pair_blocks, members, got, stations):
    cols = got.shape[2]
    return pl.pallas_call(
        unpack_kernel,
        out_shape=jax.ShapeDtypeStruct((1, stations, cols), F32),
        in_specs=[
            pl.BlockSpec(memory_space=pltpu.SMEM),
            pl.BlockSpec(memory_space=pltpu.VMEM),
            pl.BlockSpec(memory_space=pltpu.VMEM),
        ],
        out_specs=pl.BlockSpec(memory_space=pltpu.VMEM),
        scratch_shapes=[pltpu.VMEM((stations, cols), F32)],
        compiler_params=pltpu.CompilerParams(vmem_limit_bytes=8 << 20),
        name="unpack",
    )(pair_blocks, members, got)


def prepare_kernel(b, slot_ref, observed_ref, orders_ref, seen_ref, env_ref):
    lags = observed_ref.shape[1]
    two = 2 * b

    def some(step, carry):
        rows = observed_ref[pl.ds(pl.multiple_of(step * two, two), two), :]
        turned = lax.dot_general(orders_ref[...], rows, (((1,), (1,)), ((), ())), preferred_element_type=F32)
        seen = turned[:lags]
        hil = turned[lags:2 * lags] + turned[2 * lags:]
        seen_ref[step] = seen.astype(BF16)
        env_ref[step] = 1.0 + jnp.sqrt(seen * seen + hil * hil)
        return carry

    lax.fori_loop(0, seen_ref.shape[0], some, 0, unroll=4)


def prepare(slot, observed, orders, parts):
    _, rows, lags = observed.shape
    b = math.isqrt(rows)
    shape = (b // 2, lags, 2 * b)
    block = (b // 2 // parts, lags, 2 * b)
    spec = pltpu.PrefetchScalarGridSpec(
        num_scalar_prefetch=1,
        grid=(parts,),
        in_specs=[
            pl.BlockSpec((None, rows // parts, lags), lambda s, slot_ref: (slot_ref[0], s, 0)),
            pl.BlockSpec(orders.shape, lambda s, slot_ref: (0, 0)),
        ],
        out_specs=[pl.BlockSpec(block, lambda s, slot_ref: (s, 0, 0))] * 2,
    )
    return pl.pallas_call(
        functools.partial(prepare_kernel, b),
        out_shape=[pltpu.HBM(shape, BF16), pltpu.HBM(shape, F32)],
        grid_spec=spec,
        compiler_params=pltpu.CompilerParams(vmem_limit_bytes=8 << 20),
        cost_estimate=pl.CostEstimate(flops=2 * rows * lags * lags, bytes_accessed=8 * rows * lags, transcendentals=0),
        name="prepare",
    )(slot, observed, orders)


def tile_lanes(tiles, d, t):
    return slice((d * tiles + t) * TILE, (d * tiles + t + 1) * TILE)


def part(t):
    return slice(t * TILE, (t + 1) * TILE)


def turn_columns(got_ref, share, b, table_ref, into, row=None):
    _, days, _, cols = got_ref.shape
    tiles = cols // TILE
    half = table_ref.shape[1] // 2
    row = share if row is None else row
    for d in range(days):
        for t in range(tiles):
            at = tile_lanes(tiles, d, t)
            u = got_ref[share, d, b:, part(t)].astype(F32)
            v = swap_halves(u)
            for k in range(half):
                one = u * table_ref[row, k:k + 1, part(t)]
                two = v * table_ref[row, half + k:half + k + 1, part(t)]
                into[k * b:(k + 1) * b, at] = (one + two).astype(BF16)
                into[(half + k) * b:(half + k + 1) * b, at] = (one - two).astype(BF16)


def turn_rows(got_ref, share, b, table_ref, into, rows_u, rows_v, mask_ref=None, row=None):
    _, days, _, cols = got_ref.shape
    tiles = cols // TILE
    half = table_ref.shape[1] // 2 - 1
    row = share if row is None else row
    pieces = [(d, t) for d in range(days) for t in range(tiles)]
    for d, t in pieces:
        at = tile_lanes(tiles, d, t)
        u = got_ref[share, d, :b, part(t)].astype(F32)
        if mask_ref is not None:
            u = u * mask_ref[d]
        u = turn_half(u, table_ref, row, t, 1)
        rows_u[:, at] = u
        rows_v[:, at] = swap_halves(u)
    for d, t in pieces:
        at = tile_lanes(tiles, d, t)
        cosine = table_ref[row, :half, part(t)]
        sine = table_ref[row, half:2 * half, part(t)]
        for k in range(b):
            one = rows_u[k:k + 1, at] * cosine
            two = rows_v[k:k + 1, at] * sine
            into[2 * k * half:2 * (k + 1) * half, at] = jnp.concatenate([one + two, one - two], axis=0).astype(BF16)


def turn_half(u, table_ref, share, t, sign):
    at = table_ref.shape[1] - 2
    one = u * table_ref[share, at:at + 1, part(t)]
    two = swap_halves(u) * table_ref[share, at + 1:at + 2, part(t)]
    return one + two if sign > 0 else one - two


def forward_kernel(b, last, offset_ref, mask_ref, got_ref, fine_ref, coarse_ref, *refs):
    before_ref, refs = (refs[0], refs[1:]) if last else (None, refs)
    out_ref, refs = refs[0], refs[1:]
    sent_ref, refs = (refs[0], refs[1:]) if last else (None, refs)
    kept_ref, even_a, even_b, odd_a, odd_b, rows_u, rows_v, sem = refs
    shares = got_ref.shape[0]
    even = (even_a, even_b)
    odd = (odd_a, odd_b)
    keep = pltpu.make_async_copy(got_ref, kept_ref, sem)
    keep.start()

    def make(share, into):
        row = offset_ref[0] + share
        turn_columns(got_ref, share, b, coarse_ref, into[1], row)
        turn_rows(got_ref, share, b, fine_ref, into[0], rows_u, rows_v, mask_ref, row)

    def product(made):
        return lax.dot_general(made[0][...], made[1][...], (((1,), (1,)), ((), ())), preferred_element_type=F32)

    make(0, even)
    out_ref[...] = before_ref[...] + product(even) if last else product(even)
    make(1, odd)

    def two_shares(step, carry):
        out_ref[...] += product(odd)
        make(2 * step + 2, even)
        out_ref[...] += product(even)
        make(2 * step + 3, odd)
        return carry

    lax.fori_loop(0, shares // 2 - 1, two_shares, 0)
    total = out_ref[...] + product(odd)
    out_ref[...] = total
    if last:
        sent_ref[...] = total.astype(sent_ref.dtype)
    keep.wait()


def forward_pass(offset, mask, got, fine, coarse, before):
    shares, days, rows, cols = got.shape
    assert shares % 2 == 0
    b = rows // 2
    n_fine = fine.shape[1] - 2
    n_coarse = coarse.shape[1]
    vmem = pl.BlockSpec(memory_space=pltpu.VMEM)
    smem = pl.BlockSpec(memory_space=pltpu.SMEM)
    shape = (n_fine * b, n_coarse * b)
    sent = [jax.ShapeDtypeStruct(shape, BF16)] * len(before)
    return pl.pallas_call(
        functools.partial(forward_kernel, b, bool(before)),
        out_shape=[pltpu.VMEM(shape, F32)] + sent + [pltpu.HBM(got.shape, BF16)],
        in_specs=[smem, smem, vmem, vmem, vmem] + [vmem] * len(before),
        out_specs=[vmem] + [vmem] * len(before) + [pl.BlockSpec(memory_space=pltpu.HBM)],
        input_output_aliases={5: 0} if before else {},
        scratch_shapes=[
            pltpu.VMEM((n_fine * b, days * cols), BF16),
            pltpu.VMEM((n_coarse * b, days * cols), BF16),
            pltpu.VMEM((n_fine * b, days * cols), BF16),
            pltpu.VMEM((n_coarse * b, days * cols), BF16),
            pltpu.VMEM((b, days * cols), F32),
            pltpu.VMEM((b, days * cols), F32),
            pltpu.SemaphoreType.DMA,
        ],
        compiler_params=pltpu.CompilerParams(vmem_limit_bytes=16 << 20),
        name="forward",
    )(offset, mask, got, fine, coarse, *before)


def residual_stage(
    b, group, scalars_ref, mine_ref, other_ref, seen_hbm, env_hbm, hilbert_hbm, seen_ref, env_ref, hilbert_ref, lagged,
    back, res, res_t, sems_s, sems_e, sem, begin,
):
    n_fine = mine_ref.shape[0] // b
    slabs = mine_ref.shape[1] // TILE
    days = scalars_ref.shape[0] - 1
    block = group * n_fine
    left = left_lanes((n_fine, 2 * b))

    def bring(step):
        some = pl.ds(step * (group // 2), group // 2)
        return (
            pltpu.make_async_copy(seen_hbm.at[some], seen_ref.at[some], sems_s.at[step]),
            pltpu.make_async_copy(env_hbm.at[some], env_ref.at[some], sems_e.at[step]),
        )

    first = pltpu.make_async_copy(hilbert_hbm, hilbert_ref, sem)
    first.start()
    for step in range(b // group):
        for copy in bring(step):
            copy.start()
    begin()
    first.wait()

    def residual_rows(step, carry):
        for copy in bring(step):
            copy.wait()
        for two in range(0, group, 2):
            rows = []
            for slab in range(slabs):
                got = []
                for k in (two, two + 1):
                    at = pl.ds(pl.multiple_of(step * block + k * n_fine, n_fine), n_fine)
                    got.append((mine_ref[at, part(slab)] + other_ref[at, part(slab)].astype(F32)) * scalars_ref[days])
                rows.append(jnp.where(left, got[0], swap_halves(got[1])))
                rows.append(jnp.where(left, swap_halves(got[0]), got[1]))
            stacked = jnp.concatenate(rows, axis=0)
            high = stacked.astype(BF16)
            low = (stacked - high.astype(F32)).astype(BF16)
            hil = dot(hilbert_ref[...], jnp.concatenate([high, high, low], axis=0))
            env_s = 1.0 + jnp.sqrt(stacked * stacked + hil * hil)
            env_o = env_ref[step * (group // 2) + two // 2]
            value = (stacked - seen_ref[step * (group // 2) + two // 2].astype(F32)) * (env_s / (env_s + env_o - 1.0))
            for slab in range(slabs):
                even = value[2 * slab * n_fine:(2 * slab + 1) * n_fine, :]
                odd = value[(2 * slab + 1) * n_fine:(2 * slab + 2) * n_fine, :]
                first = jnp.where(left, even, swap_halves(odd))
                second = jnp.where(left, swap_halves(even), odd)
                for k, rows in ((two, first), (two + 1, second)):
                    lagged[slab, pl.ds(step * group + k, n_fine, stride=b), :] = rows
                    back[k * n_fine:(k + 1) * n_fine, part(slab)] = rows
        at = pl.ds(pl.multiple_of(step * block, block), block)
        for slab in range(slabs):
            res_t[part(slab), at] = back[:, part(slab)].T.astype(BF16)
        return carry

    lax.fori_loop(0, b // group, residual_rows, 0)

    def round_rows(step, carry):
        at = pl.ds(pl.multiple_of(step * b, b), b)
        for slab in range(slabs):
            res[at, part(slab)] = lagged[slab, at, :].astype(BF16)
        return carry

    lax.fori_loop(0, n_fine, round_rows, 0)


def adjoint_stage(
    sizes, starts_ref, scalars_ref, near_ref, far_ref, fine_hbm, coarse_hbm, out_ref, got_ref, fine_ref, coarse_ref, res,
    res_t, sums_a, sums_b, turned_a, turned_b, rows_u, rows_v, sems, before,
):
    b, scale = sizes
    shares, days, _, cols = out_ref.shape
    n_fine = fine_ref.shape[1] - 2
    n_coarse = coarse_ref.shape[1]
    tiles = cols // TILE
    count = shares // 2
    later = []
    for k, kept_ref in enumerate((near_ref, far_ref)):
        here = pl.ds(k * count, count)
        some = pl.ds(starts_ref[k], count)
        later += [
            pltpu.make_async_copy(kept_ref, got_ref.at[here], sems.at[3 * k]),
            pltpu.make_async_copy(fine_hbm.at[some], fine_ref.at[here], sems.at[3 * k + 1]),
            pltpu.make_async_copy(coarse_hbm.at[some], coarse_ref.at[here], sems.at[3 * k + 2]),
        ]

    def place(share):
        return jnp.where(share < count, starts_ref[0] + share, starts_ref[1] + share - count)

    def begin():
        for copy in later:
            copy.start()

    before(begin)

    def collect(share, side, table, n, sums):
        half = n // 2
        for d in range(days):
            for t in range(tiles):
                at = tile_lanes(tiles, d, t)
                p = jnp.zeros((b, TILE), F32)
                q = jnp.zeros((b, TILE), F32)
                for k in range(half):
                    one = sums[k * b:(k + 1) * b, at]
                    two = sums[(half + k) * b:(half + k + 1) * b, at]
                    p = p + (one + two) * table[share, k:k + 1, part(t)]
                    q = q + (one - two) * table[share, half + k:half + k + 1, part(t)]
                value = p + swap_halves(q)
                if side == 0:
                    value = turn_half(value, table, share, t, -1)
                out_ref[place(share), d, side * b:(side + 1) * b, part(t)] = (value * (scalars_ref[d] * scale)).astype(BF16)

    for copy in later:
        copy.wait()
    sums_b[...] = jnp.zeros_like(sums_b)
    turn_columns(got_ref, 0, b, coarse_ref, turned_b)

    def one_share(share, carry):
        sums_a[...] = dot(res[...], turned_b[...])
        turn_rows(got_ref, share, b, fine_ref, turned_a, rows_u, rows_v)
        collect(jnp.maximum(share - 1, 0), 1, coarse_ref, n_coarse, sums_b)
        sums_b[...] = dot(res_t[...], turned_a[...])
        collect(share, 0, fine_ref, n_fine, sums_a)
        turn_columns(got_ref, jnp.minimum(share + 1, shares - 1), b, coarse_ref, turned_b)
        return carry

    lax.fori_loop(0, shares, one_share, 0)
    collect(shares - 1, 1, coarse_ref, n_coarse, sums_b)


def adjoint_kernel(
    sizes, starts_ref, scalars_ref, mine_ref, other_ref, seen_hbm, env_hbm, hilbert_hbm, near_ref, far_ref, fine_hbm,
    coarse_hbm, out_ref, seen_ref, env_ref, hilbert_ref, lagged, back, got_ref, fine_ref, coarse_ref, res, res_t,
    sums_a, sums_b, turned_a, turned_b, rows_u, rows_v, sems_s, sems_e, sems,
):
    b, scale, group = sizes

    def before(begin):
        residual_stage(
            b, group, scalars_ref, mine_ref, other_ref, seen_hbm, env_hbm, hilbert_hbm, seen_ref, env_ref, hilbert_ref,
            lagged, back, res, res_t, sems_s, sems_e, sems.at[6], begin,
        )

    adjoint_stage(
        (b, scale), starts_ref, scalars_ref, near_ref, far_ref, fine_hbm, coarse_hbm, out_ref, got_ref, fine_ref,
        coarse_ref, res, res_t, sums_a, sums_b, turned_a, turned_b, rows_u, rows_v, sems, before,
    )


def turn_tables(columns, lags, shares, n_fine):
    freqs = columns // 2
    n_coarse = lags // n_fine
    column = np.arange(columns)
    frequency = column // TILE * HALF + column % HALF
    is_real = column % TILE < HALF

    def table(halves, sign):
        phase = frequency[None, :] * halves[:, None] % (4 * freqs)
        angles = np.pi * phase / (2 * freqs)
        sine = np.where(is_real[None, :], -sign, sign) * np.sin(angles)
        return np.concatenate([np.cos(angles), sine])

    def place(rows):
        rows = rows.astype(np.float32).reshape(rows.shape[0], shares, columns // shares)
        return np.ascontiguousarray(rows.transpose(1, 0, 2))

    fine = table(2 * np.arange(n_fine // 2) + 1, 1)
    coarse = table(n_fine * (2 * np.arange(n_coarse // 2) + 1), -1)
    return place(np.concatenate([fine, table(np.array([1]), -1)])), place(coarse)


def adjoint_pass(starts, scalars, mine, other, seen, env, hilbert, near, far, fine, coarse, parts):
    half_shares, days, rows, cols = near.shape
    shares = 2 * half_shares
    b = rows // 2
    n_fine = fine.shape[1] - 2
    n_coarse = coarse.shape[1]
    lanes = days * cols
    scale = 1.0 / math.sqrt(shares * cols // 2)
    group = b // parts
    vmem = pl.BlockSpec(memory_space=pltpu.VMEM)
    hbm = pl.BlockSpec(memory_space=pltpu.HBM)
    smem = pl.BlockSpec(memory_space=pltpu.SMEM)
    apart = [pltpu.with_memory_space_constraint(x, pltpu.HBM) for x in (seen, env, hilbert, near, far, fine, coarse)]
    shape = (shares, days, rows, cols)
    return pl.pallas_call(
        functools.partial(adjoint_kernel, (b, scale, group)),
        out_shape=jax.ShapeDtypeStruct(shape, BF16),
        in_specs=[smem, smem, vmem, vmem] + [hbm] * len(apart),
        out_specs=vmem,
        scratch_shapes=[pltpu.VMEM(x.shape, x.dtype) for x in apart[:3]]
        + [
            pltpu.VMEM((n_coarse // 2, n_fine * b, 2 * b), F32),
            pltpu.VMEM((group * n_fine, n_coarse * b), F32),
            pltpu.VMEM(shape, BF16),
            pltpu.VMEM(fine.shape, F32),
            pltpu.VMEM(coarse.shape, F32),
            pltpu.VMEM((n_fine * b, n_coarse * b), BF16),
            pltpu.VMEM((n_coarse * b, n_fine * b), BF16),
            pltpu.VMEM((n_fine * b, lanes), F32),
            pltpu.VMEM((n_coarse * b, lanes), F32),
            pltpu.VMEM((n_fine * b, lanes), BF16),
            pltpu.VMEM((n_coarse * b, lanes), BF16),
            pltpu.VMEM((b, lanes), F32),
            pltpu.VMEM((b, lanes), F32),
            pltpu.SemaphoreType.DMA((parts,)),
            pltpu.SemaphoreType.DMA((parts,)),
            pltpu.SemaphoreType.DMA((7,)),
        ],
        compiler_params=pltpu.CompilerParams(vmem_limit_bytes=24 << 20),
        name="adjoint",
    )(starts, scalars, mine, other, *apart)


def body(spectra, observed, pair_blocks, members, day_mask):
    half_shares = lax.axis_size("near")
    shares = 2 * half_shares
    slots, b, _, lags = observed.shape
    _, stations, cols = spectra.shape
    n_fine = 16
    fine, coarse = turn_tables(shares * cols, lags, shares, n_fine)
    orders, hilbert = hilbert_parts(lags, n_fine)
    slot = lax.axis_index("slot")
    members = members.reshape(1, stations)
    pair_blocks = pair_blocks.T
    first_day = lax.axis_index("outer") * slots * CORES + lax.axis_index("core")
    mask = lax.dynamic_slice_in_dim(day_mask, slot, 1, 0)[0].astype(F32)
    mask_here = jnp.stack([lax.dynamic_index_in_dim(mask, first_day + k * CORES, 0, False) for k in range(slots)])
    count = jnp.sum(mask)
    scale = 1.0 / math.sqrt(shares * cols // 2)
    scalars = jnp.concatenate([mask_here / count, scale / count[None]])

    half = lax.axis_index("half")
    start_far = ((1 - half) * half_shares)[None]
    start_near = (half * half_shares)[None]
    first_pair = start_near * slots

    def exchange(x):
        flat = x.reshape(half_shares * slots, 2 * b, cols)
        moved = lax.all_to_all(flat, ("near", "slot"), 0, 0, tiled=True)
        return moved

    shape = (half_shares, slots, 2 * b, cols)
    opposite = lax.ppermute(spectra, "half", [(0, 1), (1, 0)])
    got_near = exchange(pack(first_pair, pair_blocks, members, spectra, b))
    orders, hilbert, fine, coarse = [jnp.asarray(x) for x in (orders, hilbert, fine, coarse)]
    parts = 4
    seen, env = prepare(slot[None], observed.reshape(slots, b * b, lags), orders, parts)
    got_near, opposite, seen, env, mask_here, scalars = lax.optimization_barrier(
        (got_near, opposite, seen, env, mask_here, scalars)
    )
    got_far = exchange(pack(first_pair, pair_blocks, members, opposite, b))
    mine, kept_near = forward_pass(start_near, mask_here, got_near.reshape(shape), fine, coarse, [])
    got_far, mine = lax.optimization_barrier((got_far, mine))
    mine, sent, kept_far = forward_pass(start_far, mask_here, got_far.reshape(shape), fine, coarse, [mine])
    for axis in ("outer", "core"):
        n = lax.axis_size(axis)
        others = [lax.ppermute(sent, axis, [(i, (i + k) % n) for i in range(n)]) for k in range(1, n)]
        if axis == "outer" and others:
            for other in others:
                mine = mine + other.astype(F32)
            sent = mine.astype(BF16)
    starts = jnp.concatenate([start_near, start_far])
    contrib = adjoint_pass(
        starts, scalars, mine, others[0], seen, env, hilbert, kept_near, kept_far, fine, coarse, parts
    )
    returned = lax.all_to_all(
        contrib.reshape(shares * slots, 2 * b, cols), ("half", "near", "slot"), 0, 0, tiled=True
    )
    return unpack(pair_blocks, members, returned, stations)


def solution(mesh):
    shares, days = mesh.devices.shape
    names = ("half", "near", "outer", "slot", "core")

    def run(spectra, observed, pair_blocks, members, day_mask):
        slots = observed.shape[0] // shares
        split = (2, shares // 2, days // CORES // slots, slots, CORES)
        finer = Mesh(mesh.devices.reshape(split), names)
        day_axes = names[2:]
        pair_axes = names[:2]
        return jax.shard_map(
            body,
            mesh=finer,
            in_specs=(
                P(day_axes, None, pair_axes),
                P(pair_axes, None, None, None),
                P(),
                P(),
                P(pair_axes, None),
            ),
            out_specs=P(day_axes, None, pair_axes),
            check_vma=False,
        )(spectra, observed, pair_blocks, members, day_mask)

    return run
```

```python
import functools
import math

import jax
import jax.numpy as jnp
import ml_dtypes
import numpy as np
from jax import lax
from jax.experimental import pallas as pl
from jax.experimental.pallas import tpu as pltpu
from jax.sharding import Mesh, PartitionSpec as P

HALF = 64
TILE = 128
CORES = 2
F32 = jnp.float32
BF16 = jnp.bfloat16


def lag_order(lags, n_fine):
    n_coarse = lags // n_fine
    half_f, half_c = n_fine // 2, n_coarse // 2
    fine = np.concatenate([half_f + np.arange(half_f), half_f - 1 - np.arange(half_f)])
    coarse = np.concatenate([half_c + np.arange(half_c), half_c - 1 - np.arange(half_c)])
    return (n_fine * coarse[:, None] + fine[None, :]).reshape(-1)


def split_bf16(table):
    high = table.astype(ml_dtypes.bfloat16)
    return high, (table - high.astype(np.float32)).astype(ml_dtypes.bfloat16)


def hilbert_parts(lags, n_fine):
    offset = (np.arange(lags)[None, :] - np.arange(lags)[:, None]) % lags
    angles = np.float32(math.pi) * offset.astype(np.float32) / np.float32(lags)
    odd = offset % 2 == 1
    safe = np.where(odd, np.sin(angles), np.float32(1.0))
    table = np.where(odd, np.float32(2.0 / lags) * np.cos(angles) / safe, np.float32(0.0))
    table = table.astype(np.float32).T
    order = lag_order(lags, n_fine)
    high, low = split_bf16(table[order])
    chosen = np.eye(lags, dtype=np.float32)[order].astype(ml_dtypes.bfloat16)
    high_both, low_both = split_bf16(table[order][:, order])
    return (
        np.concatenate([chosen, high, low], axis=0),
        np.concatenate([high_both, low_both, high_both], axis=1),
    )


def left_lanes(shape):
    return lax.broadcasted_iota(jnp.int32, shape, len(shape) - 1) % TILE < HALF


def swap_halves(x):
    return pltpu.roll(x, HALF, 1)


def dot(a, b):
    return jnp.dot(a, b, preferred_element_type=F32)


def pack_rows(first_ref, blocks_ref, members_ref, spectra_ref, out_ref, ordered, rows_there=None, blocks_there=None):
    stations = spectra_ref.shape[1]
    b = out_ref.shape[1] // 2
    station = lax.broadcasted_iota(jnp.int32, (stations, stations), 0)
    chosen = (station == members_ref[...]).astype(F32).astype(BF16)
    if rows_there is not None:
        rows_there()
    ordered[...] = lax.dot_general(
        chosen, spectra_ref[0], (((0,), (0,)), ((), ())), preferred_element_type=F32
    ).astype(BF16)
    if blocks_there is not None:
        blocks_there()
    for p in range(out_ref.shape[0]):
        for side in range(2):
            row = pl.multiple_of(blocks_ref[side, first_ref[0] + p] * b, b)
            out_ref[p, side * b:(side + 1) * b, :] = ordered[pl.ds(row, b), :]


def pack_kernel(first_ref, blocks_hbm, members_hbm, spectra_hbm, out_ref, blocks_ref, members_ref, spectra_ref, ordered, sems):
    copies = (
        pltpu.make_async_copy(spectra_hbm, spectra_ref, sems.at[0]),
        pltpu.make_async_copy(members_hbm, members_ref, sems.at[1]),
        pltpu.make_async_copy(blocks_hbm, blocks_ref, sems.at[2]),
    )
    for copy in copies:
        copy.start()
    copies[1].wait()
    pack_rows(
        first_ref, blocks_ref, members_ref, spectra_ref, out_ref, ordered, copies[0].wait, copies[2].wait
    )


def repack(first, pair_blocks, members, spectra, b):
    _, stations, cols = spectra.shape
    smem = pl.BlockSpec(memory_space=pltpu.SMEM)
    vmem = pl.BlockSpec(memory_space=pltpu.VMEM)
    return pl.pallas_call(
        pack_rows,
        out_shape=pltpu.VMEM((pair_blocks.shape[1] // 2, 2 * b, cols), BF16),
        in_specs=[smem, smem, vmem, vmem],
        out_specs=vmem,
        scratch_shapes=[pltpu.VMEM((stations, cols), BF16)],
        compiler_params=pltpu.CompilerParams(vmem_limit_bytes=8 << 20),
        name="repack",
    )(first, pair_blocks, members, spectra)


def pack(first, pair_blocks, members, spectra, b):
    _, stations, cols = spectra.shape
    n_pairs = pair_blocks.shape[1] // 2
    arrays = [pltpu.with_memory_space_constraint(x, pltpu.HBM) for x in (pair_blocks, members, spectra)]
    return pl.pallas_call(
        pack_kernel,
        out_shape=pltpu.VMEM((n_pairs, 2 * b, cols), BF16),
        in_specs=[pl.BlockSpec(memory_space=pltpu.SMEM)] + [pl.BlockSpec(memory_space=pltpu.HBM)] * 3,
        out_specs=pl.BlockSpec(memory_space=pltpu.VMEM),
        scratch_shapes=[
            pltpu.SMEM(pair_blocks.shape, pair_blocks.dtype),
            pltpu.VMEM(members.shape, members.dtype),
            pltpu.VMEM(spectra.shape, BF16),
            pltpu.VMEM((stations, cols), BF16),
            pltpu.SemaphoreType.DMA((3,)),
        ],
        compiler_params=pltpu.CompilerParams(vmem_limit_bytes=8 << 20),
        name="pack",
    )(first, *arrays)


def unpack_kernel(blocks_ref, members_ref, got_ref, out_ref, total):
    stations = out_ref.shape[1]
    b = got_ref.shape[1] // 2
    total[...] = jnp.zeros_like(total)
    for p in range(got_ref.shape[0]):
        for side in range(2):
            rows = pl.ds(pl.multiple_of(blocks_ref[side, p] * b, b), b)
            total[rows, :] += got_ref[p, side * b:(side + 1) * b, :].astype(F32)
    station = lax.broadcasted_iota(jnp.int32, (stations, stations), 0)
    chosen = (station == members_ref[...]).astype(F32).astype(BF16)
    whole = total[...]
    high = whole.astype(BF16)
    rest = whole - high.astype(F32)
    mid = rest.astype(BF16)
    low = (rest - mid.astype(F32)).astype(BF16)
    out_ref[0] = dot(chosen, high) + (dot(chosen, mid) + dot(chosen, low))


def unpack(pair_blocks, members, got, stations):
    cols = got.shape[2]
    return pl.pallas_call(
        unpack_kernel,
        out_shape=jax.ShapeDtypeStruct((1, stations, cols), F32),
        in_specs=[
            pl.BlockSpec(memory_space=pltpu.SMEM),
            pl.BlockSpec(memory_space=pltpu.VMEM),
            pl.BlockSpec(memory_space=pltpu.VMEM),
        ],
        out_specs=pl.BlockSpec(memory_space=pltpu.VMEM),
        scratch_shapes=[pltpu.VMEM((stations, cols), F32)],
        compiler_params=pltpu.CompilerParams(vmem_limit_bytes=8 << 20),
        name="unpack",
    )(pair_blocks, members, got)


def prepare_kernel(b, slot_ref, observed_ref, orders_ref, seen_ref, env_ref):
    lags = observed_ref.shape[1]
    two = 2 * b

    def some(step, carry):
        rows = observed_ref[pl.ds(pl.multiple_of(step * two, two), two), :]
        turned = lax.dot_general(orders_ref[...], rows, (((1,), (1,)), ((), ())), preferred_element_type=F32)
        seen = turned[:lags]
        hil = turned[lags:2 * lags] + turned[2 * lags:]
        seen_ref[step] = seen.astype(BF16)
        env_ref[step] = 1.0 + jnp.sqrt(seen * seen + hil * hil)
        return carry

    lax.fori_loop(0, seen_ref.shape[0], some, 0, unroll=4)


def prepare(slot, observed, orders, parts):
    _, rows, lags = observed.shape
    b = math.isqrt(rows)
    shape = (b // 2, lags, 2 * b)
    block = (b // 2 // parts, lags, 2 * b)
    spec = pltpu.PrefetchScalarGridSpec(
        num_scalar_prefetch=1,
        grid=(parts,),
        in_specs=[
            pl.BlockSpec((None, rows // parts, lags), lambda s, slot_ref: (slot_ref[0], s, 0)),
            pl.BlockSpec(orders.shape, lambda s, slot_ref: (0, 0)),
        ],
        out_specs=[pl.BlockSpec(block, lambda s, slot_ref: (s, 0, 0))] * 2,
    )
    return pl.pallas_call(
        functools.partial(prepare_kernel, b),
        out_shape=[pltpu.HBM(shape, BF16), pltpu.HBM(shape, F32)],
        grid_spec=spec,
        compiler_params=pltpu.CompilerParams(vmem_limit_bytes=8 << 20),
        cost_estimate=pl.CostEstimate(flops=2 * rows * lags * lags, bytes_accessed=8 * rows * lags, transcendentals=0),
        name="prepare",
    )(slot, observed, orders)


def tile_lanes(tiles, d, t):
    return slice((d * tiles + t) * TILE, (d * tiles + t + 1) * TILE)


def part(t):
    return slice(t * TILE, (t + 1) * TILE)


def turn_columns(got_ref, share, b, table_ref, into, row=None):
    _, days, _, cols = got_ref.shape
    tiles = cols // TILE
    half = table_ref.shape[1] // 2
    row = share if row is None else row
    for d in range(days):
        for t in range(tiles):
            at = tile_lanes(tiles, d, t)
            u = got_ref[share, d, b:, part(t)].astype(F32)
            v = swap_halves(u)
            for k in range(half):
                one = u * table_ref[row, k:k + 1, part(t)]
                two = v * table_ref[row, half + k:half + k + 1, part(t)]
                into[k * b:(k + 1) * b, at] = (one + two).astype(BF16)
                into[(half + k) * b:(half + k + 1) * b, at] = (one - two).astype(BF16)


def turn_rows(got_ref, share, b, table_ref, into, rows_u, rows_v, mask_ref=None, row=None):
    _, days, _, cols = got_ref.shape
    tiles = cols // TILE
    half = table_ref.shape[1] // 2 - 1
    row = share if row is None else row
    pieces = [(d, t) for d in range(days) for t in range(tiles)]
    for d, t in pieces:
        at = tile_lanes(tiles, d, t)
        u = got_ref[share, d, :b, part(t)].astype(F32)
        if mask_ref is not None:
            u = u * mask_ref[d]
        u = turn_half(u, table_ref, row, t, 1)
        rows_u[:, at] = u
        rows_v[:, at] = swap_halves(u)
    for d, t in pieces:
        at = tile_lanes(tiles, d, t)
        cosine = table_ref[row, :half, part(t)]
        sine = table_ref[row, half:2 * half, part(t)]
        for k in range(b):
            one = rows_u[k:k + 1, at] * cosine
            two = rows_v[k:k + 1, at] * sine
            into[2 * k * half:2 * (k + 1) * half, at] = jnp.concatenate([one + two, one - two], axis=0).astype(BF16)


def turn_half(u, table_ref, share, t, sign):
    at = table_ref.shape[1] - 2
    one = u * table_ref[share, at:at + 1, part(t)]
    two = swap_halves(u) * table_ref[share, at + 1:at + 2, part(t)]
    return one + two if sign > 0 else one - two


def forward_kernel(b, last, offset_ref, mask_ref, got_ref, fine_ref, coarse_ref, *refs):
    before_ref, refs = (refs[0], refs[1:]) if last else (None, refs)
    out_ref, refs = refs[0], refs[1:]
    sent_ref, refs = (refs[0], refs[1:]) if last else (None, refs)
    kept_ref, even_a, even_b, odd_a, odd_b, rows_u, rows_v, sem = refs
    shares = got_ref.shape[0]
    even = (even_a, even_b)
    odd = (odd_a, odd_b)
    keep = pltpu.make_async_copy(got_ref, kept_ref, sem)
    keep.start()

    def make(share, into):
        row = offset_ref[0] + share
        turn_columns(got_ref, share, b, coarse_ref, into[1], row)
        turn_rows(got_ref, share, b, fine_ref, into[0], rows_u, rows_v, mask_ref, row)

    def product(made):
        return lax.dot_general(made[0][...], made[1][...], (((1,), (1,)), ((), ())), preferred_element_type=F32)

    make(0, even)
    out_ref[...] = before_ref[...] + product(even) if last else product(even)
    make(1, odd)

    def two_shares(step, carry):
        out_ref[...] += product(odd)
        make(2 * step + 2, even)
        out_ref[...] += product(even)
        make(2 * step + 3, odd)
        return carry

    lax.fori_loop(0, shares // 2 - 1, two_shares, 0)
    total = out_ref[...] + product(odd)
    out_ref[...] = total
    if last:
        sent_ref[...] = total.astype(sent_ref.dtype)
    keep.wait()


def forward_pass(offset, mask, got, fine, coarse, before):
    shares, days, rows, cols = got.shape
    assert shares % 2 == 0
    b = rows // 2
    n_fine = fine.shape[1] - 2
    n_coarse = coarse.shape[1]
    vmem = pl.BlockSpec(memory_space=pltpu.VMEM)
    smem = pl.BlockSpec(memory_space=pltpu.SMEM)
    shape = (n_fine * b, n_coarse * b)
    sent = [jax.ShapeDtypeStruct(shape, BF16)] * len(before)
    return pl.pallas_call(
        functools.partial(forward_kernel, b, bool(before)),
        out_shape=[pltpu.VMEM(shape, F32)] + sent + [pltpu.HBM(got.shape, BF16)],
        in_specs=[smem, smem, vmem, vmem, vmem] + [vmem] * len(before),
        out_specs=[vmem] + [vmem] * len(before) + [pl.BlockSpec(memory_space=pltpu.HBM)],
        input_output_aliases={5: 0} if before else {},
        scratch_shapes=[
            pltpu.VMEM((n_fine * b, days * cols), BF16),
            pltpu.VMEM((n_coarse * b, days * cols), BF16),
            pltpu.VMEM((n_fine * b, days * cols), BF16),
            pltpu.VMEM((n_coarse * b, days * cols), BF16),
            pltpu.VMEM((b, days * cols), F32),
            pltpu.VMEM((b, days * cols), F32),
            pltpu.SemaphoreType.DMA,
        ],
        compiler_params=pltpu.CompilerParams(vmem_limit_bytes=16 << 20),
        name="forward",
    )(offset, mask, got, fine, coarse, *before)


def residual_stage(
    b, group, scalars_ref, mine_ref, other_ref, seen_hbm, env_hbm, hilbert_hbm, seen_ref, env_ref, hilbert_ref, lagged,
    back, res, res_t, sems_s, sems_e, sem, begin,
):
    n_fine = mine_ref.shape[0] // b
    slabs = mine_ref.shape[1] // TILE
    days = scalars_ref.shape[0] - 1
    block = group * n_fine
    left = left_lanes((n_fine, 2 * b))

    def bring(step):
        some = pl.ds(step * (group // 2), group // 2)
        return (
            pltpu.make_async_copy(seen_hbm.at[some], seen_ref.at[some], sems_s.at[step]),
            pltpu.make_async_copy(env_hbm.at[some], env_ref.at[some], sems_e.at[step]),
        )

    first = pltpu.make_async_copy(hilbert_hbm, hilbert_ref, sem)
    first.start()
    for step in range(b // group):
        for copy in bring(step):
            copy.start()
    begin()
    first.wait()

    def residual_rows(step, carry):
        for copy in bring(step):
            copy.wait()
        for two in range(0, group, 2):
            rows = []
            for slab in range(slabs):
                got = []
                for k in (two, two + 1):
                    at = pl.ds(pl.multiple_of(step * block + k * n_fine, n_fine), n_fine)
                    got.append((mine_ref[at, part(slab)] + other_ref[at, part(slab)].astype(F32)) * scalars_ref[days])
                rows.append(jnp.where(left, got[0], swap_halves(got[1])))
                rows.append(jnp.where(left, swap_halves(got[0]), got[1]))
            stacked = jnp.concatenate(rows, axis=0)
            high = stacked.astype(BF16)
            low = (stacked - high.astype(F32)).astype(BF16)
            hil = dot(hilbert_ref[...], jnp.concatenate([high, high, low], axis=0))
            env_s = 1.0 + jnp.sqrt(stacked * stacked + hil * hil)
            env_o = env_ref[step * (group // 2) + two // 2]
            value = (stacked - seen_ref[step * (group // 2) + two // 2].astype(F32)) * (env_s / (env_s + env_o - 1.0))
            for slab in range(slabs):
                even = value[2 * slab * n_fine:(2 * slab + 1) * n_fine, :]
                odd = value[(2 * slab + 1) * n_fine:(2 * slab + 2) * n_fine, :]
                first = jnp.where(left, even, swap_halves(odd))
                second = jnp.where(left, swap_halves(even), odd)
                for k, rows in ((two, first), (two + 1, second)):
                    lagged[slab, pl.ds(step * group + k, n_fine, stride=b), :] = rows
                    back[k * n_fine:(k + 1) * n_fine, part(slab)] = rows
        at = pl.ds(pl.multiple_of(step * block, block), block)
        for slab in range(slabs):
            res_t[part(slab), at] = back[:, part(slab)].T.astype(BF16)
        return carry

    lax.fori_loop(0, b // group, residual_rows, 0)

    def round_rows(step, carry):
        at = pl.ds(pl.multiple_of(step * b, b), b)
        for slab in range(slabs):
            res[at, part(slab)] = lagged[slab, at, :].astype(BF16)
        return carry

    lax.fori_loop(0, n_fine, round_rows, 0)


def adjoint_stage(
    sizes, starts_ref, scalars_ref, near_ref, far_ref, fine_hbm, coarse_hbm, out_ref, got_ref, fine_ref, coarse_ref, res,
    res_t, sums_a, sums_b, turned_a, turned_b, rows_u, rows_v, sems, before,
):
    b, scale = sizes
    shares, days, _, cols = out_ref.shape
    n_fine = fine_ref.shape[1] - 2
    n_coarse = coarse_ref.shape[1]
    tiles = cols // TILE
    count = shares // 2
    later = []
    for k, kept_ref in enumerate((near_ref, far_ref)):
        here = pl.ds(k * count, count)
        some = pl.ds(starts_ref[k], count)
        later += [
            pltpu.make_async_copy(kept_ref, got_ref.at[here], sems.at[3 * k]),
            pltpu.make_async_copy(fine_hbm.at[some], fine_ref.at[here], sems.at[3 * k + 1]),
            pltpu.make_async_copy(coarse_hbm.at[some], coarse_ref.at[here], sems.at[3 * k + 2]),
        ]

    def place(share):
        return jnp.where(share < count, starts_ref[0] + share, starts_ref[1] + share - count)

    def begin():
        for copy in later:
            copy.start()

    before(begin)

    def collect(share, side, table, n, sums):
        half = n // 2
        for d in range(days):
            for t in range(tiles):
                at = tile_lanes(tiles, d, t)
                p = jnp.zeros((b, TILE), F32)
                q = jnp.zeros((b, TILE), F32)
                for k in range(half):
                    one = sums[k * b:(k + 1) * b, at]
                    two = sums[(half + k) * b:(half + k + 1) * b, at]
                    p = p + (one + two) * table[share, k:k + 1, part(t)]
                    q = q + (one - two) * table[share, half + k:half + k + 1, part(t)]
                value = p + swap_halves(q)
                if side == 0:
                    value = turn_half(value, table, share, t, -1)
                out_ref[place(share), d, side * b:(side + 1) * b, part(t)] = (value * (scalars_ref[d] * scale)).astype(BF16)

    for copy in later:
        copy.wait()
    sums_b[...] = jnp.zeros_like(sums_b)
    turn_columns(got_ref, 0, b, coarse_ref, turned_b)

    def one_share(share, carry):
        sums_a[...] = dot(res[...], turned_b[...])
        turn_rows(got_ref, share, b, fine_ref, turned_a, rows_u, rows_v)
        collect(jnp.maximum(share - 1, 0), 1, coarse_ref, n_coarse, sums_b)
        sums_b[...] = dot(res_t[...], turned_a[...])
        collect(share, 0, fine_ref, n_fine, sums_a)
        turn_columns(got_ref, jnp.minimum(share + 1, shares - 1), b, coarse_ref, turned_b)
        return carry

    lax.fori_loop(0, shares, one_share, 0)
    collect(shares - 1, 1, coarse_ref, n_coarse, sums_b)


def adjoint_kernel(
    sizes, starts_ref, scalars_ref, mine_ref, other_ref, seen_hbm, env_hbm, hilbert_hbm, near_ref, far_ref, fine_hbm,
    coarse_hbm, out_ref, seen_ref, env_ref, hilbert_ref, lagged, back, got_ref, fine_ref, coarse_ref, res, res_t,
    sums_a, sums_b, turned_a, turned_b, rows_u, rows_v, sems_s, sems_e, sems,
):
    b, scale, group = sizes

    def before(begin):
        residual_stage(
            b, group, scalars_ref, mine_ref, other_ref, seen_hbm, env_hbm, hilbert_hbm, seen_ref, env_ref, hilbert_ref,
            lagged, back, res, res_t, sems_s, sems_e, sems.at[6], begin,
        )

    adjoint_stage(
        (b, scale), starts_ref, scalars_ref, near_ref, far_ref, fine_hbm, coarse_hbm, out_ref, got_ref, fine_ref,
        coarse_ref, res, res_t, sums_a, sums_b, turned_a, turned_b, rows_u, rows_v, sems, before,
    )


def turn_tables(columns, lags, shares, n_fine):
    freqs = columns // 2
    n_coarse = lags // n_fine
    column = np.arange(columns)
    frequency = column // TILE * HALF + column % HALF
    is_real = column % TILE < HALF

    def table(halves, sign):
        phase = frequency[None, :] * halves[:, None] % (4 * freqs)
        angles = np.pi * phase / (2 * freqs)
        sine = np.where(is_real[None, :], -sign, sign) * np.sin(angles)
        return np.concatenate([np.cos(angles), sine])

    def place(rows):
        rows = rows.astype(np.float32).reshape(rows.shape[0], shares, columns // shares)
        return np.ascontiguousarray(rows.transpose(1, 0, 2))

    fine = table(2 * np.arange(n_fine // 2) + 1, 1)
    coarse = table(n_fine * (2 * np.arange(n_coarse // 2) + 1), -1)
    return place(np.concatenate([fine, table(np.array([1]), -1)])), place(coarse)


def adjoint_pass(starts, scalars, mine, other, seen, env, hilbert, near, far, fine, coarse, parts):
    half_shares, days, rows, cols = near.shape
    shares = 2 * half_shares
    b = rows // 2
    n_fine = fine.shape[1] - 2
    n_coarse = coarse.shape[1]
    lanes = days * cols
    scale = 1.0 / math.sqrt(shares * cols // 2)
    group = b // parts
    vmem = pl.BlockSpec(memory_space=pltpu.VMEM)
    hbm = pl.BlockSpec(memory_space=pltpu.HBM)
    smem = pl.BlockSpec(memory_space=pltpu.SMEM)
    apart = [pltpu.with_memory_space_constraint(x, pltpu.HBM) for x in (seen, env, hilbert, near, far, fine, coarse)]
    shape = (shares, days, rows, cols)
    return pl.pallas_call(
        functools.partial(adjoint_kernel, (b, scale, group)),
        out_shape=jax.ShapeDtypeStruct(shape, BF16),
        in_specs=[smem, smem, vmem, vmem] + [hbm] * len(apart),
        out_specs=vmem,
        scratch_shapes=[pltpu.VMEM(x.shape, x.dtype) for x in apart[:3]]
        + [
            pltpu.VMEM((n_coarse // 2, n_fine * b, 2 * b), F32),
            pltpu.VMEM((group * n_fine, n_coarse * b), F32),
            pltpu.VMEM(shape, BF16),
            pltpu.VMEM(fine.shape, F32),
            pltpu.VMEM(coarse.shape, F32),
            pltpu.VMEM((n_fine * b, n_coarse * b), BF16),
            pltpu.VMEM((n_coarse * b, n_fine * b), BF16),
            pltpu.VMEM((n_fine * b, lanes), F32),
            pltpu.VMEM((n_coarse * b, lanes), F32),
            pltpu.VMEM((n_fine * b, lanes), BF16),
            pltpu.VMEM((n_coarse * b, lanes), BF16),
            pltpu.VMEM((b, lanes), F32),
            pltpu.VMEM((b, lanes), F32),
            pltpu.SemaphoreType.DMA((parts,)),
            pltpu.SemaphoreType.DMA((parts,)),
            pltpu.SemaphoreType.DMA((7,)),
        ],
        compiler_params=pltpu.CompilerParams(vmem_limit_bytes=24 << 20),
        name="adjoint",
    )(starts, scalars, mine, other, *apart)


def body(spectra, observed, pair_blocks, members, day_mask):
    half_shares = lax.axis_size("near")
    shares = 2 * half_shares
    slots, b, _, lags = observed.shape
    _, stations, cols = spectra.shape
    n_fine = 16
    fine, coarse = turn_tables(shares * cols, lags, shares, n_fine)
    orders, hilbert = hilbert_parts(lags, n_fine)
    slot = lax.axis_index("slot")
    members = members.reshape(1, stations)
    pair_blocks = pair_blocks.T
    first_day = lax.axis_index("outer") * slots * CORES + lax.axis_index("core")
    mask = lax.dynamic_slice_in_dim(day_mask, slot, 1, 0)[0].astype(F32)
    mask_here = jnp.stack([lax.dynamic_index_in_dim(mask, first_day + k * CORES, 0, False) for k in range(slots)])
    count = jnp.sum(mask)
    scale = 1.0 / math.sqrt(shares * cols // 2)
    scalars = jnp.concatenate([mask_here / count, scale / count[None]])

    half = lax.axis_index("half")
    start_far = ((1 - half) * half_shares)[None]
    start_near = (half * half_shares)[None]
    first_pair = start_near * slots

    def exchange(x):
        flat = x.reshape(half_shares * slots, 2 * b, cols)
        moved = lax.all_to_all(flat, ("near", "slot"), 0, 0, tiled=True)
        return moved

    shape = (half_shares, slots, 2 * b, cols)
    opposite = lax.ppermute(spectra, "half", [(0, 1), (1, 0)])
    got_near = exchange(pack(first_pair, pair_blocks, members, spectra, b))
    orders, hilbert, fine, coarse = [jnp.asarray(x) for x in (orders, hilbert, fine, coarse)]
    parts = 4
    seen, env = prepare(slot[None], observed.reshape(slots, b * b, lags), orders, parts)
    got_near, opposite, seen, env, mask_here, scalars = lax.optimization_barrier(
        (got_near, opposite, seen, env, mask_here, scalars)
    )
    got_far = exchange(repack(first_pair, pair_blocks, members, opposite, b))
    mine, kept_near = forward_pass(start_near, mask_here, got_near.reshape(shape), fine, coarse, [])
    got_far, mine = lax.optimization_barrier((got_far, mine))
    mine, sent, kept_far = forward_pass(start_far, mask_here, got_far.reshape(shape), fine, coarse, [mine])
    for axis in ("outer", "core"):
        n = lax.axis_size(axis)
        others = [lax.ppermute(sent, axis, [(i, (i + k) % n) for i in range(n)]) for k in range(1, n)]
        if axis == "outer" and others:
            for other in others:
                mine = mine + other.astype(F32)
            sent = mine.astype(BF16)
    starts = jnp.concatenate([start_near, start_far])
    contrib = adjoint_pass(
        starts, scalars, mine, others[0], seen, env, hilbert, kept_near, kept_far, fine, coarse, parts
    )
    returned = lax.all_to_all(
        contrib.reshape(shares * slots, 2 * b, cols), ("half", "near", "slot"), 0, 0, tiled=True
    )
    return unpack(pair_blocks, members, returned, stations)


def solution(mesh):
    shares, days = mesh.devices.shape
    names = ("half", "near", "outer", "slot", "core")

    def run(spectra, observed, pair_blocks, members, day_mask):
        slots = observed.shape[0] // shares
        split = (2, shares // 2, days // CORES // slots, slots, CORES)
        finer = Mesh(mesh.devices.reshape(split), names)
        day_axes = names[2:]
        pair_axes = names[:2]
        return jax.shard_map(
            body,
            mesh=finer,
            in_specs=(
                P(day_axes, None, pair_axes),
                P(pair_axes, None, None, None),
                P(),
                P(),
                P(pair_axes, None),
            ),
            out_specs=P(day_axes, None, pair_axes),
            check_vma=False,
        )(spectra, observed, pair_blocks, members, day_mask)

    return run
```
